128 devices in a mesh: tile: 16 (over y_lo, x, core), mp: 8 (over y_hi, z).
Axes of the slice: x: 4, y: 4 (y_hi: 2, y_lo: 2; y = y_hi * 2 + y_lo), z: 4, core: 2. Of those that a mesh axis runs over, the one named last changes fastest.
Arguments:
- tokens: bfloat16 [128, 256, 1024], P('tile', 'mp'), may hold values from -6 to 6
- ln_gain_one: float32 [1024], replicated, may hold values from 0.5 to 1.5
- ln_gain_two: float32 [1024], replicated, may hold values from 0.5 to 1.5
- qkv_weight: bfloat16 [3, 1024, 1024], P(None, None, 'mp'), may hold values from -2 to 2
- out_weight: bfloat16 [1024, 1024], P('mp'), may hold values from -0.1875 to 0.1875
- in_weight: bfloat16 [4096, 1024], P('mp'), may hold values from -0.1875 to 0.1875
- mlp_out_weight: bfloat16 [4096, 1024], P('mp'), may hold values from -0.09375 to 0.09375
- proj_weight: bfloat16 [1024, 256], replicated, may hold values from -0.1875 to 0.1875
- land_mask: int32 [128], P('tile'), may hold values 0 or 1
- placement: int32 [128], replicated, may hold values from 0 to 127, as said below
- guide: bfloat16 [512, 256, 256], P(('tile', 'mp')), may hold values from -6 to 6
- conv_weights: bfloat16 [3, 3, 3, 256, 256], replicated, may hold values from -0.125 to 0.125
- conv_bias: float32 [3, 256], replicated, may hold values from -3 to 3
Outputs:
- dense_map: bfloat16 [512, 256, 256], P(('tile', 'mp'))
The draws below stay inside these ranges and needn't reach their ends.
Inputs may be any that keep to these rules, and one draw needn't show every extreme that they name: placement is a permutation of the scene positions; the tiles of one group land in different slabs (entry // 8), so each slab receives at most one tile of each group.
All inputs are finite; a program needn't handle non-finite values. No bound on the sum of `land_mask` on one device may be relied on, other than what follows from the above.
Results may differ from the reference program's by a relative error of at most 0.018.
The reference program's roundings to bfloat16 on the way count: a program that leaves them out, or rounds other values in their place, can miss the bound.
Values may be sent and summed in bfloat16 or wider, within the bound.
No kernel may reach another device: no remote copies, remote signals or barrier semaphores. Data moves between devices by JAX's collectives and lax.ppermute only.
A program may use at most 128 MiB of HBM per device.

```python
import jax
import jax.numpy as jnp
from jax import lax

D = 1024
HEADS = 16
HEAD = 64
FF = 4096
SIDE = 16
C = 256
UP = 2
TILE_DEV = 8
PATCHES = 256
TILES = 128
PX_ROWS = 512
PX_COLS = 256
N_TILE = 16


def draw_tokens(key, part):
    key = jax.random.fold_in(key, 13)
    return jnp.clip(jax.random.normal(key, (TILES, PATCHES, D), jnp.float32), -6.0, 6.0).astype(jnp.bfloat16)


def draw_qkv_weight(key, part):
    key = jax.random.fold_in(key, 11)
    return (jnp.clip(jax.random.normal(key, (3, D, D), jnp.float32), -6.0, 6.0) * D ** (-0.5)).astype(jnp.bfloat16)


def draw_placement(key, part):
    key = jax.random.fold_in(key, 7)
    key_shift, key_offset, key_column = jax.random.split(key, 3)
    group_shift = jax.random.permutation(key_shift, N_TILE)
    offsets = jax.random.permutation(key_offset, N_TILE)[:TILE_DEV]
    tile_index = jnp.arange(TILES, dtype=jnp.int32)
    tile_group = tile_index // TILE_DEV
    within = tile_index % TILE_DEV
    slab_index = (group_shift[tile_group] + offsets[within]) % N_TILE
    scores = jax.random.randint(key_column, (N_TILE, TILE_DEV), 0, 1 << 20) * TILE_DEV + jnp.arange(TILE_DEV)[None, :]
    column_order = jnp.argsort(scores, axis=1)
    column = column_order[slab_index, within]
    return (slab_index * TILE_DEV + column).astype(jnp.int32)


def place_ends(drawn, stream_key, least, largest):
    longest = drawn.shape.index(max(drawn.shape))
    spots = []
    for shift in (0, 1):
        where = [jax.random.randint(jax.random.fold_in(stream_key, axis), (), 0, length) for axis, length in enumerate(drawn.shape)]
        where[longest] = (where[longest] + shift) % drawn.shape[longest]
        spots.append(tuple(where))
    return drawn.at[spots[0]].set(least).at[spots[1]].set(largest)


def shard_levels(own_key, extent, shards, least, largest):
    factor_of = 1.0
    for axis_at, shards_of in shards:
        draws = jax.random.uniform(jax.random.fold_in(jax.random.fold_in(own_key, 6), axis_at), (shards_of,), jnp.float32, least / len(shards), largest / len(shards))
        factor_of = factor_of * jnp.repeat(jnp.exp(draws), extent[axis_at] // shards_of).reshape((-1,) + (1,) * (len(extent) - 1 - axis_at))
    return factor_of


def noise(own_key, shape, scale, reach, shards=(), held_as=jnp.bfloat16):
    values = scale * jax.random.normal(own_key, shape, jnp.float32)
    if shards:
        values = values * shard_levels(own_key, shape, shards, -0.22, 0.18)
    return jnp.clip(values, -reach, reach).astype(held_as)


def setup_inputs(seed: int = 0) -> dict:
    keys = jax.random.split(jax.random.key(seed), 14)
    return {
        "tokens": draw_tokens(jax.random.fold_in(keys[13], 71), 0),
        "ln_gain_one": jnp.clip(1.0 + 0.1 * jax.random.normal(keys[1], (D,), jnp.float32), 0.5, 1.5),
        "ln_gain_two": jnp.clip(1.0 + 0.1 * jax.random.normal(keys[2], (D,), jnp.float32), 0.5, 1.5),
        "qkv_weight": draw_qkv_weight(jax.random.fold_in(keys[13], 71), 0),
        "out_weight": noise(keys[4], (D, D), D ** -0.5, 0.1875, ((0, 8),)),
        "in_weight": noise(keys[5], (FF, D), D ** -0.5, 0.1875, ((0, 8),)),
        "mlp_out_weight": noise(keys[6], (FF, D), FF ** -0.5, 0.09375, ((0, 8),)),
        "proj_weight": noise(keys[7], (D, C), D ** -0.5, 0.1875),
        "land_mask": place_ends((jax.random.randint(keys[8], (TILES,), 0, 4) < 3).astype(jnp.int32), jax.random.fold_in(keys[8], 1), 0, 1),
        "placement": draw_placement(jax.random.fold_in(keys[13], 71), 0),
        "guide": noise(keys[10], (PX_ROWS, PX_COLS, C), 1.0, 6.0, ((0, 128),)),
        "conv_weights": noise(keys[11], (3, 3, 3, C, C), (9 * C) ** -0.5, 0.125),
        "conv_bias": noise(keys[12], (3, C), 0.5, 3.0, (), jnp.float32),
    }


def layer_norm(values, gain):
    widened = values.astype(jnp.float32)
    centre = lax.optimization_barrier(jnp.mean(widened, axis=-1, keepdims=True))
    spread = lax.optimization_barrier(jnp.mean((widened - centre) ** 2, axis=-1, keepdims=True))
    return ((widened - centre) * lax.rsqrt(spread + 1e-06) * gain).astype(jnp.bfloat16)

def one_tile(tile_tokens, ln_gain_one, ln_gain_two, qkv_weight, out_weight, in_weight, mlp_out_weight):
    normed = layer_norm(tile_tokens, ln_gain_one)
    query = jnp.dot(normed, qkv_weight[0], preferred_element_type=jnp.float32).astype(jnp.bfloat16)
    keys_all = jnp.dot(normed, qkv_weight[1], preferred_element_type=jnp.float32).astype(jnp.bfloat16)
    values_all = jnp.dot(normed, qkv_weight[2], preferred_element_type=jnp.float32).astype(jnp.bfloat16)
    query = query.reshape(PATCHES, HEADS, HEAD).astype(jnp.float32)
    keys_all = keys_all.reshape(PATCHES, HEADS, HEAD).astype(jnp.float32)
    values_all = values_all.reshape(PATCHES, HEADS, HEAD).astype(jnp.float32)
    scores = jnp.einsum('phe,qhe->hpq', query, keys_all) * HEAD ** (-0.5)
    soft = jax.nn.softmax(scores, axis=-1).astype(jnp.bfloat16)
    context = jnp.einsum('hpq,qhe->phe', soft.astype(jnp.float32), values_all).astype(jnp.bfloat16).reshape(PATCHES, D)
    attention = jnp.dot(context, out_weight, preferred_element_type=jnp.float32)
    middle = (tile_tokens.astype(jnp.float32) + attention).astype(jnp.bfloat16)
    normed_mid = layer_norm(middle, ln_gain_two)
    hidden = jax.nn.gelu(jnp.dot(normed_mid, in_weight.T, preferred_element_type=jnp.float32)).astype(jnp.bfloat16)
    mlp_part = jnp.dot(hidden, mlp_out_weight, preferred_element_type=jnp.float32)
    return (middle.astype(jnp.float32) + mlp_part).astype(jnp.bfloat16)

def convolve(image, kernel, shift):
    result = lax.conv_general_dilated(image.astype(jnp.float32)[None], kernel.astype(jnp.float32), (1, 1), 'SAME', dimension_numbers=('NHWC', 'HWIO', 'NHWC'), precision=lax.Precision.HIGHEST)
    return result[0] + shift

def reference(tokens, ln_gain_one, ln_gain_two, qkv_weight, out_weight, in_weight, mlp_out_weight, proj_weight, land_mask, placement, guide, conv_weights, conv_bias):
    features = lax.map(lambda tile_tokens: one_tile(tile_tokens, ln_gain_one, ln_gain_two, qkv_weight, out_weight, in_weight, mlp_out_weight), tokens)
    embed = jnp.dot(features.reshape(TILES * PATCHES, D), proj_weight, preferred_element_type=jnp.float32)
    embed = embed.astype(jnp.bfloat16).reshape(TILES, PATCHES, C) * land_mask.astype(jnp.bfloat16)[:, None, None]
    inverse = jnp.zeros((TILES,), jnp.int32).at[placement].set(jnp.arange(TILES, dtype=jnp.int32))
    arranged = embed[inverse].reshape(TILES // TILE_DEV, TILE_DEV, SIDE, SIDE, C)
    scene_grid = jnp.transpose(arranged, (0, 2, 1, 3, 4)).reshape(PX_ROWS // UP, PX_COLS // UP, C)
    upsampled = jnp.repeat(jnp.repeat(scene_grid, UP, axis=0), UP, axis=1)
    guided = (upsampled.astype(jnp.float32) + guide.astype(jnp.float32)).astype(jnp.bfloat16)
    first = jax.nn.gelu(convolve(guided, conv_weights[0], conv_bias[0])).astype(jnp.bfloat16)
    second = jax.nn.gelu(convolve(first, conv_weights[1], conv_bias[1])).astype(jnp.bfloat16)
    return (guided.astype(jnp.float32) + convolve(second, conv_weights[2], conv_bias[2])).astype(jnp.bfloat16)
```

```python
import jax
import jax.numpy as jnp
from jax import lax
from jax.sharding import Mesh, PartitionSpec as P

HEAD = 64
SIDE = 16
UP = 2
AXES = ("yl", "x", "c", "yh", "z")
TILE = ("yl", "x", "c")
MP = ("yh", "z")
F32 = jnp.float32
BF16 = jnp.bfloat16
FAR = 64.0


def layer_norm(values, gain):
    widened = values.astype(F32)
    centre = jnp.mean(widened, axis=-1, keepdims=True)
    spread = jnp.mean((widened - centre) ** 2, axis=-1, keepdims=True)
    return ((widened - centre) * lax.rsqrt(spread + 1e-06) * gain).astype(BF16)


def ring(axis, step):
    count = lax.axis_size(axis)
    return [(i, (i + step) % count) for i in range(count)]


def swap_cores(block):
    return lax.ppermute(block, "c", [(0, 1), (1, 0)])


def type_exchange(block):
    def at(pos, core):
        return ((pos % 2) * 2 + core) * 2 + pos // 2

    pairs = []
    for core in range(2):
        for pos in range(4):
            if pos // 2 == core:
                pairs.append((at(pos, core), at(3 - pos, core)))
    received = lax.ppermute(block, ("yl", "c", "yh"), pairs)
    mine = lax.axis_index("yh") == lax.axis_index("c")
    return jnp.where(mine, block, received)


def conv_layer(extended, kernel, shift, out_count):
    width_px = extended.shape[1]
    padded = jnp.pad(extended, ((0, 0), (1, 1), (0, 0)))
    running = jnp.zeros((out_count, width_px, kernel.shape[-1]), F32) + shift
    for row_shift in range(3):
        for col_shift in range(3):
            window = padded[row_shift : row_shift + out_count, col_shift : col_shift + width_px]
            running = running + jnp.einsum(
                "rwc,cd->rwd", window, kernel[row_shift, col_shift], preferred_element_type=F32
            )
    return running


def per_device(
    tokens,
    ln_gain_one,
    ln_gain_two,
    qkv_weight,
    out_weight,
    in_weight,
    mlp_out_weight,
    proj_weight,
    land_mask,
    placement,
    guide,
    conv_weights,
    conv_bias,
):
    tiles, seg, width = tokens.shape
    groups = lax.axis_size(TILE)
    here = lax.axis_index(TILE)
    core = lax.axis_index("c")

    parity = lax.axis_index("x") % 2
    heads_t = jnp.transpose(qkv_weight, (0, 2, 1))
    own_qkv = lax.dynamic_slice_in_dim(heads_t, parity * HEAD, HEAD, 1)
    own_out = lax.dynamic_slice_in_dim(out_weight, parity * HEAD, HEAD, 0)
    own_attn = jnp.concatenate([own_qkv.reshape(3 * HEAD, width), own_out], axis=0)
    piece = type_exchange(own_attn)
    pieces = [piece] + [lax.ppermute(piece, "z", ring("z", s)) for s in (1, 3, 2)]
    first_half = jnp.stack(pieces)
    from_above = lax.ppermute(first_half[:2], "x", ring("x", 3))
    from_below = lax.ppermute(first_half[2:], "x", ring("x", 1))
    attn_w = jnp.concatenate([first_half, from_above, from_below], axis=0)

    ff_half = in_weight.shape[0] // 2
    slice_rows = ff_half // 8
    start = core * ff_half + lax.axis_index(("x", "yl")) * slice_rows
    mlp_own = jnp.concatenate(
        [
            lax.dynamic_slice_in_dim(in_weight, start, slice_rows, 0),
            lax.dynamic_slice_in_dim(mlp_out_weight, start, slice_rows, 0),
        ],
        axis=0,
    )
    mlp_w = lax.all_gather(mlp_own, ("x", "yh", "yl", "z"), axis=0, tiled=False)
    w_in = mlp_w[:, :slice_rows].reshape(-1, width)
    w_out = mlp_w[:, slice_rows:].reshape(-1, width)

    slab_all = placement // tiles
    column_all = placement % tiles
    group_all = jnp.arange(placement.shape[0], dtype=jnp.int32) // tiles
    slab_local = lax.dynamic_slice_in_dim(slab_all, here * tiles, tiles, 0)
    selector = (slab_local[None, :] == jnp.arange(groups, dtype=jnp.int32)[:, None]).astype(BF16)
    in_slab = slab_all == here
    column_hot = (
        column_all[:, None] == jnp.arange(tiles, dtype=jnp.int32)[None, :]
    ) & in_slab[:, None]
    group_hot = group_all[:, None] == jnp.arange(groups, dtype=jnp.int32)[None, :]
    arrange = jnp.einsum(
        "tk,tg->kg", column_hot.astype(F32), group_hot.astype(F32)
    ).astype(BF16)
    marked = jnp.where((land_mask == 0)[:, None, None], jnp.asarray(FAR, BF16), tokens)
    outgoing = jnp.einsum("sj,jpd->spd", selector, marked, preferred_element_type=F32).astype(BF16)
    incoming = lax.all_to_all(outgoing, TILE, split_axis=0, concat_axis=0, tiled=True)
    slab_tokens = jnp.einsum(
        "kg,gpd->kpd", arrange, incoming, preferred_element_type=F32
    ).astype(BF16)
    land = slab_tokens[:, 0, 0] < FAR / 2
    tile_tokens = lax.all_to_all(slab_tokens, MP, split_axis=0, concat_axis=0, tiled=True)
    tile_tokens = tile_tokens.reshape(tiles * seg, width)

    count = tiles * seg
    normed = layer_norm(tile_tokens, ln_gain_one)
    pair = jnp.stack([normed, swap_cores(normed)])
    q, k, v = (
        jnp.einsum(
            "tpd,hed->thpe", pair, attn_w[:, i * HEAD : (i + 1) * HEAD], preferred_element_type=F32
        ).astype(BF16)
        for i in range(3)
    )
    scores = jnp.einsum("thpe,thqe->thpq", q, k, preferred_element_type=F32) * HEAD ** (-0.5)
    soft = jax.nn.softmax(scores, axis=-1).astype(BF16)
    context = jnp.einsum("thpq,thqe->thpe", soft, v, preferred_element_type=F32).astype(BF16)
    partial = jnp.einsum(
        "thpe,hed->tpd", context, attn_w[:, 3 * HEAD :], preferred_element_type=F32
    )
    attention = partial[0] + swap_cores(partial[1].astype(BF16)).astype(F32)
    middle = (tile_tokens.astype(F32) + attention).astype(BF16)

    middle = lax.all_to_all(
        middle.reshape(tiles, seg, width), MP, split_axis=0, concat_axis=0, tiled=True
    ).reshape(count, width)
    normed_mid = layer_norm(middle, ln_gain_two)
    pair_mid = jnp.concatenate([normed_mid, swap_cores(normed_mid)], axis=0)
    hidden = jnp.einsum("pd,fd->pf", pair_mid, w_in, preferred_element_type=F32)
    hidden = jax.nn.gelu(hidden).astype(BF16)
    mlp = jnp.einsum("pf,fd->pd", hidden, w_out, preferred_element_type=F32)
    mlp_sum = mlp[:count] + swap_cores(mlp[count:].astype(BF16)).astype(F32)
    features = (middle.astype(F32) + mlp_sum).astype(BF16)
    embed = jnp.einsum("pd,dc->pc", features, proj_weight, preferred_element_type=F32).astype(BF16)
    channels = proj_weight.shape[1]
    token_rows = seg // SIDE
    embed = embed.reshape(tiles, token_rows, SIDE, channels) * land.astype(BF16)[:, None, None, None]
    image = jnp.transpose(embed, (1, 0, 2, 3)).reshape(token_rows, tiles * SIDE, channels)

    total = lax.axis_size(AXES)
    forward = [(i, i + 1) for i in range(total - 1)]
    backward = [(b, a) for a, b in forward]
    rows = guide.shape[0]
    guide_low = lax.ppermute(guide[rows - 3 :], AXES, forward)
    guide_high = lax.ppermute(guide[:3], AXES, backward)
    image_low = lax.ppermute(image, AXES, forward)
    image_high = lax.ppermute(image, AXES, backward)
    image = jnp.concatenate([image_low, image, image_high], axis=0)
    guide = jnp.concatenate([guide_low, guide, guide_high], axis=0)
    upsampled = jnp.repeat(jnp.repeat(image, UP, axis=0), UP, axis=1)[1:-1]
    guided = (upsampled.astype(F32) + guide.astype(F32)).astype(BF16)

    first_row = lax.axis_index(AXES) * rows
    last_row = total * rows

    def inside(values, margin):
        row = first_row - margin + jnp.arange(values.shape[0], dtype=jnp.int32)
        return jnp.where(((row >= 0) & (row < last_row))[:, None, None], values, 0)

    first = jax.nn.gelu(conv_layer(guided, conv_weights[0], conv_bias[0], rows + 4))
    first = inside(first.astype(BF16), 2)
    second = jax.nn.gelu(conv_layer(first, conv_weights[1], conv_bias[1], rows + 2))
    second = inside(second.astype(BF16), 1)
    last_term = conv_layer(second, conv_weights[2], conv_bias[2], rows)
    return (guided[3:-3].astype(F32) + last_term).astype(BF16)


def solution(mesh):
    fine = Mesh(mesh.devices.reshape(2, 4, 2, 2, 4), AXES)
    in_specs = (
        P(TILE, MP, None),
        P(),
        P(),
        P(None, None, MP),
        P(MP, None),
        P(MP, None),
        P(MP, None),
        P(),
        P(TILE),
        P(),
        P(AXES, None, None),
        P(),
        P(),
    )
    return jax.shard_map(
        per_device, mesh=fine, in_specs=in_specs, out_specs=P(AXES, None, None), check_vma=False
    )
```

```python
import jax
import jax.numpy as jnp
from jax import lax
from jax.experimental import pallas as pl
from jax.experimental.pallas import tpu as pltpu
from jax.sharding import Mesh, PartitionSpec as P

HEAD = 64
SIDE = 16
AXES = ("yl", "x", "c", "yh", "z")
TILE = ("yl", "x", "c")
MP = ("yh", "z")
F32 = jnp.float32
BF16 = jnp.bfloat16
FAR = 64.0

def shift(block, axis, step):
    if axis == "y":
        def at(pos):
            return (pos % 2) * 2 + pos // 2

        pairs = [(at((pos + step) % 4), at(pos)) for pos in range(4)]
        return lax.ppermute(block, ("yl", "yh"), pairs)
    count = lax.axis_size(axis)
    return lax.ppermute(block, axis, [((i + step) % count, i) for i in range(count)])


def swap_cores(block):
    return lax.ppermute(block, "c", [(0, 1), (1, 0)])


def type_exchange(mine, sent):
    def at(pos, core):
        return ((pos % 2) * 2 + core) * 2 + pos // 2

    pairs = []
    for core in range(2):
        for pos in range(4):
            if pos // 2 == core:
                pairs.append((at(pos, core), at(3 - pos, core)))
    received = lax.ppermute(sent, ("yl", "c", "yh"), pairs)
    return jnp.where(lax.axis_index("yh") == lax.axis_index("c"), mine, received)


def along_z(piece):
    return jnp.stack([piece] + [shift(piece, "z", step) for step in (1, 3, 2)])


def across(base, one, two):
    return (
        base,
        shift(base, one, 1),
        shift(base, one, 3),
        shift(base[:2], two, 1),
        shift(base[2:], two, 3),
    )


VMEM_LIMIT = 56 * 2**20
NT = (((1,), (1,)), ((), ()))


def whole(memory):
    return pl.BlockSpec(memory_space=memory)


def normalise(values, gain):
    widened = values.astype(F32)
    centre = jnp.mean(widened, axis=-1, keepdims=True)
    spread = jnp.mean((widened - centre) ** 2, axis=-1, keepdims=True)
    return ((widened - centre) * lax.rsqrt(spread + 1e-06) * gain).astype(BF16)


def attention_kernel(
    parity, own, other, gain, base, plus, minus, two_low, two_high,
    near_out, far_out, held_base, held_plus, held_minus, held_two, normed, queries, values, context, sems
):
    copies = [
        pltpu.make_async_copy(base, held_base, sems.at[0]),
        pltpu.make_async_copy(minus, held_minus, sems.at[1]),
        pltpu.make_async_copy(plus, held_plus, sems.at[2]),
        pltpu.make_async_copy(two_low, held_two.at[0:2], sems.at[3]),
        pltpu.make_async_copy(two_high, held_two.at[2:4], sems.at[4]),
    ]
    for copy in copies:
        copy.start()
    even = parity[0] == 0
    count = own.shape[0]
    normed[0:count] = normalise(own[...], gain[...])
    normed[count:] = normalise(other[...], gain[...])
    for copy in copies:
        copy.wait()
    width = own.shape[1]
    half = 4 * HEAD

    def pick(one, two, rows):
        first = one[:, rows].reshape(-1, width)
        return jnp.where(even, first, two[:, rows].reshape(-1, width))

    everything = slice(0, 2 * HEAD)
    upper = slice(0, HEAD)
    lower = slice(HEAD, 2 * HEAD)
    sides = (
        ((held_base, held_minus), (held_plus, held_base)),
        ((held_two, held_plus), (held_minus, held_two)),
    )
    for side, (qk, vo) in enumerate(sides):
        queries[:, side * 2 * half : (side + 1) * 2 * half] = lax.dot_general(
            normed[...], pick(*qk, everything), NT, preferred_element_type=F32
        ).astype(BF16)
        values[:, side * half : (side + 1) * half] = lax.dot_general(
            normed[...], pick(*vo, upper), NT, preferred_element_type=F32
        ).astype(BF16)
    for tile in range(2):
        rows = slice(tile * count, (tile + 1) * count)
        for head in range(8):
            q = queries[rows, head * 2 * HEAD : head * 2 * HEAD + HEAD]
            k = queries[rows, head * 2 * HEAD + HEAD : (head + 1) * 2 * HEAD]
            v = values[rows, head * HEAD : (head + 1) * HEAD]
            scores = lax.dot_general(q, k, NT, preferred_element_type=F32) * HEAD ** (-0.5)
            scores = jnp.exp(scores - jnp.max(scores, axis=-1, keepdims=True))
            soft = (scores / jnp.sum(scores, axis=-1, keepdims=True)).astype(BF16)
            context[rows, head * HEAD : (head + 1) * HEAD] = jnp.dot(
                soft, v, preferred_element_type=F32
            ).astype(BF16)
    total = None
    for side, (qk, vo) in enumerate(sides):
        term = jnp.dot(
            context[:, side * half : (side + 1) * half], pick(*vo, lower), preferred_element_type=F32
        )
        total = term if total is None else total + term
    near_out[...] = total[:count]
    far_out[...] = total[count:].astype(BF16)


def attention(parity, own, other, gain, base, plus, minus, two_low, two_high):
    count, width = own.shape
    stack = pltpu.VMEM((4, 2 * HEAD, width), BF16)
    return pl.pallas_call(
        attention_kernel,
        out_shape=(
            jax.ShapeDtypeStruct((count, width), F32),
            jax.ShapeDtypeStruct((count, width), BF16),
        ),
        in_specs=[whole(pltpu.SMEM)] + [whole(pltpu.VMEM)] * 3 + [whole(pl.ANY)] * 5,
        out_specs=(whole(pltpu.VMEM), whole(pltpu.VMEM)),
        scratch_shapes=[stack] * 4
        + [
            pltpu.VMEM((2 * count, width), BF16),
            pltpu.VMEM((2 * count, 16 * HEAD), BF16),
            pltpu.VMEM((2 * count, 8 * HEAD), BF16),
            pltpu.VMEM((2 * count, 8 * HEAD), BF16),
            pltpu.SemaphoreType.DMA((5,)),
        ],
        compiler_params=pltpu.CompilerParams(vmem_limit_bytes=VMEM_LIMIT),
        cost_estimate=pl.CostEstimate(flops=3 * 10**9, bytes_accessed=7 * 10**6, transcendentals=2**20),
        name="attention",
    )(parity, own, other, gain, base, plus, minus, two_low, two_high)


def mlp_kernel(own, other, gain, *rest):
    groups = rest[:10]
    near_out, far_out, held, normed, total, sems = rest[10:]
    copies = []
    slot = 0
    for at, group in enumerate(groups):
        size = group.shape[0]
        copies.append(pltpu.make_async_copy(group, held.at[slot : slot + size], sems.at[at]))
        slot += size
    for copy in copies:
        copy.start()
    count, width = own.shape
    normed[0:count] = normalise(own[...], gain[...])
    normed[count:] = normalise(other[...], gain[...])
    slot = 0
    for at, group in enumerate(groups):
        copies[at].wait()
        size = group.shape[0]
        w_in = held[slot : slot + size, :HEAD].reshape(-1, width)
        w_out = held[slot : slot + size, HEAD:].reshape(-1, width)
        hidden = lax.dot_general(normed[...], w_in, NT, preferred_element_type=F32)
        hidden = jax.nn.gelu(hidden).astype(BF16)
        term = jnp.dot(hidden, w_out, preferred_element_type=F32)
        if at == 0:
            total[...] = term
        else:
            total[...] += term
        slot += size
    near_out[...] = total[:count]
    far_out[...] = total[count:].astype(BF16)


def mlp(own, other, gain, groups):
    count, width = own.shape
    return pl.pallas_call(
        mlp_kernel,
        out_shape=(
            jax.ShapeDtypeStruct((count, width), F32),
            jax.ShapeDtypeStruct((count, width), BF16),
        ),
        in_specs=[whole(pltpu.VMEM)] * 3 + [whole(pl.ANY)] * 10,
        out_specs=(whole(pltpu.VMEM), whole(pltpu.VMEM)),
        scratch_shapes=[
            pltpu.VMEM((32, 2 * HEAD, width), BF16),
            pltpu.VMEM((2 * count, width), BF16),
            pltpu.VMEM((2 * count, width), F32),
            pltpu.SemaphoreType.DMA((10,)),
        ],
        compiler_params=pltpu.CompilerParams(vmem_limit_bytes=VMEM_LIMIT),
        cost_estimate=pl.CostEstimate(flops=5 * 10**9, bytes_accessed=12 * 10**6, transcendentals=2**20),
        name="mlp",
    )(own, other, gain, *groups)


def conv_kernel(
    place, image_low, image, image_high, guide_low, guide, guide_high, weights, bias,
    out, guided, first, second, held, sems
):
    copies = [pltpu.make_async_copy(weights.at[k], held.at[k], sems.at[k]) for k in range(3)]
    for copy in copies:
        copy.start()
    cols = guide.shape[1]
    tokens = image.shape[1]
    channels = image.shape[2]
    pixel = lax.broadcasted_iota(jnp.int32, (cols, tokens), 0)
    token = lax.broadcasted_iota(jnp.int32, (cols, tokens), 1)
    spread = jnp.where(pixel // 2 == token, 1.0, 0.0).astype(BF16)
    rows = guide.shape[0]
    token_rows = (
        (image_low, 0), (image_low, 1), (image, 0), (image, 1), (image_high, 0), (image_high, 1)
    )
    for at, (source, row) in enumerate(token_rows):
        wide = jnp.dot(spread, source[row], preferred_element_type=F32)
        for pixel_row in (2 * at - 4, 2 * at - 3):
            if -3 <= pixel_row < 0:
                addend = guide_low[pixel_row + 3]
            elif 0 <= pixel_row < rows:
                addend = guide[pixel_row]
            elif rows <= pixel_row < rows + 3:
                addend = guide_high[pixel_row - rows]
            else:
                continue
            guided[pixel_row + 3] = (wide + addend.astype(F32)).astype(BF16)
    first_row = place[0]
    last_row = place[1]
    column = lax.broadcasted_iota(jnp.int32, (1, cols, channels), 1)
    at_left = column == 0
    at_right = column == cols - 1

    def layer(source, layer_at, start, size):
        sums = []
        for col in range(3):
            total = None
            for row in range(3):
                block = source[start + row : start + row + size].reshape(size * cols, channels)
                term = jnp.dot(block, held[layer_at, row, col], preferred_element_type=F32)
                total = term if total is None else total + term
            sums.append(total)
        left = pltpu.roll(sums[0], 1, 0).reshape(size, cols, channels)
        right = pltpu.roll(sums[2], size * cols - 1, 0).reshape(size, cols, channels)
        middle = sums[1].reshape(size, cols, channels)
        return (
            middle
            + jnp.where(at_left, 0.0, left)
            + jnp.where(at_right, 0.0, right)
            + bias[layer_at : layer_at + 1, :].reshape(1, 1, channels)
        )

    def inside(values, top):
        for row in range(values.shape[0]):
            at = first_row + top + row
            keep = jnp.logical_and(at >= 0, at < last_row)
            yield row, jnp.where(keep, values[row], 0.0).astype(BF16)

    copies[0].wait()
    for start in range(0, rows + 4, 2):
        for row, value in inside(jax.nn.gelu(layer(guided, 0, start, 2)), start - 2):
            first[start + row] = value
    copies[1].wait()
    for start in range(0, rows + 2, 2):
        for row, value in inside(jax.nn.gelu(layer(first, 1, start, 2)), start - 1):
            second[start + row] = value
    copies[2].wait()
    for start in range(0, rows, 2):
        last = layer(second, 2, start, 2) + guided[start + 3 : start + 5].astype(F32)
        out[start : start + 2] = last.astype(BF16)


def conv_stage(place, image_low, image, image_high, guide_low, guide, guide_high, weights, bias):
    rows, cols, channels = guide.shape
    return pl.pallas_call(
        conv_kernel,
        out_shape=jax.ShapeDtypeStruct(guide.shape, BF16),
        in_specs=[whole(pltpu.SMEM)] + [whole(pltpu.VMEM)] * 6 + [whole(pl.ANY), whole(pltpu.VMEM)],
        out_specs=whole(pltpu.VMEM),
        scratch_shapes=[
            pltpu.VMEM((rows + 6, cols, channels), BF16),
            pltpu.VMEM((rows + 4, cols, channels), BF16),
            pltpu.VMEM((rows + 2, cols, channels), BF16),
            pltpu.VMEM(weights.shape, BF16),
            pltpu.SemaphoreType.DMA((3,)),
        ],
        compiler_params=pltpu.CompilerParams(vmem_limit_bytes=VMEM_LIMIT),
        cost_estimate=pl.CostEstimate(flops=6 * 10**9, bytes_accessed=6 * 10**6, transcendentals=2**20),
        name="convs",
    )(place, image_low, image, image_high, guide_low, guide, guide_high, weights, bias)


def per_device(
    tokens,
    ln_gain_one,
    ln_gain_two,
    qkv_weight,
    out_weight,
    in_weight,
    mlp_out_weight,
    proj_weight,
    land_mask,
    placement,
    guide,
    conv_weights,
    conv_bias,
):
    tiles, seg, width = tokens.shape
    groups = lax.axis_size(TILE)
    here = lax.axis_index(TILE)

    x_at = lax.axis_index("x")
    y_at = lax.axis_index("yh") * 2 + lax.axis_index("yl")
    colour_x = (x_at + 2 * y_at) % 4
    colour_x_beside = (x_at + 2 * (3 - y_at)) % 4
    colour_y = (y_at + 2 * x_at) % 4
    colour_y_beside = (3 - y_at + 2 * x_at) % 4

    by_head = jnp.transpose(qkv_weight, (0, 2, 1)).reshape(3, 2, HEAD, width)
    out_heads = out_weight.reshape(2, HEAD, width)
    attn_all = jnp.stack(
        [by_head[0], by_head[1], by_head[2], out_heads], axis=1
    ).reshape(4, 2 * HEAD, width)
    attn_base = along_z(type_exchange(attn_all[colour_x], attn_all[colour_x_beside]))
    attn_w = across(attn_base, "x", "y")

    in_parts = in_weight.reshape(2, 4, HEAD, width)
    out_parts = mlp_out_weight.reshape(2, 4, HEAD, width)

    def mlp_slice(half, colour):
        return jnp.concatenate([in_parts[half, colour], out_parts[half, colour]], axis=0)

    mlp_pieces = type_exchange(
        jnp.stack([mlp_slice(0, colour_y), mlp_slice(1, colour_x)]),
        jnp.stack([mlp_slice(0, colour_y_beside), mlp_slice(1, colour_x_beside)]),
    )
    mlp_w = across(along_z(mlp_pieces[0]), "y", "x") + across(along_z(mlp_pieces[1]), "x", "y")

    slab_all = placement // tiles
    column_all = placement % tiles
    group_all = jnp.arange(placement.shape[0], dtype=jnp.int32) // tiles
    slab_local = lax.dynamic_slice_in_dim(slab_all, here * tiles, tiles, 0)
    selector = (slab_local[None, :] == jnp.arange(groups, dtype=jnp.int32)[:, None]).astype(BF16)
    in_slab = slab_all == here
    column_hot = (
        column_all[:, None] == jnp.arange(tiles, dtype=jnp.int32)[None, :]
    ) & in_slab[:, None]
    group_hot = group_all[:, None] == jnp.arange(groups, dtype=jnp.int32)[None, :]
    arrange = jnp.einsum(
        "tk,tg->kg", column_hot.astype(F32), group_hot.astype(F32)
    ).astype(BF16)
    marked = jnp.where((land_mask == 0)[:, None, None], jnp.asarray(FAR, BF16), tokens)
    outgoing = jnp.einsum("sj,jpd->spd", selector, marked, preferred_element_type=F32).astype(BF16)
    incoming = lax.all_to_all(outgoing, TILE, split_axis=0, concat_axis=0, tiled=True)
    slab_tokens = jnp.einsum(
        "kg,gpd->kpd", arrange, incoming, preferred_element_type=F32
    ).astype(BF16)
    land = slab_tokens[:, 0, 0] < FAR / 2
    tile_tokens = lax.all_to_all(slab_tokens, MP, split_axis=0, concat_axis=0, tiled=True)
    tile_tokens = tile_tokens.reshape(tiles * seg, width)

    count = tiles * seg
    near, far = attention(
        (x_at % 2).astype(jnp.int32).reshape(1),
        tile_tokens,
        swap_cores(tile_tokens),
        ln_gain_one.reshape(1, width),
        *attn_w,
    )
    summed = near + swap_cores(far).astype(F32)
    middle = (tile_tokens.astype(F32) + summed).astype(BF16)

    middle = lax.all_to_all(
        middle.reshape(tiles, seg, width), MP, split_axis=0, concat_axis=0, tiled=True
    ).reshape(count, width)
    near, far = mlp(middle, swap_cores(middle), ln_gain_two.reshape(1, width), mlp_w)
    summed = near + swap_cores(far).astype(F32)
    features = (middle.astype(F32) + summed).astype(BF16)
    embed = jnp.einsum("pd,dc->pc", features, proj_weight, preferred_element_type=F32).astype(BF16)
    channels = proj_weight.shape[1]
    token_rows = seg // SIDE
    embed = embed.reshape(tiles, token_rows, SIDE, channels) * land.astype(BF16)[:, None, None, None]
    image = jnp.transpose(embed, (1, 0, 2, 3)).reshape(token_rows, tiles * SIDE, channels)

    total = lax.axis_size(AXES)
    forward = [(i, i + 1) for i in range(total - 1)]
    backward = [(b, a) for a, b in forward]
    rows = guide.shape[0]
    guide_low = lax.ppermute(guide[rows - 3 :], AXES, forward)
    guide_high = lax.ppermute(guide[:3], AXES, backward)
    image_low = lax.ppermute(image, AXES, forward)
    image_high = lax.ppermute(image, AXES, backward)
    place = jnp.stack([lax.axis_index(AXES) * rows, jnp.int32(total * rows)])
    return conv_stage(
        place, image_low, image, image_high, guide_low, guide, guide_high, conv_weights, conv_bias
    )


def solution(mesh):
    fine = Mesh(mesh.devices.reshape(2, 4, 2, 2, 4), AXES)
    in_specs = (
        P(TILE, MP, None),
        P(),
        P(),
        P(None, None, MP),
        P(MP, None),
        P(MP, None),
        P(MP, None),
        P(),
        P(TILE),
        P(),
        P(AXES, None, None),
        P(),
        P(),
    )
    return jax.shard_map(
        per_device, mesh=fine, in_specs=in_specs, out_specs=P(AXES, None, None), check_vma=False
    )
```

```python
import jax
import jax.numpy as jnp
from jax import lax
from jax.experimental import pallas as pl
from jax.experimental.pallas import tpu as pltpu
from jax.sharding import Mesh, PartitionSpec as P

HEAD = 64
SIDE = 16
AXES = ("yl", "x", "c", "yh", "z")
TILE = ("yl", "x", "c")
MP = ("yh", "z")
F32 = jnp.float32
BF16 = jnp.bfloat16
FAR = 64.0

def shift(block, axis, step):
    if axis == "y":
        def at(pos):
            return (pos % 2) * 2 + pos // 2

        pairs = [(at((pos + step) % 4), at(pos)) for pos in range(4)]
        return lax.ppermute(block, ("yl", "yh"), pairs)
    count = lax.axis_size(axis)
    return lax.ppermute(block, axis, [((i + step) % count, i) for i in range(count)])


def swap_cores(block):
    return lax.ppermute(block, "c", [(0, 1), (1, 0)])


def type_exchange(mine, sent):
    def at(pos, core):
        return ((pos % 2) * 2 + core) * 2 + pos // 2

    pairs = []
    for core in range(2):
        for pos in range(4):
            if pos // 2 == core:
                pairs.append((at(pos, core), at(3 - pos, core)))
    received = lax.ppermute(sent, ("yl", "c", "yh"), pairs)
    return jnp.where(lax.axis_index("yh") == lax.axis_index("c"), mine, received)


def along_z(piece):
    return jnp.stack([piece] + [shift(piece, "z", step) for step in (1, 3, 2)])


def across(base, one, two):
    return (
        base,
        shift(base, one, 1),
        shift(base, one, 3),
        shift(base[:2], two, 1),
        shift(base[2:], two, 3),
    )


VMEM_LIMIT = 56 * 2**20
NT = (((1,), (1,)), ((), ()))
PARTS = 4


def whole(memory):
    return pl.BlockSpec(memory_space=memory)


def normalise(values, gain):
    widened = values.astype(F32)
    centre = jnp.mean(widened, axis=-1, keepdims=True)
    spread = jnp.mean((widened - centre) ** 2, axis=-1, keepdims=True)
    return ((widened - centre) * lax.rsqrt(spread + 1e-06) * gain).astype(BF16)


def attention_kernel(
    parity, own, other, gain, base, plus, minus, two_low, two_high,
    near_out, far_out, held_base, held_plus, held_minus, held_two, normed, queries, values, context, sems
):
    copies = [
        pltpu.make_async_copy(base, held_base, sems.at[0]),
        pltpu.make_async_copy(minus, held_minus, sems.at[1]),
        pltpu.make_async_copy(plus, held_plus, sems.at[2]),
        pltpu.make_async_copy(two_low, held_two.at[0:2], sems.at[3]),
        pltpu.make_async_copy(two_high, held_two.at[2:4], sems.at[4]),
    ]
    for copy in copies:
        copy.start()
    even = parity[0] == 0
    count = own.shape[0]
    normed[0:count] = normalise(own[...], gain[...])
    normed[count:] = normalise(other[...], gain[...])
    for copy in copies:
        copy.wait()
    width = own.shape[1]
    half = 4 * HEAD

    def pick(one, two, rows):
        first = one[:, rows].reshape(-1, width)
        return jnp.where(even, first, two[:, rows].reshape(-1, width))

    everything = slice(0, 2 * HEAD)
    upper = slice(0, HEAD)
    lower = slice(HEAD, 2 * HEAD)
    sides = (
        ((held_base, held_minus), (held_plus, held_base)),
        ((held_two, held_plus), (held_minus, held_two)),
    )
    for side, (qk, vo) in enumerate(sides):
        queries[:, side * 2 * half : (side + 1) * 2 * half] = lax.dot_general(
            normed[...], pick(*qk, everything), NT, preferred_element_type=F32
        ).astype(BF16)
        values[:, side * half : (side + 1) * half] = lax.dot_general(
            normed[...], pick(*vo, upper), NT, preferred_element_type=F32
        ).astype(BF16)
    for tile in range(2):
        rows = slice(tile * count, (tile + 1) * count)
        for head in range(8):
            q = queries[rows, head * 2 * HEAD : head * 2 * HEAD + HEAD]
            k = queries[rows, head * 2 * HEAD + HEAD : (head + 1) * 2 * HEAD]
            v = values[rows, head * HEAD : (head + 1) * HEAD]
            scores = lax.dot_general(q, k, NT, preferred_element_type=F32) * HEAD ** (-0.5)
            scores = jnp.exp(scores - jnp.max(scores, axis=-1, keepdims=True))
            soft = (scores / jnp.sum(scores, axis=-1, keepdims=True)).astype(BF16)
            context[rows, head * HEAD : (head + 1) * HEAD] = jnp.dot(
                soft, v, preferred_element_type=F32
            ).astype(BF16)
    total = None
    for side, (qk, vo) in enumerate(sides):
        term = jnp.dot(
            context[:, side * half : (side + 1) * half], pick(*vo, lower), preferred_element_type=F32
        )
        total = term if total is None else total + term
    near_out[...] = total[:count]
    far_out[...] = total[count:].astype(BF16)


def attention(parity, own, other, gain, base, plus, minus, two_low, two_high):
    count, width = own.shape
    stack = pltpu.VMEM((4, 2 * HEAD, width), BF16)
    return pl.pallas_call(
        attention_kernel,
        out_shape=(
            jax.ShapeDtypeStruct((count, width), F32),
            jax.ShapeDtypeStruct((count, width), BF16),
        ),
        in_specs=[whole(pltpu.SMEM)] + [whole(pltpu.VMEM)] * 3 + [whole(pl.ANY)] * 5,
        out_specs=(whole(pltpu.VMEM), whole(pltpu.VMEM)),
        scratch_shapes=[stack] * 4
        + [
            pltpu.VMEM((2 * count, width), BF16),
            pltpu.VMEM((2 * count, 16 * HEAD), BF16),
            pltpu.VMEM((2 * count, 8 * HEAD), BF16),
            pltpu.VMEM((2 * count, 8 * HEAD), BF16),
            pltpu.SemaphoreType.DMA((5,)),
        ],
        compiler_params=pltpu.CompilerParams(vmem_limit_bytes=VMEM_LIMIT),
        cost_estimate=pl.CostEstimate(flops=3 * 10**9, bytes_accessed=7 * 10**6, transcendentals=2**20),
        name="attention",
    )(parity, own, other, gain, base, plus, minus, two_low, two_high)


def mlp_kernel(own, other, gain, weights, near_out, far_out, held, normed, total, sems):
    parts = sems.shape[0]
    size = weights.shape[0] // parts
    half = weights.shape[1] // 2
    copies = [
        pltpu.make_async_copy(
            weights.at[at * size : (at + 1) * size], held.at[at * size : (at + 1) * size], sems.at[at]
        )
        for at in range(parts)
    ]
    for copy in copies:
        copy.start()
    count, width = own.shape
    normed[0:count] = normalise(own[...], gain[...])
    normed[count:] = normalise(other[...], gain[...])
    for at in range(parts):
        copies[at].wait()
        w_in = held[at * size : (at + 1) * size, :half].reshape(-1, width)
        w_out = held[at * size : (at + 1) * size, half:].reshape(-1, width)
        hidden = lax.dot_general(normed[...], w_in, NT, preferred_element_type=F32)
        hidden = jax.nn.gelu(hidden).astype(BF16)
        term = jnp.dot(hidden, w_out, preferred_element_type=F32)
        if at == 0:
            total[...] = term
        else:
            total[...] += term
    near_out[...] = total[:count]
    far_out[...] = total[count:].astype(BF16)


def mlp(own, other, gain, weights, parts=PARTS):
    count, width = own.shape
    return pl.pallas_call(
        mlp_kernel,
        out_shape=(
            jax.ShapeDtypeStruct((count, width), F32),
            jax.ShapeDtypeStruct((count, width), BF16),
        ),
        in_specs=[whole(pltpu.VMEM)] * 3 + [whole(pl.ANY)],
        out_specs=(whole(pltpu.VMEM), whole(pltpu.VMEM)),
        scratch_shapes=[
            pltpu.VMEM(weights.shape, BF16),
            pltpu.VMEM((2 * count, width), BF16),
            pltpu.VMEM((2 * count, width), F32),
            pltpu.SemaphoreType.DMA((parts,)),
        ],
        compiler_params=pltpu.CompilerParams(vmem_limit_bytes=VMEM_LIMIT),
        cost_estimate=pl.CostEstimate(flops=5 * 10**9, bytes_accessed=12 * 10**6, transcendentals=2**20),
        name="mlp",
    )(own, other, gain, weights)


def conv_kernel(
    place, image_low, image, image_high, guide_low, guide, guide_high, weights, bias,
    out, guided, first, second, held, sems
):
    copies = [pltpu.make_async_copy(weights.at[k], held.at[k], sems.at[k]) for k in range(3)]
    for copy in copies:
        copy.start()
    cols = guide.shape[1]
    tokens = image.shape[1]
    channels = image.shape[2]
    pixel = lax.broadcasted_iota(jnp.int32, (cols, tokens), 0)
    token = lax.broadcasted_iota(jnp.int32, (cols, tokens), 1)
    spread = jnp.where(pixel // 2 == token, 1.0, 0.0).astype(BF16)
    rows = guide.shape[0]
    token_rows = (
        (image_low, 0), (image_low, 1), (image, 0), (image, 1), (image_high, 0), (image_high, 1)
    )
    for at, (source, row) in enumerate(token_rows):
        wide = jnp.dot(spread, source[row], preferred_element_type=F32)
        for pixel_row in (2 * at - 4, 2 * at - 3):
            if -3 <= pixel_row < 0:
                addend = guide_low[pixel_row + 3]
            elif 0 <= pixel_row < rows:
                addend = guide[pixel_row]
            elif rows <= pixel_row < rows + 3:
                addend = guide_high[pixel_row - rows]
            else:
                continue
            guided[pixel_row + 3] = (wide + addend.astype(F32)).astype(BF16)
    first_row = place[0]
    last_row = place[1]
    column = lax.broadcasted_iota(jnp.int32, (1, cols, channels), 1)
    at_left = column == 0
    at_right = column == cols - 1

    def layer(source, layer_at, start, size):
        sums = []
        for col in range(3):
            total = None
            for row in range(3):
                block = source[start + row : start + row + size].reshape(size * cols, channels)
                term = jnp.dot(block, held[layer_at, row, col], preferred_element_type=F32)
                total = term if total is None else total + term
            sums.append(total)
        left = pltpu.roll(sums[0], 1, 0).reshape(size, cols, channels)
        right = pltpu.roll(sums[2], size * cols - 1, 0).reshape(size, cols, channels)
        middle = sums[1].reshape(size, cols, channels)
        return (
            middle
            + jnp.where(at_left, 0.0, left)
            + jnp.where(at_right, 0.0, right)
            + bias[layer_at : layer_at + 1, :].reshape(1, 1, channels)
        )

    def inside(values, top):
        for row in range(values.shape[0]):
            at = first_row + top + row
            keep = jnp.logical_and(at >= 0, at < last_row)
            yield row, jnp.where(keep, values[row], 0.0).astype(BF16)

    copies[0].wait()
    for start in range(0, rows + 4, 2):
        for row, value in inside(jax.nn.gelu(layer(guided, 0, start, 2)), start - 2):
            first[start + row] = value
    copies[1].wait()
    for start in range(0, rows + 2, 2):
        for row, value in inside(jax.nn.gelu(layer(first, 1, start, 2)), start - 1):
            second[start + row] = value
    copies[2].wait()
    for start in range(0, rows, 2):
        last = layer(second, 2, start, 2) + guided[start + 3 : start + 5].astype(F32)
        out[start : start + 2] = last.astype(BF16)


def conv_stage(place, image_low, image, image_high, guide_low, guide, guide_high, weights, bias):
    rows, cols, channels = guide.shape
    return pl.pallas_call(
        conv_kernel,
        out_shape=jax.ShapeDtypeStruct(guide.shape, BF16),
        in_specs=[whole(pltpu.SMEM)] + [whole(pltpu.VMEM)] * 6 + [whole(pl.ANY), whole(pltpu.VMEM)],
        out_specs=whole(pltpu.VMEM),
        scratch_shapes=[
            pltpu.VMEM((rows + 6, cols, channels), BF16),
            pltpu.VMEM((rows + 4, cols, channels), BF16),
            pltpu.VMEM((rows + 2, cols, channels), BF16),
            pltpu.VMEM(weights.shape, BF16),
            pltpu.SemaphoreType.DMA((3,)),
        ],
        compiler_params=pltpu.CompilerParams(vmem_limit_bytes=VMEM_LIMIT),
        cost_estimate=pl.CostEstimate(flops=6 * 10**9, bytes_accessed=6 * 10**6, transcendentals=2**20),
        name="convs",
    )(place, image_low, image, image_high, guide_low, guide, guide_high, weights, bias)


def per_device(
    tokens,
    ln_gain_one,
    ln_gain_two,
    qkv_weight,
    out_weight,
    in_weight,
    mlp_out_weight,
    proj_weight,
    land_mask,
    placement,
    guide,
    conv_weights,
    conv_bias,
):
    tiles, seg, width = tokens.shape
    groups = lax.axis_size(TILE)
    here = lax.axis_index(TILE)

    x_at = lax.axis_index("x")
    y_at = lax.axis_index("yh") * 2 + lax.axis_index("yl")
    colour_x = (x_at + 2 * y_at) % 4
    colour_x_beside = (x_at + 2 * (3 - y_at)) % 4

    by_head = jnp.transpose(qkv_weight, (0, 2, 1)).reshape(3, 2, HEAD, width)
    out_heads = out_weight.reshape(2, HEAD, width)
    attn_all = jnp.stack(
        [by_head[0], by_head[1], by_head[2], out_heads], axis=1
    ).reshape(4, 2 * HEAD, width)
    attn_piece = type_exchange(attn_all[colour_x], attn_all[colour_x_beside])
    attn_base = along_z(attn_piece)
    attn_w = across(attn_base, "x", "y")

    slice_rows = in_weight.shape[0] // 16
    start = (lax.axis_index("c") * 8 + lax.axis_index(("x", "yl"))) * slice_rows
    mlp_own = jnp.concatenate(
        [
            lax.dynamic_slice_in_dim(in_weight, start, slice_rows, 0),
            lax.dynamic_slice_in_dim(mlp_out_weight, start, slice_rows, 0),
        ],
        axis=0,
    )
    mlp_w = lax.all_gather(mlp_own, ("x", "yh", "yl", "z"), axis=0, tiled=False)

    slab_all = placement // tiles
    column_all = placement % tiles
    group_all = jnp.arange(placement.shape[0], dtype=jnp.int32) // tiles
    slab_local = lax.dynamic_slice_in_dim(slab_all, here * tiles, tiles, 0)
    selector = (slab_local[None, :] == jnp.arange(groups, dtype=jnp.int32)[:, None]).astype(BF16)
    in_slab = slab_all == here
    column_hot = (
        column_all[:, None] == jnp.arange(tiles, dtype=jnp.int32)[None, :]
    ) & in_slab[:, None]
    group_hot = group_all[:, None] == jnp.arange(groups, dtype=jnp.int32)[None, :]
    arrange = jnp.einsum(
        "tk,tg->kg", column_hot.astype(F32), group_hot.astype(F32)
    ).astype(BF16)
    marked = jnp.where((land_mask == 0)[:, None, None], jnp.asarray(FAR, BF16), tokens)
    outgoing = jnp.einsum("sj,jpd->spd", selector, marked, preferred_element_type=F32).astype(BF16)
    outgoing, _ = lax.optimization_barrier((outgoing, attn_piece))
    incoming = lax.all_to_all(outgoing, TILE, split_axis=0, concat_axis=0, tiled=True)
    slab_tokens = jnp.einsum(
        "kg,gpd->kpd", arrange, incoming, preferred_element_type=F32
    ).astype(BF16)
    land = slab_tokens[:, 0, 0] < FAR / 2
    tile_tokens = lax.all_to_all(slab_tokens, MP, split_axis=0, concat_axis=0, tiled=True)
    tile_tokens = tile_tokens.reshape(tiles * seg, width)

    count = tiles * seg
    near, far = attention(
        (x_at % 2).astype(jnp.int32).reshape(1),
        tile_tokens,
        swap_cores(tile_tokens),
        ln_gain_one.reshape(1, width),
        *attn_w,
    )
    summed = near + swap_cores(far).astype(F32)
    middle = (tile_tokens.astype(F32) + summed).astype(BF16)

    total = lax.axis_size(AXES)
    forward = [(i, i + 1) for i in range(total - 1)]
    backward = [(b, a) for a, b in forward]
    rows = guide.shape[0]
    guide_ends, _ = lax.optimization_barrier(((guide[rows - 3 :], guide[:3]), tile_tokens))
    guide_low = lax.ppermute(guide_ends[0], AXES, forward)
    guide_high = lax.ppermute(guide_ends[1], AXES, backward)

    middle = lax.all_to_all(
        middle.reshape(tiles, seg, width), MP, split_axis=0, concat_axis=0, tiled=True
    ).reshape(count, width)
    middle, guide_low, guide_high = lax.optimization_barrier((middle, guide_low, guide_high))
    near, far = mlp(middle, swap_cores(middle), ln_gain_two.reshape(1, width), mlp_w)
    summed = near + swap_cores(far).astype(F32)
    features = (middle.astype(F32) + summed).astype(BF16)
    embed = jnp.einsum("pd,dc->pc", features, proj_weight, preferred_element_type=F32).astype(BF16)
    channels = proj_weight.shape[1]
    token_rows = seg // SIDE
    embed = embed.reshape(tiles, token_rows, SIDE, channels) * land.astype(BF16)[:, None, None, None]
    image = jnp.transpose(embed, (1, 0, 2, 3)).reshape(token_rows, tiles * SIDE, channels)

    image_low = lax.ppermute(image, AXES, forward)
    image_high = lax.ppermute(image, AXES, backward)
    place = jnp.stack([lax.axis_index(AXES) * rows, jnp.int32(total * rows)])
    return conv_stage(
        place, image_low, image, image_high, guide_low, guide, guide_high, conv_weights, conv_bias
    )


def solution(mesh):
    fine = Mesh(mesh.devices.reshape(2, 4, 2, 2, 4), AXES)
    in_specs = (
        P(TILE, MP, None),
        P(),
        P(),
        P(None, None, MP),
        P(MP, None),
        P(MP, None),
        P(MP, None),
        P(),
        P(TILE),
        P(),
        P(AXES, None, None),
        P(),
        P(),
    )
    return jax.shard_map(
        per_device, mesh=fine, in_specs=in_specs, out_specs=P(AXES, None, None), check_vma=False
    )
```

```python
import jax
import jax.numpy as jnp
from jax import lax
from jax.experimental import pallas as pl
from jax.experimental.pallas import tpu as pltpu
from jax.sharding import Mesh, PartitionSpec as P

HEAD = 64
SIDE = 16
AXES = ("yl", "x", "c", "yh", "z")
TILE = ("yl", "x", "c")
MP = ("yh", "z")
F32 = jnp.float32
BF16 = jnp.bfloat16
FAR = 64.0

def shift(block, axis, step):
    if axis == "y":
        def at(pos):
            return (pos % 2) * 2 + pos // 2

        pairs = [(at((pos + step) % 4), at(pos)) for pos in range(4)]
        return lax.ppermute(block, ("yl", "yh"), pairs)
    count = lax.axis_size(axis)
    return lax.ppermute(block, axis, [((i + step) % count, i) for i in range(count)])


def swap_cores(block):
    return lax.ppermute(block, "c", [(0, 1), (1, 0)])


def type_exchange(mine, sent):
    def at(pos, core):
        return ((pos % 2) * 2 + core) * 2 + pos // 2

    pairs = []
    for core in range(2):
        for pos in range(4):
            if pos // 2 == core:
                pairs.append((at(pos, core), at(3 - pos, core)))
    received = lax.ppermute(sent, ("yl", "c", "yh"), pairs)
    return jnp.where(lax.axis_index("yh") == lax.axis_index("c"), mine, received)


def along_z(piece):
    return [piece] + [shift(piece, "z", step) for step in (1, 3, 2)]


def across(pieces, one, two):
    base = jnp.stack(pieces)
    return base, shift(base, one, 1), shift(base, one, 3), shift(base, two, 1)


NT = (((1,), (1,)), ((), ()))
PARTS = 4


def whole(memory):
    return pl.BlockSpec(memory_space=memory)


def normalise(values, gain):
    widened = values.astype(F32)
    centre = jnp.mean(widened, axis=-1, keepdims=True)
    spread = jnp.mean((widened - centre) ** 2, axis=-1, keepdims=True)
    return ((widened - centre) * lax.rsqrt(spread + 1e-06) * gain).astype(BF16)


def attention_kernel(
    parity, own, other, gain, base, plus, minus, two,
    near_out, far_out, held_base, held_plus, held_minus, held_two, normed, queries, values, context, sems
):
    copies = [
        pltpu.make_async_copy(base, held_base, sems.at[0]),
        pltpu.make_async_copy(minus, held_minus, sems.at[1]),
        pltpu.make_async_copy(plus, held_plus, sems.at[2]),
        pltpu.make_async_copy(two, held_two, sems.at[3]),
    ]
    for copy in copies:
        copy.start()
    even = parity[0] == 0
    count = own.shape[0]
    normed[0:count] = normalise(own[...], gain[...])
    normed[count:] = normalise(other[...], gain[...])
    for copy in copies:
        copy.wait()
    width = own.shape[1]
    half = 4 * HEAD

    def pick(one, two, rows):
        first = one[:, rows].reshape(-1, width)
        return jnp.where(even, first, two[:, rows].reshape(-1, width))

    everything = slice(0, 2 * HEAD)
    upper = slice(0, HEAD)
    lower = slice(HEAD, 2 * HEAD)
    sides = (
        ((held_base, held_minus), (held_plus, held_base)),
        ((held_two, held_plus), (held_minus, held_two)),
    )
    for side, (qk, vo) in enumerate(sides):
        queries[:, side * 2 * half : (side + 1) * 2 * half] = lax.dot_general(
            normed[...], pick(*qk, everything), NT, preferred_element_type=F32
        ).astype(BF16)
        values[:, side * half : (side + 1) * half] = lax.dot_general(
            normed[...], pick(*vo, upper), NT, preferred_element_type=F32
        ).astype(BF16)
    for tile in range(2):
        rows = slice(tile * count, (tile + 1) * count)
        for head in range(8):
            q = queries[rows, head * 2 * HEAD : head * 2 * HEAD + HEAD] * BF16(HEAD ** (-0.5))
            k = queries[rows, head * 2 * HEAD + HEAD : (head + 1) * 2 * HEAD]
            v = values[rows, head * HEAD : (head + 1) * HEAD]
            scores = lax.dot_general(q, k, NT, preferred_element_type=F32)
            scores = jnp.exp(scores - jnp.max(scores, axis=-1, keepdims=True))
            soft = (scores * (1.0 / jnp.sum(scores, axis=-1, keepdims=True))).astype(BF16)
            context[rows, head * HEAD : (head + 1) * HEAD] = jnp.dot(
                soft, v, preferred_element_type=F32
            ).astype(BF16)
    total = None
    for side, (qk, vo) in enumerate(sides):
        term = jnp.dot(
            context[:, side * half : (side + 1) * half], pick(*vo, lower), preferred_element_type=F32
        )
        total = term if total is None else total + term
    near_out[...] = own[...].astype(F32) + total[:count]
    far_out[...] = total[count:].astype(BF16)


def attention(parity, own, other, gain, base, plus, minus, two):
    count, width = own.shape
    stack = pltpu.VMEM((4, 2 * HEAD, width), BF16)
    return pl.pallas_call(
        attention_kernel,
        out_shape=(
            jax.ShapeDtypeStruct((count, width), F32),
            jax.ShapeDtypeStruct((count, width), BF16),
        ),
        in_specs=[whole(pltpu.SMEM)] + [whole(pltpu.VMEM)] * 3 + [whole(pl.ANY)] * 4,
        out_specs=(whole(pltpu.VMEM), whole(pltpu.VMEM)),
        scratch_shapes=[stack] * 4
        + [
            pltpu.VMEM((2 * count, width), BF16),
            pltpu.VMEM((2 * count, 16 * HEAD), BF16),
            pltpu.VMEM((2 * count, 8 * HEAD), BF16),
            pltpu.VMEM((2 * count, 8 * HEAD), BF16),
            pltpu.SemaphoreType.DMA((4,)),
        ],
        compiler_params=pltpu.CompilerParams(vmem_limit_bytes=24 * 2**20),
        cost_estimate=pl.CostEstimate(flops=3 * 10**9, bytes_accessed=7 * 10**6, transcendentals=2**20),
        name="attention",
    )(parity, own, other, gain, base, plus, minus, two)


def mlp_kernel(own, other, gain, weights, near_out, far_out, held, normed, total, sems):
    parts = sems.shape[0]
    size = weights.shape[0] // parts
    half = weights.shape[1] // 2
    copies = [
        pltpu.make_async_copy(
            weights.at[at * size : (at + 1) * size], held.at[at * size : (at + 1) * size], sems.at[at]
        )
        for at in range(parts)
    ]
    for copy in copies:
        copy.start()
    count, width = own.shape
    normed[0:count] = normalise(own[...], gain[...])
    normed[count:] = normalise(other[...], gain[...])
    for at in range(parts):
        copies[at].wait()
        w_in = held[at * size : (at + 1) * size, :half].reshape(-1, width)
        w_out = held[at * size : (at + 1) * size, half:].reshape(-1, width)
        hidden = lax.dot_general(normed[...], w_in, NT, preferred_element_type=F32)
        hidden = jax.nn.gelu(hidden).astype(BF16)
        term = jnp.dot(hidden, w_out, preferred_element_type=F32)
        if at == 0:
            total[...] = term
        else:
            total[...] += term
    near_out[...] = own[...].astype(F32) + total[:count]
    far_out[...] = total[count:].astype(BF16)


def mlp(own, other, gain, weights, parts=PARTS):
    count, width = own.shape
    return pl.pallas_call(
        mlp_kernel,
        out_shape=(
            jax.ShapeDtypeStruct((count, width), F32),
            jax.ShapeDtypeStruct((count, width), BF16),
        ),
        in_specs=[whole(pltpu.VMEM)] * 3 + [whole(pl.ANY)],
        out_specs=(whole(pltpu.VMEM), whole(pltpu.VMEM)),
        scratch_shapes=[
            pltpu.VMEM(weights.shape, BF16),
            pltpu.VMEM((2 * count, width), BF16),
            pltpu.VMEM((2 * count, width), F32),
            pltpu.SemaphoreType.DMA((parts,)),
        ],
        compiler_params=pltpu.CompilerParams(vmem_limit_bytes=28 * 2**20),
        cost_estimate=pl.CostEstimate(flops=5 * 10**9, bytes_accessed=12 * 10**6, transcendentals=2**20),
        name="mlp",
    )(own, other, gain, weights)


def conv_kernel(
    place, image_low, image, image_high, guide_low, guide, guide_high, weights, bias,
    out, guided, first, second, held, sems
):
    copies = [pltpu.make_async_copy(weights.at[k], held.at[k], sems.at[k]) for k in range(3)]
    for copy in copies:
        copy.start()
    cols = guide.shape[1]
    tokens = image.shape[1]
    channels = image.shape[2]
    pixel = lax.broadcasted_iota(jnp.int32, (cols, tokens), 0)
    token = lax.broadcasted_iota(jnp.int32, (cols, tokens), 1)
    spread = jnp.where(pixel // 2 == token, 1.0, 0.0).astype(BF16)
    rows = guide.shape[0]
    token_rows = (
        (image_low, 0), (image_low, 1), (image, 0), (image, 1), (image_high, 0), (image_high, 1)
    )
    for at, (source, row) in enumerate(token_rows):
        wide = jnp.dot(spread, source[row], preferred_element_type=F32)
        for pixel_row in (2 * at - 4, 2 * at - 3):
            if -3 <= pixel_row < 0:
                addend = guide_low[pixel_row + 3]
            elif 0 <= pixel_row < rows:
                addend = guide[pixel_row]
            elif rows <= pixel_row < rows + 3:
                addend = guide_high[pixel_row - rows]
            else:
                continue
            guided[pixel_row + 3] = (wide + addend.astype(F32)).astype(BF16)
    first_row = place[0]
    last_row = place[1]
    column = lax.broadcasted_iota(jnp.int32, (1, cols, channels), 1)
    at_left = column == 0
    at_right = column == cols - 1

    def layer(source, layer_at, start, size):
        sums = []
        for col in range(3):
            total = None
            for row in range(3):
                block = source[start + row : start + row + size].reshape(size * cols, channels)
                term = jnp.dot(block, held[layer_at, row, col], preferred_element_type=F32)
                total = term if total is None else total + term
            sums.append(total)
        left = pltpu.roll(sums[0], 1, 0).reshape(size, cols, channels)
        right = pltpu.roll(sums[2], size * cols - 1, 0).reshape(size, cols, channels)
        middle = sums[1].reshape(size, cols, channels)
        return (
            middle
            + jnp.where(at_left, 0.0, left)
            + jnp.where(at_right, 0.0, right)
            + bias[layer_at : layer_at + 1, :].reshape(1, 1, channels)
        )

    def inside(values, top):
        for row in range(values.shape[0]):
            at = first_row + top + row
            keep = jnp.logical_and(at >= 0, at < last_row)
            yield row, jnp.where(keep, values[row], 0.0).astype(BF16)

    copies[0].wait()
    for start in range(0, rows + 4, 2):
        for row, value in inside(jax.nn.gelu(layer(guided, 0, start, 2)), start - 2):
            first[start + row] = value
    copies[1].wait()
    for start in range(0, rows + 2, 2):
        for row, value in inside(jax.nn.gelu(layer(first, 1, start, 2)), start - 1):
            second[start + row] = value
    copies[2].wait()
    for start in range(0, rows, 2):
        last = layer(second, 2, start, 2) + guided[start + 3 : start + 5].astype(F32)
        out[start : start + 2] = last.astype(BF16)


def conv_stage(place, image_low, image, image_high, guide_low, guide, guide_high, weights, bias):
    rows, cols, channels = guide.shape
    return pl.pallas_call(
        conv_kernel,
        out_shape=jax.ShapeDtypeStruct(guide.shape, BF16),
        in_specs=[whole(pltpu.SMEM)] + [whole(pltpu.VMEM)] * 6 + [whole(pl.ANY), whole(pltpu.VMEM)],
        out_specs=whole(pltpu.VMEM),
        scratch_shapes=[
            pltpu.VMEM((rows + 6, cols, channels), BF16),
            pltpu.VMEM((rows + 4, cols, channels), BF16),
            pltpu.VMEM((rows + 2, cols, channels), BF16),
            pltpu.VMEM(weights.shape, BF16),
            pltpu.SemaphoreType.DMA((3,)),
        ],
        compiler_params=pltpu.CompilerParams(vmem_limit_bytes=24 * 2**20),
        cost_estimate=pl.CostEstimate(flops=6 * 10**9, bytes_accessed=6 * 10**6, transcendentals=2**20),
        name="convs",
    )(place, image_low, image, image_high, guide_low, guide, guide_high, weights, bias)


def per_device(
    tokens,
    ln_gain_one,
    ln_gain_two,
    qkv_weight,
    out_weight,
    in_weight,
    mlp_out_weight,
    proj_weight,
    land_mask,
    placement,
    guide,
    conv_weights,
    conv_bias,
):
    tiles, seg, width = tokens.shape
    groups = lax.axis_size(TILE)
    here = lax.axis_index(TILE)

    x_at = lax.axis_index("x")
    y_at = lax.axis_index("yh") * 2 + lax.axis_index("yl")
    colour_x = (x_at + 2 * y_at) % 4
    colour_x_beside = (x_at + 2 * (3 - y_at)) % 4

    by_head = jnp.transpose(qkv_weight, (0, 2, 1)).reshape(3, 2, HEAD, width)
    out_heads = out_weight.reshape(2, HEAD, width)
    attn_all = jnp.stack(
        [by_head[0], by_head[1], by_head[2], out_heads], axis=1
    ).reshape(4, 2 * HEAD, width)
    attn_piece = type_exchange(attn_all[colour_x], attn_all[colour_x_beside])
    attn_w = across(along_z(attn_piece), "x", "y")

    slice_rows = in_weight.shape[0] // 16
    start = (lax.axis_index("c") * 8 + lax.axis_index(("x", "yl"))) * slice_rows
    mlp_own = jnp.concatenate(
        [
            lax.dynamic_slice_in_dim(in_weight, start, slice_rows, 0),
            lax.dynamic_slice_in_dim(mlp_out_weight, start, slice_rows, 0),
        ],
        axis=0,
    )
    mlp_w = lax.all_gather(mlp_own, ("x", "yh", "yl", "z"), axis=0, tiled=False)

    slab_all = placement // tiles
    column_all = placement % tiles
    group_all = jnp.arange(placement.shape[0], dtype=jnp.int32) // tiles
    slab_local = lax.dynamic_slice_in_dim(slab_all, here * tiles, tiles, 0)
    selector = (slab_local[None, :] == jnp.arange(groups, dtype=jnp.int32)[:, None]).astype(BF16)
    in_slab = slab_all == here
    column_hot = (
        column_all[:, None] == jnp.arange(tiles, dtype=jnp.int32)[None, :]
    ) & in_slab[:, None]
    group_hot = group_all[:, None] == jnp.arange(groups, dtype=jnp.int32)[None, :]
    arrange = jnp.einsum(
        "tk,tg->kg", column_hot.astype(F32), group_hot.astype(F32)
    ).astype(BF16)
    marked = jnp.where((land_mask == 0)[:, None, None], jnp.asarray(FAR, BF16), tokens)
    marked, _ = lax.optimization_barrier((marked, attn_piece))
    outgoing = jnp.einsum("sj,jpd->spd", selector, marked, preferred_element_type=F32).astype(BF16)
    incoming = lax.all_to_all(outgoing, TILE, split_axis=0, concat_axis=0, tiled=True)
    slab_tokens = jnp.einsum(
        "kg,gpd->kpd", arrange, incoming, preferred_element_type=F32
    ).astype(BF16)
    land = slab_tokens[:, 0, 0] < FAR / 2
    tile_tokens = lax.all_to_all(slab_tokens, MP, split_axis=0, concat_axis=0, tiled=True)
    tile_tokens = tile_tokens.reshape(tiles * seg, width)
    other_tokens = swap_cores(tile_tokens)

    total = lax.axis_size(AXES)
    forward = [(i, i + 1) for i in range(total - 1)]
    backward = [(b, a) for a, b in forward]
    rows = guide.shape[0]
    guide_ends, _ = lax.optimization_barrier(((guide[rows - 3 :], guide[:3]), attn_w[0]))
    guide_low = lax.ppermute(guide_ends[0], AXES, forward)
    guide_high = lax.ppermute(guide_ends[1], AXES, backward)
    tile_tokens, guide_low, guide_high = lax.optimization_barrier(
        (tile_tokens, guide_low, guide_high)
    )

    count = tiles * seg
    near, far = attention(
        (x_at % 2).astype(jnp.int32).reshape(1),
        tile_tokens,
        other_tokens,
        ln_gain_one.reshape(1, width),
        *attn_w,
    )
    middle = (near + swap_cores(far).astype(F32)).astype(BF16)

    middle = lax.all_to_all(
        middle.reshape(tiles, seg, width), MP, split_axis=0, concat_axis=0, tiled=True
    ).reshape(count, width)
    near, far = mlp(middle, swap_cores(middle), ln_gain_two.reshape(1, width), mlp_w)
    features = (near + swap_cores(far).astype(F32)).astype(BF16)
    embed = jnp.einsum("pd,dc->pc", features, proj_weight, preferred_element_type=F32).astype(BF16)
    channels = proj_weight.shape[1]
    token_rows = seg // SIDE
    embed = embed.reshape(tiles, token_rows, SIDE, channels) * land.astype(BF16)[:, None, None, None]
    image = jnp.transpose(embed, (1, 0, 2, 3)).reshape(token_rows, tiles * SIDE, channels)

    image_low = lax.ppermute(image, AXES, forward)
    image_high = lax.ppermute(image, AXES, backward)
    place = jnp.stack([lax.axis_index(AXES) * rows, jnp.int32(total * rows)])
    return conv_stage(
        place, image_low, image, image_high, guide_low, guide, guide_high, conv_weights, conv_bias
    )


def solution(mesh):
    fine = Mesh(mesh.devices.reshape(2, 4, 2, 2, 4), AXES)
    in_specs = (
        P(TILE, MP, None),
        P(),
        P(),
        P(None, None, MP),
        P(MP, None),
        P(MP, None),
        P(MP, None),
        P(),
        P(TILE),
        P(),
        P(AXES, None, None),
        P(),
        P(),
    )
    return jax.shard_map(
        per_device, mesh=fine, in_specs=in_specs, out_specs=P(AXES, None, None), check_vma=False
    )
```

```python
import jax
import jax.numpy as jnp
from jax import lax
from jax.experimental import pallas as pl
from jax.experimental.pallas import tpu as pltpu
from jax.sharding import Mesh, PartitionSpec as P

HEAD = 64
SIDE = 16
AXES = ("yl", "x", "c", "yh", "z")
TILE = ("yl", "x", "c")
MP = ("yh", "z")
F32 = jnp.float32
BF16 = jnp.bfloat16
FAR = 64.0

def shift(block, axis, step):
    if axis == "y":
        def at(pos):
            return (pos % 2) * 2 + pos // 2

        pairs = [(at((pos + step) % 4), at(pos)) for pos in range(4)]
        return lax.ppermute(block, ("yl", "yh"), pairs)
    count = lax.axis_size(axis)
    return lax.ppermute(block, axis, [((i + step) % count, i) for i in range(count)])


def swap_cores(block):
    return lax.ppermute(block, "c", [(0, 1), (1, 0)])


def type_exchange(mine, sent):
    def at(pos, core):
        return ((pos % 2) * 2 + core) * 2 + pos // 2

    pairs = []
    for core in range(2):
        for pos in range(4):
            if pos // 2 == core:
                pairs.append((at(pos, core), at(3 - pos, core)))
    received = lax.ppermute(sent, ("yl", "c", "yh"), pairs)
    return jnp.where(lax.axis_index("yh") == lax.axis_index("c"), mine, received)


def along_z(piece):
    return [piece] + [shift(piece, "z", step) for step in (1, 3, 2)]


def across(pieces, one, two):
    base = jnp.stack(pieces)
    return base, shift(base, one, 1), shift(base, one, 3), shift(base, two, 1)


NT = (((1,), (1,)), ((), ()))
PARTS = 4


def whole(memory):
    return pl.BlockSpec(memory_space=memory)


def normalise(values, gain):
    widened = values.astype(F32)
    centre = jnp.mean(widened, axis=-1, keepdims=True)
    spread = jnp.mean((widened - centre) ** 2, axis=-1, keepdims=True)
    return ((widened - centre) * lax.rsqrt(spread + 1e-06) * gain).astype(BF16)


def attention_kernel(
    parity, own, other, gain, base, plus, minus, two,
    near_out, far_out, held_base, held_plus, held_minus, held_two, normed, queries, values, context, sems
):
    copies = [
        pltpu.make_async_copy(base, held_base, sems.at[0]),
        pltpu.make_async_copy(minus, held_minus, sems.at[1]),
        pltpu.make_async_copy(plus, held_plus, sems.at[2]),
        pltpu.make_async_copy(two, held_two, sems.at[3]),
    ]
    for copy in copies:
        copy.start()
    even = parity[0] == 0
    count = own.shape[0]
    normed[0:count] = normalise(own[...], gain[...])
    normed[count:] = normalise(other[...], gain[...])
    for copy in copies:
        copy.wait()
    width = own.shape[1]
    half = 4 * HEAD

    def pick(one, two, rows):
        first = one[:, rows].reshape(-1, width)
        return jnp.where(even, first, two[:, rows].reshape(-1, width))

    everything = slice(0, 2 * HEAD)
    upper = slice(0, HEAD)
    lower = slice(HEAD, 2 * HEAD)
    sides = (
        ((held_base, held_minus), (held_plus, held_base)),
        ((held_two, held_plus), (held_minus, held_two)),
    )
    for side, (qk, vo) in enumerate(sides):
        queries[:, side * 2 * half : (side + 1) * 2 * half] = lax.dot_general(
            normed[...], pick(*qk, everything), NT, preferred_element_type=F32
        ).astype(BF16)
        values[:, side * half : (side + 1) * half] = lax.dot_general(
            normed[...], pick(*vo, upper), NT, preferred_element_type=F32
        ).astype(BF16)
    for tile in range(2):
        rows = slice(tile * count, (tile + 1) * count)
        for head in range(8):
            q = queries[rows, head * 2 * HEAD : head * 2 * HEAD + HEAD] * BF16(HEAD ** (-0.5))
            k = queries[rows, head * 2 * HEAD + HEAD : (head + 1) * 2 * HEAD]
            v = values[rows, head * HEAD : (head + 1) * HEAD]
            scores = lax.dot_general(q, k, NT, preferred_element_type=F32)
            scores = jnp.exp(scores - jnp.max(scores, axis=-1, keepdims=True))
            soft = (scores * (1.0 / jnp.sum(scores, axis=-1, keepdims=True))).astype(BF16)
            context[rows, head * HEAD : (head + 1) * HEAD] = jnp.dot(
                soft, v, preferred_element_type=F32
            ).astype(BF16)
    total = None
    for side, (qk, vo) in enumerate(sides):
        term = jnp.dot(
            context[:, side * half : (side + 1) * half], pick(*vo, lower), preferred_element_type=F32
        )
        total = term if total is None else total + term
    near_out[...] = own[...].astype(F32) + total[:count]
    far_out[...] = total[count:].astype(BF16)


def attention(parity, own, other, gain, base, plus, minus, two):
    count, width = own.shape
    stack = pltpu.VMEM((4, 2 * HEAD, width), BF16)
    return pl.pallas_call(
        attention_kernel,
        out_shape=(
            jax.ShapeDtypeStruct((count, width), F32),
            jax.ShapeDtypeStruct((count, width), BF16),
        ),
        in_specs=[whole(pltpu.SMEM)] + [whole(pltpu.VMEM)] * 3 + [whole(pl.ANY)] * 4,
        out_specs=(whole(pltpu.VMEM), whole(pltpu.VMEM)),
        scratch_shapes=[stack] * 4
        + [
            pltpu.VMEM((2 * count, width), BF16),
            pltpu.VMEM((2 * count, 16 * HEAD), BF16),
            pltpu.VMEM((2 * count, 8 * HEAD), BF16),
            pltpu.VMEM((2 * count, 8 * HEAD), BF16),
            pltpu.SemaphoreType.DMA((4,)),
        ],
        compiler_params=pltpu.CompilerParams(vmem_limit_bytes=24 * 2**20),
        cost_estimate=pl.CostEstimate(flops=3 * 10**9, bytes_accessed=7 * 10**6, transcendentals=2**20),
        name="attention",
    )(parity, own, other, gain, base, plus, minus, two)


def mlp_kernel(own, other, gain, weights, near_out, far_out, held, normed, total, sems):
    parts = sems.shape[0]
    size = weights.shape[0] // parts
    half = weights.shape[1] // 2
    copies = [
        pltpu.make_async_copy(
            weights.at[at * size : (at + 1) * size], held.at[at * size : (at + 1) * size], sems.at[at]
        )
        for at in range(parts)
    ]
    for copy in copies:
        copy.start()
    count, width = own.shape
    normed[0:count] = normalise(own[...], gain[...])
    normed[count:] = normalise(other[...], gain[...])
    for at in range(parts):
        copies[at].wait()
        w_in = held[at * size : (at + 1) * size, :half].reshape(-1, width)
        w_out = held[at * size : (at + 1) * size, half:].reshape(-1, width)
        hidden = lax.dot_general(normed[...], w_in, NT, preferred_element_type=F32)
        hidden = jax.nn.gelu(hidden).astype(BF16)
        term = jnp.dot(hidden, w_out, preferred_element_type=F32)
        if at == 0:
            total[...] = term
        else:
            total[...] += term
    near_out[...] = own[...].astype(F32) + total[:count]
    far_out[...] = total[count:].astype(BF16)


def mlp(own, other, gain, weights, parts=PARTS):
    count, width = own.shape
    return pl.pallas_call(
        mlp_kernel,
        out_shape=(
            jax.ShapeDtypeStruct((count, width), F32),
            jax.ShapeDtypeStruct((count, width), BF16),
        ),
        in_specs=[whole(pltpu.VMEM)] * 3 + [whole(pl.ANY)],
        out_specs=(whole(pltpu.VMEM), whole(pltpu.VMEM)),
        scratch_shapes=[
            pltpu.VMEM(weights.shape, BF16),
            pltpu.VMEM((2 * count, width), BF16),
            pltpu.VMEM((2 * count, width), F32),
            pltpu.SemaphoreType.DMA((parts,)),
        ],
        compiler_params=pltpu.CompilerParams(vmem_limit_bytes=56 * 2**20),
        cost_estimate=pl.CostEstimate(flops=5 * 10**9, bytes_accessed=12 * 10**6, transcendentals=2**20),
        name="mlp",
    )(own, other, gain, weights)


def conv_kernel(
    place, image_low, image, image_high, guide_low, guide, guide_high, weights, bias,
    out, guided, first, second, held, sems
):
    copies = [pltpu.make_async_copy(weights.at[k], held.at[k], sems.at[k]) for k in range(3)]
    for copy in copies:
        copy.start()
    cols = guide.shape[1]
    tokens = image.shape[1]
    channels = image.shape[2]
    pixel = lax.broadcasted_iota(jnp.int32, (cols, tokens), 0)
    token = lax.broadcasted_iota(jnp.int32, (cols, tokens), 1)
    spread = jnp.where(pixel // 2 == token, 1.0, 0.0).astype(BF16)
    rows = guide.shape[0]
    token_rows = (
        (image_low, 0), (image_low, 1), (image, 0), (image, 1), (image_high, 0), (image_high, 1)
    )
    for at, (source, row) in enumerate(token_rows):
        wide = jnp.dot(spread, source[row], preferred_element_type=F32)
        for pixel_row in (2 * at - 4, 2 * at - 3):
            if -3 <= pixel_row < 0:
                addend = guide_low[pixel_row + 3]
            elif 0 <= pixel_row < rows:
                addend = guide[pixel_row]
            elif rows <= pixel_row < rows + 3:
                addend = guide_high[pixel_row - rows]
            else:
                continue
            guided[pixel_row + 3] = (wide + addend.astype(F32)).astype(BF16)
    first_row = place[0]
    last_row = place[1]
    column = lax.broadcasted_iota(jnp.int32, (1, cols, channels), 1)
    at_left = column == 0
    at_right = column == cols - 1

    def layer(source, layer_at, start, size):
        sums = []
        for col in range(3):
            total = None
            for row in range(3):
                block = source[start + row : start + row + size].reshape(size * cols, channels)
                term = jnp.dot(block, held[layer_at, row, col], preferred_element_type=F32)
                total = term if total is None else total + term
            sums.append(total)
        left = pltpu.roll(sums[0], 1, 0).reshape(size, cols, channels)
        right = pltpu.roll(sums[2], size * cols - 1, 0).reshape(size, cols, channels)
        middle = sums[1].reshape(size, cols, channels)
        return (
            middle
            + jnp.where(at_left, 0.0, left)
            + jnp.where(at_right, 0.0, right)
            + bias[layer_at : layer_at + 1, :].reshape(1, 1, channels)
        )

    def inside(values, top):
        for row in range(values.shape[0]):
            at = first_row + top + row
            keep = jnp.logical_and(at >= 0, at < last_row)
            yield row, jnp.where(keep, values[row], 0.0).astype(BF16)

    copies[0].wait()
    for start in range(0, rows + 4, 2):
        for row, value in inside(jax.nn.gelu(layer(guided, 0, start, 2)), start - 2):
            first[start + row] = value
    copies[1].wait()
    for start in range(0, rows + 2, 2):
        for row, value in inside(jax.nn.gelu(layer(first, 1, start, 2)), start - 1):
            second[start + row] = value
    copies[2].wait()
    for start in range(0, rows, 2):
        last = layer(second, 2, start, 2) + guided[start + 3 : start + 5].astype(F32)
        out[start : start + 2] = last.astype(BF16)


def conv_stage(place, image_low, image, image_high, guide_low, guide, guide_high, weights, bias):
    rows, cols, channels = guide.shape
    return pl.pallas_call(
        conv_kernel,
        out_shape=jax.ShapeDtypeStruct(guide.shape, BF16),
        in_specs=[whole(pltpu.SMEM)] + [whole(pltpu.VMEM)] * 6 + [whole(pl.ANY), whole(pltpu.VMEM)],
        out_specs=whole(pltpu.VMEM),
        scratch_shapes=[
            pltpu.VMEM((rows + 6, cols, channels), BF16),
            pltpu.VMEM((rows + 4, cols, channels), BF16),
            pltpu.VMEM((rows + 2, cols, channels), BF16),
            pltpu.VMEM(weights.shape, BF16),
            pltpu.SemaphoreType.DMA((3,)),
        ],
        compiler_params=pltpu.CompilerParams(vmem_limit_bytes=56 * 2**20),
        cost_estimate=pl.CostEstimate(flops=6 * 10**9, bytes_accessed=6 * 10**6, transcendentals=2**20),
        name="convs",
    )(place, image_low, image, image_high, guide_low, guide, guide_high, weights, bias)


def per_device(
    tokens,
    ln_gain_one,
    ln_gain_two,
    qkv_weight,
    out_weight,
    in_weight,
    mlp_out_weight,
    proj_weight,
    land_mask,
    placement,
    guide,
    conv_weights,
    conv_bias,
):
    tiles, seg, width = tokens.shape
    groups = lax.axis_size(TILE)
    here = lax.axis_index(TILE)

    x_at = lax.axis_index("x")
    y_at = lax.axis_index("yh") * 2 + lax.axis_index("yl")
    colour_x = (x_at + 2 * y_at) % 4
    colour_x_beside = (x_at + 2 * (3 - y_at)) % 4

    by_head = jnp.transpose(qkv_weight, (0, 2, 1)).reshape(3, 2, HEAD, width)
    out_heads = out_weight.reshape(2, HEAD, width)
    attn_all = jnp.stack(
        [by_head[0], by_head[1], by_head[2], out_heads], axis=1
    ).reshape(4, 2 * HEAD, width)
    attn_piece = type_exchange(attn_all[colour_x], attn_all[colour_x_beside])
    attn_w = across(along_z(attn_piece), "x", "y")

    slice_rows = in_weight.shape[0] // 16
    start = (lax.axis_index("c") * 8 + lax.axis_index(("x", "yl"))) * slice_rows
    mlp_own = jnp.concatenate(
        [
            lax.dynamic_slice_in_dim(in_weight, start, slice_rows, 0),
            lax.dynamic_slice_in_dim(mlp_out_weight, start, slice_rows, 0),
        ],
        axis=0,
    )
    mlp_w = lax.all_gather(mlp_own, ("x", "yh", "yl", "z"), axis=0, tiled=False)

    slab_all = placement // tiles
    column_all = placement % tiles
    group_all = jnp.arange(placement.shape[0], dtype=jnp.int32) // tiles
    slab_local = lax.dynamic_slice_in_dim(slab_all, here * tiles, tiles, 0)
    selector = (slab_local[None, :] == jnp.arange(groups, dtype=jnp.int32)[:, None]).astype(BF16)
    in_slab = slab_all == here
    column_hot = (
        column_all[:, None] == jnp.arange(tiles, dtype=jnp.int32)[None, :]
    ) & in_slab[:, None]
    group_hot = group_all[:, None] == jnp.arange(groups, dtype=jnp.int32)[None, :]
    arrange = jnp.einsum(
        "tk,tg->kg", column_hot.astype(F32), group_hot.astype(F32)
    ).astype(BF16)
    marked = jnp.where((land_mask == 0)[:, None, None], jnp.asarray(FAR, BF16), tokens)
    marked, _ = lax.optimization_barrier((marked, attn_piece))
    outgoing = jnp.einsum("sj,jpd->spd", selector, marked, preferred_element_type=F32).astype(BF16)
    incoming = lax.all_to_all(outgoing, TILE, split_axis=0, concat_axis=0, tiled=True)
    slab_tokens = jnp.einsum(
        "kg,gpd->kpd", arrange, incoming, preferred_element_type=F32
    ).astype(BF16)
    land = slab_tokens[:, 0, 0] < FAR / 2
    tile_tokens = lax.all_to_all(slab_tokens, MP, split_axis=0, concat_axis=0, tiled=True)
    tile_tokens = tile_tokens.reshape(tiles * seg, width)
    other_tokens = swap_cores(tile_tokens)

    count = tiles * seg
    near, far = attention(
        (x_at % 2).astype(jnp.int32).reshape(1),
        tile_tokens,
        other_tokens,
        ln_gain_one.reshape(1, width),
        *attn_w,
    )
    middle = (near + swap_cores(far).astype(F32)).astype(BF16)

    total = lax.axis_size(AXES)
    forward = [(i, i + 1) for i in range(total - 1)]
    backward = [(b, a) for a, b in forward]
    rows = guide.shape[0]
    guide_ends, _ = lax.optimization_barrier(((guide[rows - 3 :], guide[:3]), far))
    guide_low = lax.ppermute(guide_ends[0], AXES, forward)
    guide_high = lax.ppermute(guide_ends[1], AXES, backward)

    middle = lax.all_to_all(
        middle.reshape(tiles, seg, width), MP, split_axis=0, concat_axis=0, tiled=True
    ).reshape(count, width)
    middle, guide_low, guide_high = lax.optimization_barrier((middle, guide_low, guide_high))
    near, far = mlp(middle, swap_cores(middle), ln_gain_two.reshape(1, width), mlp_w)
    features = (near + swap_cores(far).astype(F32)).astype(BF16)
    embed = jnp.einsum("pd,dc->pc", features, proj_weight, preferred_element_type=F32).astype(BF16)
    channels = proj_weight.shape[1]
    token_rows = seg // SIDE
    embed = embed.reshape(tiles, token_rows, SIDE, channels) * land.astype(BF16)[:, None, None, None]
    image = jnp.transpose(embed, (1, 0, 2, 3)).reshape(token_rows, tiles * SIDE, channels)

    image_low = lax.ppermute(image, AXES, forward)
    image_high = lax.ppermute(image, AXES, backward)
    place = jnp.stack([lax.axis_index(AXES) * rows, jnp.int32(total * rows)])
    return conv_stage(
        place, image_low, image, image_high, guide_low, guide, guide_high, conv_weights, conv_bias
    )


def solution(mesh):
    fine = Mesh(mesh.devices.reshape(2, 4, 2, 2, 4), AXES)
    in_specs = (
        P(TILE, MP, None),
        P(),
        P(),
        P(None, None, MP),
        P(MP, None),
        P(MP, None),
        P(MP, None),
        P(),
        P(TILE),
        P(),
        P(AXES, None, None),
        P(),
        P(),
    )
    return jax.shard_map(
        per_device, mesh=fine, in_specs=in_specs, out_specs=P(AXES, None, None), check_vma=False
    )
```

```python
import jax
import jax.numpy as jnp
from jax import lax
from jax.experimental import pallas as pl
from jax.experimental.pallas import tpu as pltpu
from jax.sharding import Mesh, PartitionSpec as P

HEAD = 64
SIDE = 16
AXES = ("yl", "x", "c", "yh", "z")
TILE = ("yl", "x", "c")
MP = ("yh", "z")
F32 = jnp.float32
BF16 = jnp.bfloat16
FAR = 64.0

def shift(block, axis, step):
    if axis == "y":
        def at(pos):
            return (pos % 2) * 2 + pos // 2

        pairs = [(at((pos + step) % 4), at(pos)) for pos in range(4)]
        return lax.ppermute(block, ("yl", "yh"), pairs)
    count = lax.axis_size(axis)
    return lax.ppermute(block, axis, [((i + step) % count, i) for i in range(count)])


def swap_cores(block):
    return lax.ppermute(block, "c", [(0, 1), (1, 0)])


def type_exchange(mine, sent):
    def at(pos, core):
        return ((pos % 2) * 2 + core) * 2 + pos // 2

    pairs = []
    for core in range(2):
        for pos in range(4):
            if pos // 2 == core:
                pairs.append((at(pos, core), at(3 - pos, core)))
    received = lax.ppermute(sent, ("yl", "c", "yh"), pairs)
    return jnp.where(lax.axis_index("yh") == lax.axis_index("c"), mine, received)


def along_z(piece):
    return [piece] + [shift(piece, "z", step) for step in (1, 3, 2)]


def across(pieces, one, two):
    base = jnp.stack(pieces)
    low = shift(jnp.stack(pieces[:2]), two, 1)
    high = shift(jnp.stack(pieces[2:]), two, 3)
    return base, shift(base, one, 1), shift(base, one, 3), low, high


NT = (((1,), (1,)), ((), ()))
PARTS = 4


def whole(memory):
    return pl.BlockSpec(memory_space=memory)


def normalise(values, gain):
    widened = values.astype(F32)
    centre = jnp.mean(widened, axis=-1, keepdims=True)
    spread = jnp.mean((widened - centre) ** 2, axis=-1, keepdims=True)
    return ((widened - centre) * lax.rsqrt(spread + 1e-06) * gain).astype(BF16)


def attention_kernel(
    parity, own, other, gain, base, plus, minus, two_low, two_high,
    near_out, far_out, held_base, held_plus, held_minus, held_two, normed, queries, values, context, sems
):
    copies = [
        pltpu.make_async_copy(base, held_base, sems.at[0]),
        pltpu.make_async_copy(minus, held_minus, sems.at[1]),
        pltpu.make_async_copy(plus, held_plus, sems.at[2]),
        pltpu.make_async_copy(two_low, held_two.at[0:2], sems.at[3]),
        pltpu.make_async_copy(two_high, held_two.at[2:4], sems.at[4]),
    ]
    for copy in copies:
        copy.start()
    even = parity[0] == 0
    count = own.shape[0]
    normed[0:count] = normalise(own[...], gain[...])
    normed[count:] = normalise(other[...], gain[...])
    for copy in copies:
        copy.wait()
    width = own.shape[1]
    half = 4 * HEAD

    def pick(one, two, rows):
        first = one[:, rows].reshape(-1, width)
        return jnp.where(even, first, two[:, rows].reshape(-1, width))

    everything = slice(0, 2 * HEAD)
    upper = slice(0, HEAD)
    lower = slice(HEAD, 2 * HEAD)
    sides = (
        ((held_base, held_minus), (held_plus, held_base)),
        ((held_two, held_plus), (held_minus, held_two)),
    )
    for side, (qk, vo) in enumerate(sides):
        queries[:, side * 2 * half : (side + 1) * 2 * half] = lax.dot_general(
            normed[...], pick(*qk, everything), NT, preferred_element_type=F32
        ).astype(BF16)
        values[:, side * half : (side + 1) * half] = lax.dot_general(
            normed[...], pick(*vo, upper), NT, preferred_element_type=F32
        ).astype(BF16)
    for tile in range(2):
        rows = slice(tile * count, (tile + 1) * count)
        for head in range(8):
            q = queries[rows, head * 2 * HEAD : head * 2 * HEAD + HEAD] * BF16(HEAD ** (-0.5))
            k = queries[rows, head * 2 * HEAD + HEAD : (head + 1) * 2 * HEAD]
            v = values[rows, head * HEAD : (head + 1) * HEAD]
            scores = lax.dot_general(q, k, NT, preferred_element_type=F32)
            scores = jnp.exp(scores - jnp.max(scores, axis=-1, keepdims=True))
            soft = (scores * (1.0 / jnp.sum(scores, axis=-1, keepdims=True))).astype(BF16)
            context[rows, head * HEAD : (head + 1) * HEAD] = jnp.dot(
                soft, v, preferred_element_type=F32
            ).astype(BF16)
    total = None
    for side, (qk, vo) in enumerate(sides):
        term = jnp.dot(
            context[:, side * half : (side + 1) * half], pick(*vo, lower), preferred_element_type=F32
        )
        total = term if total is None else total + term
    near_out[...] = own[...].astype(F32) + total[:count]
    far_out[...] = total[count:].astype(BF16)


def attention(parity, own, other, gain, base, plus, minus, two_low, two_high):
    count, width = own.shape
    stack = pltpu.VMEM((4, 2 * HEAD, width), BF16)
    return pl.pallas_call(
        attention_kernel,
        out_shape=(
            jax.ShapeDtypeStruct((count, width), F32),
            jax.ShapeDtypeStruct((count, width), BF16),
        ),
        in_specs=[whole(pltpu.SMEM)] + [whole(pltpu.VMEM)] * 3 + [whole(pl.ANY)] * 5,
        out_specs=(whole(pltpu.VMEM), whole(pltpu.VMEM)),
        scratch_shapes=[stack] * 4
        + [
            pltpu.VMEM((2 * count, width), BF16),
            pltpu.VMEM((2 * count, 16 * HEAD), BF16),
            pltpu.VMEM((2 * count, 8 * HEAD), BF16),
            pltpu.VMEM((2 * count, 8 * HEAD), BF16),
            pltpu.SemaphoreType.DMA((5,)),
        ],
        compiler_params=pltpu.CompilerParams(vmem_limit_bytes=24 * 2**20),
        cost_estimate=pl.CostEstimate(flops=3 * 10**9, bytes_accessed=7 * 10**6, transcendentals=2**20),
        name="attention",
    )(parity, own, other, gain, base, plus, minus, two_low, two_high)


def mlp_kernel(own, other, gain, weights, near_out, far_out, held, normed, total, sems):
    parts = sems.shape[0]
    size = weights.shape[0] // parts
    half = weights.shape[1] // 2
    copies = [
        pltpu.make_async_copy(
            weights.at[at * size : (at + 1) * size], held.at[at * size : (at + 1) * size], sems.at[at]
        )
        for at in range(parts)
    ]
    for copy in copies:
        copy.start()
    count, width = own.shape
    normed[0:count] = normalise(own[...], gain[...])
    normed[count:] = normalise(other[...], gain[...])
    for at in range(parts):
        copies[at].wait()
        w_in = held[at * size : (at + 1) * size, :half].reshape(-1, width)
        w_out = held[at * size : (at + 1) * size, half:].reshape(-1, width)
        hidden = lax.dot_general(normed[...], w_in, NT, preferred_element_type=F32)
        hidden = jax.nn.gelu(hidden).astype(BF16)
        term = jnp.dot(hidden, w_out, preferred_element_type=F32)
        if at == 0:
            total[...] = term
        else:
            total[...] += term
    near_out[...] = own[...].astype(F32) + total[:count]
    far_out[...] = total[count:].astype(BF16)


def mlp(own, other, gain, weights, parts=PARTS):
    count, width = own.shape
    return pl.pallas_call(
        mlp_kernel,
        out_shape=(
            jax.ShapeDtypeStruct((count, width), F32),
            jax.ShapeDtypeStruct((count, width), BF16),
        ),
        in_specs=[whole(pltpu.VMEM)] * 3 + [whole(pl.ANY)],
        out_specs=(whole(pltpu.VMEM), whole(pltpu.VMEM)),
        scratch_shapes=[
            pltpu.VMEM(weights.shape, BF16),
            pltpu.VMEM((2 * count, width), BF16),
            pltpu.VMEM((2 * count, width), F32),
            pltpu.SemaphoreType.DMA((parts,)),
        ],
        compiler_params=pltpu.CompilerParams(vmem_limit_bytes=56 * 2**20),
        cost_estimate=pl.CostEstimate(flops=5 * 10**9, bytes_accessed=12 * 10**6, transcendentals=2**20),
        name="mlp",
    )(own, other, gain, weights)


def spread_tokens(cols, tokens):
    pixel = lax.broadcasted_iota(jnp.int32, (cols, tokens), 0)
    token = lax.broadcasted_iota(jnp.int32, (cols, tokens), 1)
    return jnp.where(pixel // 2 == token, 1.0, 0.0).astype(BF16)


def conv_terms(terms, weights):
    sums = []
    for col in range(3):
        total = None
        for row, at in terms:
            term = jnp.dot(row, weights[at, col], preferred_element_type=F32)
            total = term if total is None else total + term
        sums.append(total)
    cols = sums[0].shape[0]
    column = lax.broadcasted_iota(jnp.int32, sums[0].shape, 0)
    left = jnp.where(column == 0, 0.0, pltpu.roll(sums[0], 1, 0))
    right = jnp.where(column == cols - 1, 0.0, pltpu.roll(sums[2], cols - 1, 0))
    return sums[1] + left + right


def near_terms(rows, out_row):
    return [(rows[at], at - out_row + 1) for at in sorted(rows) if -1 <= at - out_row <= 1]


def early_kernel(image, guide, weights, bias, guided, part_one, first, part_two, held, sems):
    copies = [pltpu.make_async_copy(weights.at[k], held.at[k], sems.at[k]) for k in range(2)]
    for copy in copies:
        copy.start()
    rows, cols, _ = guide.shape
    spread = spread_tokens(cols, image.shape[1])
    for at in range(rows // 2):
        wide = jnp.dot(spread, image[at], preferred_element_type=F32)
        for row in (2 * at, 2 * at + 1):
            guided[row] = (wide + guide[row].astype(F32)).astype(BF16)
    own = {at: guided[at] for at in range(rows)}
    copies[0].wait()
    for at in range(rows - 2):
        value = conv_terms(near_terms(own, at + 1), held.at[0]) + bias[0:1, :]
        first[at] = jax.nn.gelu(value).astype(BF16)
    for at, row in enumerate((-1, 0, rows - 1, rows)):
        part_one[at] = conv_terms(near_terms(own, row), held.at[0]) + bias[0:1, :]
    copies[1].wait()
    inner = {at + 1: first[at] for at in range(rows - 2)}
    for at in range(rows):
        part_two[at] = conv_terms(near_terms(inner, at), held.at[1]) + bias[1:2, :]


def late_kernel(
    place, image_low, image_high, guide_low, guide_high, guided, part_one, first, part_two, weights, bias,
    out, outer, second, held, sems
):
    copies = [pltpu.make_async_copy(weights.at[k], held.at[k], sems.at[k]) for k in range(3)]
    for copy in copies:
        copy.start()
    rows, cols, _ = guided.shape
    spread = spread_tokens(cols, image_low.shape[1])
    beside = {}
    for source, addend, top in ((image_low, guide_low, -4), (image_high, guide_high, rows)):
        for at in range(2):
            wide = jnp.dot(spread, source[at], preferred_element_type=F32)
            for row in (top + 2 * at, top + 2 * at + 1):
                if -3 <= row < rows + 3:
                    added = addend[row + 3 if row < 0 else row - rows]
                    beside[row] = (wide + added.astype(F32)).astype(BF16)
    first_row = place[0]
    last_row = place[1]

    def inside(value, row):
        at = first_row + row
        return jnp.where(jnp.logical_and(at >= 0, at < last_row), value, 0.0).astype(BF16)

    copies[0].wait()
    layer = {}
    saved = {-1: 0, 0: 1, rows - 1: 2, rows: 3}
    for at, row in enumerate((-2, -1, 0, rows - 1, rows, rows + 1)):
        value = conv_terms(near_terms(beside, row), held.at[0])
        value = value + (part_one[saved[row]] if row in saved else bias[0:1, :])
        outer[at] = inside(jax.nn.gelu(value), row)
        layer[row] = outer.at[at]
    copies[1].wait()
    shown = {}
    for row in range(-1, rows + 1):
        value = conv_terms([(ref[...], at) for ref, at in near_terms(layer, row)], held.at[1]) if near_terms(
            layer, row
        ) else 0.0
        value = value + (part_two[row] if 0 <= row < rows else bias[1:2, :])
        second[row + 1] = inside(jax.nn.gelu(value), row)
        shown[row] = second.at[row + 1]
    copies[2].wait()
    for row in range(rows):
        value = conv_terms([(ref[...], at) for ref, at in near_terms(shown, row)], held.at[2])
        out[row] = (value + bias[2:3, :] + guided[row].astype(F32)).astype(BF16)


def early_stage(image, guide, weights, bias):
    rows, cols, channels = guide.shape
    wide = (rows, cols, channels)
    return pl.pallas_call(
        early_kernel,
        out_shape=(
            jax.ShapeDtypeStruct(wide, BF16),
            jax.ShapeDtypeStruct((4, cols, channels), F32),
            jax.ShapeDtypeStruct((rows - 2, cols, channels), BF16),
            jax.ShapeDtypeStruct(wide, F32),
        ),
        in_specs=[whole(pltpu.VMEM)] * 2 + [whole(pl.ANY), whole(pltpu.VMEM)],
        out_specs=(whole(pltpu.VMEM),) * 4,
        scratch_shapes=[
            pltpu.VMEM((2,) + weights.shape[1:], BF16),
            pltpu.SemaphoreType.DMA((2,)),
        ],
        compiler_params=pltpu.CompilerParams(vmem_limit_bytes=24 * 2**20),
        cost_estimate=pl.CostEstimate(flops=3 * 10**9, bytes_accessed=4 * 10**6, transcendentals=2**20),
        name="early",
    )(image, guide, weights, bias)


def late_stage(place, image_low, image_high, guide_low, guide_high, early, weights, bias):
    rows, cols, channels = early[0].shape
    return pl.pallas_call(
        late_kernel,
        out_shape=jax.ShapeDtypeStruct((rows, cols, channels), BF16),
        in_specs=[whole(pltpu.SMEM)] + [whole(pltpu.VMEM)] * 8 + [whole(pl.ANY), whole(pltpu.VMEM)],
        out_specs=whole(pltpu.VMEM),
        scratch_shapes=[
            pltpu.VMEM((6, cols, channels), BF16),
            pltpu.VMEM((rows + 2, cols, channels), BF16),
            pltpu.VMEM(weights.shape, BF16),
            pltpu.SemaphoreType.DMA((3,)),
        ],
        compiler_params=pltpu.CompilerParams(vmem_limit_bytes=32 * 2**20),
        cost_estimate=pl.CostEstimate(flops=4 * 10**9, bytes_accessed=6 * 10**6, transcendentals=2**20),
        name="late",
    )(place, image_low, image_high, guide_low, guide_high, *early, weights, bias)


def per_device(
    tokens,
    ln_gain_one,
    ln_gain_two,
    qkv_weight,
    out_weight,
    in_weight,
    mlp_out_weight,
    proj_weight,
    land_mask,
    placement,
    guide,
    conv_weights,
    conv_bias,
):
    tiles, seg, width = tokens.shape
    groups = lax.axis_size(TILE)
    here = lax.axis_index(TILE)

    x_at = lax.axis_index("x")
    y_at = lax.axis_index("yh") * 2 + lax.axis_index("yl")
    colour_x = (x_at + 2 * y_at) % 4
    colour_x_beside = (x_at + 2 * (3 - y_at)) % 4

    by_head = jnp.transpose(qkv_weight, (0, 2, 1)).reshape(3, 2, HEAD, width)
    out_heads = out_weight.reshape(2, HEAD, width)
    attn_all = jnp.stack(
        [by_head[0], by_head[1], by_head[2], out_heads], axis=1
    ).reshape(4, 2 * HEAD, width)
    attn_piece = type_exchange(attn_all[colour_x], attn_all[colour_x_beside])
    attn_w = across(along_z(attn_piece), "x", "y")

    slice_rows = in_weight.shape[0] // 16
    start = (lax.axis_index("c") * 8 + lax.axis_index(("x", "yl"))) * slice_rows
    mlp_own = jnp.concatenate(
        [
            lax.dynamic_slice_in_dim(in_weight, start, slice_rows, 0),
            lax.dynamic_slice_in_dim(mlp_out_weight, start, slice_rows, 0),
        ],
        axis=0,
    )
    mlp_w = lax.all_gather(mlp_own, ("x", "yh", "yl", "z"), axis=0, tiled=False)

    slab_all = placement // tiles
    column_all = placement % tiles
    group_all = jnp.arange(placement.shape[0], dtype=jnp.int32) // tiles
    slab_local = lax.dynamic_slice_in_dim(slab_all, here * tiles, tiles, 0)
    selector = (slab_local[None, :] == jnp.arange(groups, dtype=jnp.int32)[:, None]).astype(BF16)
    in_slab = slab_all == here
    column_hot = (
        column_all[:, None] == jnp.arange(tiles, dtype=jnp.int32)[None, :]
    ) & in_slab[:, None]
    group_hot = group_all[:, None] == jnp.arange(groups, dtype=jnp.int32)[None, :]
    arrange = jnp.einsum(
        "tk,tg->kg", column_hot.astype(F32), group_hot.astype(F32)
    ).astype(BF16)
    marked = jnp.where((land_mask == 0)[:, None, None], jnp.asarray(FAR, BF16), tokens)
    marked, _ = lax.optimization_barrier((marked, attn_piece))
    outgoing = jnp.einsum("sj,jpd->spd", selector, marked, preferred_element_type=F32).astype(BF16)
    incoming = lax.all_to_all(outgoing, TILE, split_axis=0, concat_axis=0, tiled=True)
    slab_tokens = jnp.einsum(
        "kg,gpd->kpd", arrange, incoming, preferred_element_type=F32
    ).astype(BF16)
    land = slab_tokens[:, 0, 0] < FAR / 2
    tile_tokens = lax.all_to_all(slab_tokens, MP, split_axis=0, concat_axis=0, tiled=True)
    tile_tokens = tile_tokens.reshape(tiles * seg, width)
    other_tokens = swap_cores(tile_tokens)

    count = tiles * seg
    near, far = attention(
        (x_at % 2).astype(jnp.int32).reshape(1),
        tile_tokens,
        other_tokens,
        ln_gain_one.reshape(1, width),
        *attn_w,
    )
    middle = (near + swap_cores(far).astype(F32)).astype(BF16)

    total = lax.axis_size(AXES)
    forward = [(i, i + 1) for i in range(total - 1)]
    backward = [(b, a) for a, b in forward]
    rows = guide.shape[0]
    guide_ends, _ = lax.optimization_barrier(((guide[rows - 3 :], guide[:3]), far))
    guide_low = lax.ppermute(guide_ends[0], AXES, forward)
    guide_high = lax.ppermute(guide_ends[1], AXES, backward)

    middle = lax.all_to_all(
        middle.reshape(tiles, seg, width), MP, split_axis=0, concat_axis=0, tiled=True
    ).reshape(count, width)
    middle, guide_low, guide_high = lax.optimization_barrier((middle, guide_low, guide_high))
    near, far = mlp(middle, swap_cores(middle), ln_gain_two.reshape(1, width), mlp_w)
    features = (near + swap_cores(far).astype(F32)).astype(BF16)
    embed = jnp.einsum("pd,dc->pc", features, proj_weight, preferred_element_type=F32).astype(BF16)
    channels = proj_weight.shape[1]
    token_rows = seg // SIDE
    embed = embed.reshape(tiles, token_rows, SIDE, channels) * land.astype(BF16)[:, None, None, None]
    image = jnp.transpose(embed, (1, 0, 2, 3)).reshape(token_rows, tiles * SIDE, channels)

    image_low = lax.ppermute(image, AXES, forward)
    image_high = lax.ppermute(image, AXES, backward)
    place = jnp.stack([lax.axis_index(AXES) * rows, jnp.int32(total * rows)])
    early = early_stage(image, guide, conv_weights, conv_bias)
    return late_stage(
        place, image_low, image_high, guide_low, guide_high, early, conv_weights, conv_bias
    )


def solution(mesh):
    fine = Mesh(mesh.devices.reshape(2, 4, 2, 2, 4), AXES)
    in_specs = (
        P(TILE, MP, None),
        P(),
        P(),
        P(None, None, MP),
        P(MP, None),
        P(MP, None),
        P(MP, None),
        P(),
        P(TILE),
        P(),
        P(AXES, None, None),
        P(),
        P(),
    )
    return jax.shard_map(
        per_device, mesh=fine, in_specs=in_specs, out_specs=P(AXES, None, None), check_vma=False
    )
```

```python
import jax
import jax.numpy as jnp
from jax import lax
from jax.experimental import pallas as pl
from jax.experimental.pallas import tpu as pltpu
from jax.sharding import Mesh, PartitionSpec as P

HEAD = 64
SIDE = 16
AXES = ("yl", "x", "c", "yh", "z")
TILE = ("yl", "x", "c")
MP = ("yh", "z")
F32 = jnp.float32
BF16 = jnp.bfloat16
FAR = 64.0

def shift(block, axis, step):
    if axis == "y":
        def at(pos):
            return (pos % 2) * 2 + pos // 2

        pairs = [(at((pos + step) % 4), at(pos)) for pos in range(4)]
        return lax.ppermute(block, ("yl", "yh"), pairs)
    count = lax.axis_size(axis)
    return lax.ppermute(block, axis, [((i + step) % count, i) for i in range(count)])


def swap_cores(block):
    return lax.ppermute(block, "c", [(0, 1), (1, 0)])


def type_exchange(mine, sent):
    def at(pos, core):
        return ((pos % 2) * 2 + core) * 2 + pos // 2

    pairs = []
    for core in range(2):
        for pos in range(4):
            if pos // 2 == core:
                pairs.append((at(pos, core), at(3 - pos, core)))
    received = lax.ppermute(sent, ("yl", "c", "yh"), pairs)
    return jnp.where(lax.axis_index("yh") == lax.axis_index("c"), mine, received)


def along_z(piece):
    return [piece] + [shift(piece, "z", step) for step in (1, 3, 2)]


def across(base, low, high, one, two):
    return base, shift(base, one, 1), shift(base, one, 3), shift(low, two, 1), shift(high, two, 3)


NT = (((1,), (1,)), ((), ()))
PARTS = 4


def whole(memory):
    return pl.BlockSpec(memory_space=memory)


def normalise(values, gain):
    widened = values.astype(F32)
    centre = jnp.mean(widened, axis=-1, keepdims=True)
    spread = jnp.mean((widened - centre) ** 2, axis=-1, keepdims=True)
    return ((widened - centre) * lax.rsqrt(spread + 1e-06) * gain).astype(BF16)


def attention_kernel(
    parity, own, other, gain, base, plus, minus, two_low, two_high,
    near_out, far_out, held_base, held_plus, held_minus, held_two, normed, queries, values, context, sems
):
    copies = [
        pltpu.make_async_copy(base, held_base, sems.at[0]),
        pltpu.make_async_copy(minus, held_minus, sems.at[1]),
        pltpu.make_async_copy(plus, held_plus, sems.at[2]),
        pltpu.make_async_copy(two_low, held_two.at[0:2], sems.at[3]),
        pltpu.make_async_copy(two_high, held_two.at[2:4], sems.at[4]),
    ]
    for copy in copies:
        copy.start()
    even = parity[0] == 0
    count = own.shape[0]
    normed[0:count] = normalise(own[...], gain[...])
    normed[count:] = normalise(other[...], gain[...])
    for copy in copies:
        copy.wait()
    width = own.shape[1]
    half = 4 * HEAD

    def pick(one, two, rows):
        first = one[:, rows].reshape(-1, width)
        return jnp.where(even, first, two[:, rows].reshape(-1, width))

    everything = slice(0, 2 * HEAD)
    upper = slice(0, HEAD)
    lower = slice(HEAD, 2 * HEAD)
    sides = (
        ((held_base, held_minus), (held_plus, held_base)),
        ((held_two, held_plus), (held_minus, held_two)),
    )
    for side, (qk, vo) in enumerate(sides):
        queries[:, side * 2 * half : (side + 1) * 2 * half] = lax.dot_general(
            normed[...], pick(*qk, everything), NT, preferred_element_type=F32
        ).astype(BF16)
        values[:, side * half : (side + 1) * half] = lax.dot_general(
            normed[...], pick(*vo, upper), NT, preferred_element_type=F32
        ).astype(BF16)
    for tile in range(2):
        rows = slice(tile * count, (tile + 1) * count)
        for head in range(8):
            q = queries[rows, head * 2 * HEAD : head * 2 * HEAD + HEAD] * BF16(HEAD ** (-0.5))
            k = queries[rows, head * 2 * HEAD + HEAD : (head + 1) * 2 * HEAD]
            v = values[rows, head * HEAD : (head + 1) * HEAD]
            scores = lax.dot_general(q, k, NT, preferred_element_type=F32)
            scores = jnp.exp(scores - jnp.max(scores, axis=-1, keepdims=True))
            soft = (scores * (1.0 / jnp.sum(scores, axis=-1, keepdims=True))).astype(BF16)
            context[rows, head * HEAD : (head + 1) * HEAD] = jnp.dot(
                soft, v, preferred_element_type=F32
            ).astype(BF16)
    total = None
    for side, (qk, vo) in enumerate(sides):
        term = jnp.dot(
            context[:, side * half : (side + 1) * half], pick(*vo, lower), preferred_element_type=F32
        )
        total = term if total is None else total + term
    near_out[...] = own[...].astype(F32) + total[:count]
    far_out[...] = total[count:].astype(BF16)


def attention(parity, own, other, gain, base, plus, minus, two_low, two_high):
    count, width = own.shape
    stack = pltpu.VMEM((4, 2 * HEAD, width), BF16)
    return pl.pallas_call(
        attention_kernel,
        out_shape=(
            jax.ShapeDtypeStruct((count, width), F32),
            jax.ShapeDtypeStruct((count, width), BF16),
        ),
        in_specs=[whole(pltpu.SMEM)] + [whole(pltpu.VMEM)] * 3 + [whole(pl.ANY)] * 5,
        out_specs=(whole(pltpu.VMEM), whole(pltpu.VMEM)),
        scratch_shapes=[stack] * 4
        + [
            pltpu.VMEM((2 * count, width), BF16),
            pltpu.VMEM((2 * count, 16 * HEAD), BF16),
            pltpu.VMEM((2 * count, 8 * HEAD), BF16),
            pltpu.VMEM((2 * count, 8 * HEAD), BF16),
            pltpu.SemaphoreType.DMA((5,)),
        ],
        compiler_params=pltpu.CompilerParams(vmem_limit_bytes=24 * 2**20),
        cost_estimate=pl.CostEstimate(flops=3 * 10**9, bytes_accessed=7 * 10**6, transcendentals=2**20),
        name="attention",
    )(parity, own, other, gain, base, plus, minus, two_low, two_high)


def mlp_kernel(own, other, gain, weights, near_out, far_out, held, normed, total, sems):
    parts = sems.shape[0]
    size = weights.shape[0] // parts
    half = weights.shape[1] // 2
    copies = [
        pltpu.make_async_copy(
            weights.at[at * size : (at + 1) * size], held.at[at * size : (at + 1) * size], sems.at[at]
        )
        for at in range(parts)
    ]
    for copy in copies:
        copy.start()
    count, width = own.shape
    normed[0:count] = normalise(own[...], gain[...])
    normed[count:] = normalise(other[...], gain[...])
    for at in range(parts):
        copies[at].wait()
        w_in = held[at * size : (at + 1) * size, :half].reshape(-1, width)
        w_out = held[at * size : (at + 1) * size, half:].reshape(-1, width)
        hidden = lax.dot_general(normed[...], w_in, NT, preferred_element_type=F32)
        hidden = jax.nn.gelu(hidden).astype(BF16)
        term = jnp.dot(hidden, w_out, preferred_element_type=F32)
        if at == 0:
            total[...] = term
        else:
            total[...] += term
    near_out[...] = own[...].astype(F32) + total[:count]
    far_out[...] = total[count:].astype(BF16)


def mlp(own, other, gain, weights, parts=PARTS):
    count, width = own.shape
    return pl.pallas_call(
        mlp_kernel,
        out_shape=(
            jax.ShapeDtypeStruct((count, width), F32),
            jax.ShapeDtypeStruct((count, width), BF16),
        ),
        in_specs=[whole(pltpu.VMEM)] * 3 + [whole(pl.ANY)],
        out_specs=(whole(pltpu.VMEM), whole(pltpu.VMEM)),
        scratch_shapes=[
            pltpu.VMEM(weights.shape, BF16),
            pltpu.VMEM((2 * count, width), BF16),
            pltpu.VMEM((2 * count, width), F32),
            pltpu.SemaphoreType.DMA((parts,)),
        ],
        compiler_params=pltpu.CompilerParams(vmem_limit_bytes=56 * 2**20),
        cost_estimate=pl.CostEstimate(flops=5 * 10**9, bytes_accessed=12 * 10**6, transcendentals=2**20),
        name="mlp",
    )(own, other, gain, weights)


def spread_tokens(cols, tokens):
    pixel = lax.broadcasted_iota(jnp.int32, (cols, tokens), 0)
    token = lax.broadcasted_iota(jnp.int32, (cols, tokens), 1)
    return jnp.where(pixel // 2 == token, 1.0, 0.0).astype(BF16)


def conv_terms(terms, weights):
    sums = []
    for col in range(3):
        total = None
        for row, at in terms:
            term = jnp.dot(row, weights[at, col], preferred_element_type=F32)
            total = term if total is None else total + term
        sums.append(total)
    cols = sums[0].shape[0]
    column = lax.broadcasted_iota(jnp.int32, sums[0].shape, 0)
    left = jnp.where(column == 0, 0.0, pltpu.roll(sums[0], 1, 0))
    right = jnp.where(column == cols - 1, 0.0, pltpu.roll(sums[2], cols - 1, 0))
    return sums[1] + left + right


def near_terms(rows, out_row):
    return [(rows[at], at - out_row + 1) for at in sorted(rows) if -1 <= at - out_row <= 1]


def early_kernel(image, guide, weights, bias, guided, part_one, first, part_two, held, sems):
    copies = [pltpu.make_async_copy(weights.at[k], held.at[k], sems.at[k]) for k in range(2)]
    for copy in copies:
        copy.start()
    rows, cols, _ = guide.shape
    spread = spread_tokens(cols, image.shape[1])
    for at in range(rows // 2):
        wide = jnp.dot(spread, image[at], preferred_element_type=F32)
        for row in (2 * at, 2 * at + 1):
            guided[row] = (wide + guide[row].astype(F32)).astype(BF16)
    own = {at: guided[at] for at in range(rows)}
    copies[0].wait()
    for at in range(rows - 2):
        value = conv_terms(near_terms(own, at + 1), held.at[0]) + bias[0:1, :]
        first[at] = jax.nn.gelu(value).astype(BF16)
    for at, row in enumerate((-1, 0, rows - 1, rows)):
        part_one[at] = conv_terms(near_terms(own, row), held.at[0]) + bias[0:1, :]
    copies[1].wait()
    inner = {at + 1: first[at] for at in range(rows - 2)}
    for at in range(rows):
        part_two[at] = conv_terms(near_terms(inner, at), held.at[1]) + bias[1:2, :]


def late_kernel(
    place, image_low, image_high, guide_low, guide_high, guided, part_one, first, part_two, weights, bias,
    out, outer, second, held, sems
):
    copies = [pltpu.make_async_copy(weights.at[k], held.at[k], sems.at[k]) for k in range(3)]
    for copy in copies:
        copy.start()
    rows, cols, _ = guided.shape
    spread = spread_tokens(cols, image_low.shape[1])
    beside = {}
    for source, addend, top in ((image_low, guide_low, -4), (image_high, guide_high, rows)):
        for at in range(2):
            wide = jnp.dot(spread, source[at], preferred_element_type=F32)
            for row in (top + 2 * at, top + 2 * at + 1):
                if -3 <= row < rows + 3:
                    added = addend[row + 3 if row < 0 else row - rows]
                    beside[row] = (wide + added.astype(F32)).astype(BF16)
    first_row = place[0]
    last_row = place[1]

    def inside(value, row):
        at = first_row + row
        return jnp.where(jnp.logical_and(at >= 0, at < last_row), value, 0.0).astype(BF16)

    copies[0].wait()
    layer = {}
    saved = {-1: 0, 0: 1, rows - 1: 2, rows: 3}
    for at, row in enumerate((-2, -1, 0, rows - 1, rows, rows + 1)):
        value = conv_terms(near_terms(beside, row), held.at[0])
        value = value + (part_one[saved[row]] if row in saved else bias[0:1, :])
        outer[at] = inside(jax.nn.gelu(value), row)
        layer[row] = outer.at[at]
    copies[1].wait()
    shown = {}
    for row in range(-1, rows + 1):
        value = conv_terms([(ref[...], at) for ref, at in near_terms(layer, row)], held.at[1]) if near_terms(
            layer, row
        ) else 0.0
        value = value + (part_two[row] if 0 <= row < rows else bias[1:2, :])
        second[row + 1] = inside(jax.nn.gelu(value), row)
        shown[row] = second.at[row + 1]
    copies[2].wait()
    for row in range(rows):
        value = conv_terms([(ref[...], at) for ref, at in near_terms(shown, row)], held.at[2])
        out[row] = (value + bias[2:3, :] + guided[row].astype(F32)).astype(BF16)


def early_stage(image, guide, weights, bias):
    rows, cols, channels = guide.shape
    wide = (rows, cols, channels)
    return pl.pallas_call(
        early_kernel,
        out_shape=(
            jax.ShapeDtypeStruct(wide, BF16),
            jax.ShapeDtypeStruct((4, cols, channels), F32),
            jax.ShapeDtypeStruct((rows - 2, cols, channels), BF16),
            jax.ShapeDtypeStruct(wide, F32),
        ),
        in_specs=[whole(pltpu.VMEM)] * 2 + [whole(pl.ANY), whole(pltpu.VMEM)],
        out_specs=(whole(pltpu.VMEM),) * 4,
        scratch_shapes=[
            pltpu.VMEM((2,) + weights.shape[1:], BF16),
            pltpu.SemaphoreType.DMA((2,)),
        ],
        compiler_params=pltpu.CompilerParams(vmem_limit_bytes=24 * 2**20),
        cost_estimate=pl.CostEstimate(flops=3 * 10**9, bytes_accessed=4 * 10**6, transcendentals=2**20),
        name="early",
    )(image, guide, weights, bias)


def late_stage(place, image_low, image_high, guide_low, guide_high, early, weights, bias):
    rows, cols, channels = early[0].shape
    return pl.pallas_call(
        late_kernel,
        out_shape=jax.ShapeDtypeStruct((rows, cols, channels), BF16),
        in_specs=[whole(pltpu.SMEM)] + [whole(pltpu.VMEM)] * 8 + [whole(pl.ANY), whole(pltpu.VMEM)],
        out_specs=whole(pltpu.VMEM),
        scratch_shapes=[
            pltpu.VMEM((6, cols, channels), BF16),
            pltpu.VMEM((rows + 2, cols, channels), BF16),
            pltpu.VMEM(weights.shape, BF16),
            pltpu.SemaphoreType.DMA((3,)),
        ],
        compiler_params=pltpu.CompilerParams(vmem_limit_bytes=32 * 2**20),
        cost_estimate=pl.CostEstimate(flops=4 * 10**9, bytes_accessed=6 * 10**6, transcendentals=2**20),
        name="late",
    )(place, image_low, image_high, guide_low, guide_high, *early, weights, bias)


def per_device(
    tokens,
    ln_gain_one,
    ln_gain_two,
    qkv_weight,
    out_weight,
    in_weight,
    mlp_out_weight,
    proj_weight,
    land_mask,
    placement,
    guide,
    conv_weights,
    conv_bias,
):
    tiles, seg, width = tokens.shape
    groups = lax.axis_size(TILE)
    here = lax.axis_index(TILE)

    x_at = lax.axis_index("x")
    y_at = lax.axis_index("yh") * 2 + lax.axis_index("yl")
    colour_x = (x_at + 2 * y_at) % 4
    colour_x_beside = (x_at + 2 * (3 - y_at)) % 4

    by_head = jnp.transpose(qkv_weight, (0, 2, 1)).reshape(3, 2, HEAD, width)
    out_heads = out_weight.reshape(2, HEAD, width)
    attn_all = jnp.stack(
        [by_head[0], by_head[1], by_head[2], out_heads], axis=1
    ).reshape(4, 2 * HEAD, width)
    attn_piece = type_exchange(attn_all[colour_x], attn_all[colour_x_beside])
    attn_pieces = along_z(attn_piece)

    slice_rows = in_weight.shape[0] // 16
    start = (lax.axis_index("c") * 8 + lax.axis_index(("x", "yl"))) * slice_rows
    mlp_own = jnp.concatenate(
        [
            lax.dynamic_slice_in_dim(in_weight, start, slice_rows, 0),
            lax.dynamic_slice_in_dim(mlp_out_weight, start, slice_rows, 0),
        ],
        axis=0,
    )
    mlp_w = lax.all_gather(mlp_own, ("x", "yh", "yl", "z"), axis=0, tiled=False)

    slab_all = placement // tiles
    column_all = placement % tiles
    group_all = jnp.arange(placement.shape[0], dtype=jnp.int32) // tiles
    slab_local = lax.dynamic_slice_in_dim(slab_all, here * tiles, tiles, 0)
    selector = (slab_local[None, :] == jnp.arange(groups, dtype=jnp.int32)[:, None]).astype(BF16)
    in_slab = slab_all == here
    column_hot = (
        column_all[:, None] == jnp.arange(tiles, dtype=jnp.int32)[None, :]
    ) & in_slab[:, None]
    group_hot = group_all[:, None] == jnp.arange(groups, dtype=jnp.int32)[None, :]
    arrange = jnp.einsum(
        "tk,tg->kg", column_hot.astype(F32), group_hot.astype(F32)
    ).astype(BF16)
    marked = jnp.where((land_mask == 0)[:, None, None], jnp.asarray(FAR, BF16), tokens)
    outgoing = jnp.einsum("sj,jpd->spd", selector, marked, preferred_element_type=F32).astype(BF16)
    incoming = lax.all_to_all(outgoing, TILE, split_axis=0, concat_axis=0, tiled=True)
    slab_tokens = jnp.einsum(
        "kg,gpd->kpd", arrange, incoming, preferred_element_type=F32
    ).astype(BF16)
    land = slab_tokens[:, 0, 0] < FAR / 2
    attn_pieces, _ = lax.optimization_barrier((attn_pieces, slab_tokens))
    stacks = (jnp.stack(attn_pieces), jnp.stack(attn_pieces[:2]), jnp.stack(attn_pieces[2:]))
    slab_tokens, stacks = lax.optimization_barrier((slab_tokens, stacks))
    attn_w = across(*stacks, "x", "y")
    tile_tokens = lax.all_to_all(slab_tokens, MP, split_axis=0, concat_axis=0, tiled=True)
    tile_tokens = tile_tokens.reshape(tiles * seg, width)
    other_tokens = swap_cores(tile_tokens)

    count = tiles * seg
    near, far = attention(
        (x_at % 2).astype(jnp.int32).reshape(1),
        tile_tokens,
        other_tokens,
        ln_gain_one.reshape(1, width),
        *attn_w,
    )
    middle = (near + swap_cores(far).astype(F32)).astype(BF16)

    total = lax.axis_size(AXES)
    forward = [(i, i + 1) for i in range(total - 1)]
    backward = [(b, a) for a, b in forward]
    rows = guide.shape[0]
    guide_ends, _ = lax.optimization_barrier(((guide[rows - 3 :], guide[:3]), far))
    guide_low = lax.ppermute(guide_ends[0], AXES, forward)
    guide_high = lax.ppermute(guide_ends[1], AXES, backward)

    middle = lax.all_to_all(
        middle.reshape(tiles, seg, width), MP, split_axis=0, concat_axis=0, tiled=True
    ).reshape(count, width)
    middle, guide_low, guide_high = lax.optimization_barrier((middle, guide_low, guide_high))
    near, far = mlp(middle, swap_cores(middle), ln_gain_two.reshape(1, width), mlp_w)
    features = (near + swap_cores(far).astype(F32)).astype(BF16)
    embed = jnp.einsum("pd,dc->pc", features, proj_weight, preferred_element_type=F32).astype(BF16)
    channels = proj_weight.shape[1]
    token_rows = seg // SIDE
    embed = embed.reshape(tiles, token_rows, SIDE, channels) * land.astype(BF16)[:, None, None, None]
    image = jnp.transpose(embed, (1, 0, 2, 3)).reshape(token_rows, tiles * SIDE, channels)

    image_low = lax.ppermute(image, AXES, forward)
    image_high = lax.ppermute(image, AXES, backward)
    place = jnp.stack([lax.axis_index(AXES) * rows, jnp.int32(total * rows)])
    early = early_stage(image, guide, conv_weights, conv_bias)
    return late_stage(
        place, image_low, image_high, guide_low, guide_high, early, conv_weights, conv_bias
    )


def solution(mesh):
    fine = Mesh(mesh.devices.reshape(2, 4, 2, 2, 4), AXES)
    in_specs = (
        P(TILE, MP, None),
        P(),
        P(),
        P(None, None, MP),
        P(MP, None),
        P(MP, None),
        P(MP, None),
        P(),
        P(TILE),
        P(),
        P(AXES, None, None),
        P(),
        P(),
    )
    return jax.shard_map(
        per_device, mesh=fine, in_specs=in_specs, out_specs=P(AXES, None, None), check_vma=False
    )
```

```python
import jax
import jax.numpy as jnp
from jax import lax
from jax.experimental import pallas as pl
from jax.experimental.pallas import tpu as pltpu
from jax.sharding import Mesh, PartitionSpec as P

HEAD = 64
SIDE = 16
AXES = ("yl", "x", "c", "yh", "z")
TILE = ("yl", "x", "c")
MP = ("yh", "z")
F32 = jnp.float32
BF16 = jnp.bfloat16
FAR = 64.0

def shift(block, axis, step):
    if axis == "y":
        def at(pos):
            return (pos % 2) * 2 + pos // 2

        pairs = [(at((pos + step) % 4), at(pos)) for pos in range(4)]
        return lax.ppermute(block, ("yl", "yh"), pairs)
    count = lax.axis_size(axis)
    return lax.ppermute(block, axis, [((i + step) % count, i) for i in range(count)])


def swap_cores(block):
    return lax.ppermute(block, "c", [(0, 1), (1, 0)])


def type_exchange(mine, sent):
    def at(pos, core):
        return ((pos % 2) * 2 + core) * 2 + pos // 2

    pairs = []
    for core in range(2):
        for pos in range(4):
            if pos // 2 == core:
                pairs.append((at(pos, core), at(3 - pos, core)))
    received = lax.ppermute(sent, ("yl", "c", "yh"), pairs)
    return jnp.where(lax.axis_index("yh") == lax.axis_index("c"), mine, received)


def across(half, end):
    return half, shift(half, "x", 1), shift(half, "x", 3), shift(half, "y", end)


NT = (((1,), (1,)), ((), ()))
PARTS = 4


def whole(memory):
    return pl.BlockSpec(memory_space=memory)


def normalise(values, gain):
    widened = values.astype(F32)
    centre = jnp.mean(widened, axis=-1, keepdims=True)
    spread = jnp.mean((widened - centre) ** 2, axis=-1, keepdims=True)
    return ((widened - centre) * lax.rsqrt(spread + 1e-06) * gain).astype(BF16)


def attention_kernel(
    parity, own, other, gain, *rest
):
    groups = rest[:8]
    near_out, far_out, held_base, held_plus, held_minus, held_two, normed, queries, values, context, sems = rest[8:]
    stacks = (held_base, held_plus, held_minus, held_two)
    copies = [
        pltpu.make_async_copy(
            group, stacks[at % 4].at[at // 4 * 2 : at // 4 * 2 + 2], sems.at[at]
        )
        for at, group in enumerate(groups)
    ]
    for copy in copies:
        copy.start()
    even = parity[0] == 0
    count = own.shape[0]
    normed[0:count] = normalise(own[...], gain[...])
    normed[count:] = normalise(other[...], gain[...])
    for copy in copies:
        copy.wait()
    width = own.shape[1]
    half = 4 * HEAD

    def pick(one, two, rows):
        first = one[:, rows].reshape(-1, width)
        return jnp.where(even, first, two[:, rows].reshape(-1, width))

    everything = slice(0, 2 * HEAD)
    upper = slice(0, HEAD)
    lower = slice(HEAD, 2 * HEAD)
    sides = (
        ((held_base, held_minus), (held_plus, held_base)),
        ((held_two, held_plus), (held_minus, held_two)),
    )
    for side, (qk, vo) in enumerate(sides):
        queries[:, side * 2 * half : (side + 1) * 2 * half] = lax.dot_general(
            normed[...], pick(*qk, everything), NT, preferred_element_type=F32
        ).astype(BF16)
        values[:, side * half : (side + 1) * half] = lax.dot_general(
            normed[...], pick(*vo, upper), NT, preferred_element_type=F32
        ).astype(BF16)
    for tile in range(2):
        rows = slice(tile * count, (tile + 1) * count)
        for head in range(8):
            q = queries[rows, head * 2 * HEAD : head * 2 * HEAD + HEAD] * BF16(HEAD ** (-0.5))
            k = queries[rows, head * 2 * HEAD + HEAD : (head + 1) * 2 * HEAD]
            v = values[rows, head * HEAD : (head + 1) * HEAD]
            scores = lax.dot_general(q, k, NT, preferred_element_type=F32)
            scores = jnp.exp(scores - jnp.max(scores, axis=-1, keepdims=True))
            soft = (scores * (1.0 / jnp.sum(scores, axis=-1, keepdims=True))).astype(BF16)
            context[rows, head * HEAD : (head + 1) * HEAD] = jnp.dot(
                soft, v, preferred_element_type=F32
            ).astype(BF16)
    total = None
    for side, (qk, vo) in enumerate(sides):
        term = jnp.dot(
            context[:, side * half : (side + 1) * half], pick(*vo, lower), preferred_element_type=F32
        )
        total = term if total is None else total + term
    near_out[...] = own[...].astype(F32) + total[:count]
    far_out[...] = total[count:].astype(BF16)


def attention(parity, own, other, gain, groups):
    count, width = own.shape
    stack = pltpu.VMEM((4, 2 * HEAD, width), BF16)
    return pl.pallas_call(
        attention_kernel,
        out_shape=(
            jax.ShapeDtypeStruct((count, width), F32),
            jax.ShapeDtypeStruct((count, width), BF16),
        ),
        in_specs=[whole(pltpu.SMEM)] + [whole(pltpu.VMEM)] * 3 + [whole(pl.ANY)] * 8,
        out_specs=(whole(pltpu.VMEM), whole(pltpu.VMEM)),
        scratch_shapes=[stack] * 4
        + [
            pltpu.VMEM((2 * count, width), BF16),
            pltpu.VMEM((2 * count, 16 * HEAD), BF16),
            pltpu.VMEM((2 * count, 8 * HEAD), BF16),
            pltpu.VMEM((2 * count, 8 * HEAD), BF16),
            pltpu.SemaphoreType.DMA((8,)),
        ],
        compiler_params=pltpu.CompilerParams(vmem_limit_bytes=24 * 2**20),
        cost_estimate=pl.CostEstimate(flops=3 * 10**9, bytes_accessed=7 * 10**6, transcendentals=2**20),
        name="attention",
    )(parity, own, other, gain, *groups)


def mlp_kernel(own, other, gain, weights, near_out, far_out, held, normed, total, sems):
    parts = sems.shape[0]
    size = weights.shape[0] // parts
    half = weights.shape[1] // 2
    copies = [
        pltpu.make_async_copy(
            weights.at[at * size : (at + 1) * size], held.at[at * size : (at + 1) * size], sems.at[at]
        )
        for at in range(parts)
    ]
    for copy in copies:
        copy.start()
    count, width = own.shape
    normed[0:count] = normalise(own[...], gain[...])
    normed[count:] = normalise(other[...], gain[...])
    for at in range(parts):
        copies[at].wait()
        w_in = held[at * size : (at + 1) * size, :half].reshape(-1, width)
        w_out = held[at * size : (at + 1) * size, half:].reshape(-1, width)
        hidden = lax.dot_general(normed[...], w_in, NT, preferred_element_type=F32)
        hidden = jax.nn.gelu(hidden).astype(BF16)
        term = jnp.dot(hidden, w_out, preferred_element_type=F32)
        if at == 0:
            total[...] = term
        else:
            total[...] += term
    near_out[...] = own[...].astype(F32) + total[:count]
    far_out[...] = total[count:].astype(BF16)


def mlp(own, other, gain, weights, parts=PARTS):
    count, width = own.shape
    return pl.pallas_call(
        mlp_kernel,
        out_shape=(
            jax.ShapeDtypeStruct((count, width), F32),
            jax.ShapeDtypeStruct((count, width), BF16),
        ),
        in_specs=[whole(pltpu.VMEM)] * 3 + [whole(pl.ANY)],
        out_specs=(whole(pltpu.VMEM), whole(pltpu.VMEM)),
        scratch_shapes=[
            pltpu.VMEM(weights.shape, BF16),
            pltpu.VMEM((2 * count, width), BF16),
            pltpu.VMEM((2 * count, width), F32),
            pltpu.SemaphoreType.DMA((parts,)),
        ],
        compiler_params=pltpu.CompilerParams(vmem_limit_bytes=56 * 2**20),
        cost_estimate=pl.CostEstimate(flops=5 * 10**9, bytes_accessed=12 * 10**6, transcendentals=2**20),
        name="mlp",
    )(own, other, gain, weights)


def spread_tokens(cols, tokens):
    pixel = lax.broadcasted_iota(jnp.int32, (cols, tokens), 0)
    token = lax.broadcasted_iota(jnp.int32, (cols, tokens), 1)
    return jnp.where(pixel // 2 == token, 1.0, 0.0).astype(BF16)


def conv_terms(terms, weights):
    sums = []
    for col in range(3):
        total = None
        for row, at in terms:
            term = jnp.dot(row, weights[at, col], preferred_element_type=F32)
            total = term if total is None else total + term
        sums.append(total)
    cols = sums[0].shape[0]
    column = lax.broadcasted_iota(jnp.int32, sums[0].shape, 0)
    left = jnp.where(column == 0, 0.0, pltpu.roll(sums[0], 1, 0))
    right = jnp.where(column == cols - 1, 0.0, pltpu.roll(sums[2], cols - 1, 0))
    return sums[1] + left + right


def near_terms(rows, out_row):
    return [(rows[at], at - out_row + 1) for at in sorted(rows) if -1 <= at - out_row <= 1]


def early_kernel(image, guide, weights, bias, guided, part_one, first, part_two, held, sems):
    copies = [pltpu.make_async_copy(weights.at[k], held.at[k], sems.at[k]) for k in range(2)]
    for copy in copies:
        copy.start()
    rows, cols, _ = guide.shape
    spread = spread_tokens(cols, image.shape[1])
    for at in range(rows // 2):
        wide = jnp.dot(spread, image[at], preferred_element_type=F32)
        for row in (2 * at, 2 * at + 1):
            guided[row] = (wide + guide[row].astype(F32)).astype(BF16)
    own = {at: guided[at] for at in range(rows)}
    copies[0].wait()
    for at in range(rows - 2):
        value = conv_terms(near_terms(own, at + 1), held.at[0]) + bias[0:1, :]
        first[at] = jax.nn.gelu(value).astype(BF16)
    for at, row in enumerate((-1, 0, rows - 1, rows)):
        part_one[at] = conv_terms(near_terms(own, row), held.at[0]) + bias[0:1, :]
    copies[1].wait()
    inner = {at + 1: first[at] for at in range(rows - 2)}
    for at in range(rows):
        part_two[at] = conv_terms(near_terms(inner, at), held.at[1]) + bias[1:2, :]


def late_kernel(
    place, image_low, image_high, guide_low, guide_high, guided, part_one, first, part_two, weights, bias,
    out, outer, second, held, sems
):
    copies = [pltpu.make_async_copy(weights.at[k], held.at[k], sems.at[k]) for k in range(3)]
    for copy in copies:
        copy.start()
    rows, cols, _ = guided.shape
    spread = spread_tokens(cols, image_low.shape[1])
    beside = {}
    for source, addend, top in ((image_low, guide_low, -4), (image_high, guide_high, rows)):
        for at in range(2):
            wide = jnp.dot(spread, source[at], preferred_element_type=F32)
            for row in (top + 2 * at, top + 2 * at + 1):
                if -3 <= row < rows + 3:
                    added = addend[row + 3 if row < 0 else row - rows]
                    beside[row] = (wide + added.astype(F32)).astype(BF16)
    first_row = place[0]
    last_row = place[1]

    def inside(value, row):
        at = first_row + row
        return jnp.where(jnp.logical_and(at >= 0, at < last_row), value, 0.0).astype(BF16)

    copies[0].wait()
    layer = {}
    saved = {-1: 0, 0: 1, rows - 1: 2, rows: 3}
    for at, row in enumerate((-2, -1, 0, rows - 1, rows, rows + 1)):
        value = conv_terms(near_terms(beside, row), held.at[0])
        value = value + (part_one[saved[row]] if row in saved else bias[0:1, :])
        outer[at] = inside(jax.nn.gelu(value), row)
        layer[row] = outer.at[at]
    copies[1].wait()
    shown = {}
    for row in range(-1, rows + 1):
        value = conv_terms([(ref[...], at) for ref, at in near_terms(layer, row)], held.at[1]) if near_terms(
            layer, row
        ) else 0.0
        value = value + (part_two[row] if 0 <= row < rows else bias[1:2, :])
        second[row + 1] = inside(jax.nn.gelu(value), row)
        shown[row] = second.at[row + 1]
    copies[2].wait()
    for row in range(rows):
        value = conv_terms([(ref[...], at) for ref, at in near_terms(shown, row)], held.at[2])
        out[row] = (value + bias[2:3, :] + guided[row].astype(F32)).astype(BF16)


def early_stage(image, guide, weights, bias):
    rows, cols, channels = guide.shape
    wide = (rows, cols, channels)
    return pl.pallas_call(
        early_kernel,
        out_shape=(
            jax.ShapeDtypeStruct(wide, BF16),
            jax.ShapeDtypeStruct((4, cols, channels), F32),
            jax.ShapeDtypeStruct((rows - 2, cols, channels), BF16),
            jax.ShapeDtypeStruct(wide, F32),
        ),
        in_specs=[whole(pltpu.VMEM)] * 2 + [whole(pl.ANY), whole(pltpu.VMEM)],
        out_specs=(whole(pltpu.VMEM),) * 4,
        scratch_shapes=[
            pltpu.VMEM((2,) + weights.shape[1:], BF16),
            pltpu.SemaphoreType.DMA((2,)),
        ],
        compiler_params=pltpu.CompilerParams(vmem_limit_bytes=24 * 2**20),
        cost_estimate=pl.CostEstimate(flops=3 * 10**9, bytes_accessed=4 * 10**6, transcendentals=2**20),
        name="early",
    )(image, guide, weights, bias)


def late_stage(place, image_low, image_high, guide_low, guide_high, early, weights, bias):
    rows, cols, channels = early[0].shape
    return pl.pallas_call(
        late_kernel,
        out_shape=jax.ShapeDtypeStruct((rows, cols, channels), BF16),
        in_specs=[whole(pltpu.SMEM)] + [whole(pltpu.VMEM)] * 8 + [whole(pl.ANY), whole(pltpu.VMEM)],
        out_specs=whole(pltpu.VMEM),
        scratch_shapes=[
            pltpu.VMEM((6, cols, channels), BF16),
            pltpu.VMEM((rows + 2, cols, channels), BF16),
            pltpu.VMEM(weights.shape, BF16),
            pltpu.SemaphoreType.DMA((3,)),
        ],
        compiler_params=pltpu.CompilerParams(vmem_limit_bytes=32 * 2**20),
        cost_estimate=pl.CostEstimate(flops=4 * 10**9, bytes_accessed=6 * 10**6, transcendentals=2**20),
        name="late",
    )(place, image_low, image_high, guide_low, guide_high, *early, weights, bias)


def per_device(
    tokens,
    ln_gain_one,
    ln_gain_two,
    qkv_weight,
    out_weight,
    in_weight,
    mlp_out_weight,
    proj_weight,
    land_mask,
    placement,
    guide,
    conv_weights,
    conv_bias,
):
    tiles, seg, width = tokens.shape
    groups = lax.axis_size(TILE)
    here = lax.axis_index(TILE)

    x_at = lax.axis_index("x")
    y_at = lax.axis_index("yh") * 2 + lax.axis_index("yl")
    colour_x = (x_at + 2 * y_at) % 4
    colour_x_beside = (x_at + 2 * (3 - y_at)) % 4

    by_head = jnp.transpose(qkv_weight, (0, 2, 1)).reshape(3, 2, HEAD, width)
    out_heads = out_weight.reshape(2, HEAD, width)
    attn_all = jnp.stack(
        [by_head[0], by_head[1], by_head[2], out_heads], axis=1
    ).reshape(4, 2 * HEAD, width)
    attn_piece = type_exchange(attn_all[colour_x], attn_all[colour_x_beside])
    near_half = jnp.stack([attn_piece, shift(attn_piece, "z", 1)])
    far_half = jnp.stack([shift(attn_piece, "z", 3), shift(attn_piece, "z", 2)])
    attn_w = across(near_half, 1) + across(far_half, 3)

    slice_rows = in_weight.shape[0] // 16
    start = (lax.axis_index("c") * 8 + lax.axis_index(("x", "yl"))) * slice_rows
    mlp_own = jnp.concatenate(
        [
            lax.dynamic_slice_in_dim(in_weight, start, slice_rows, 0),
            lax.dynamic_slice_in_dim(mlp_out_weight, start, slice_rows, 0),
        ],
        axis=0,
    )
    mlp_w = lax.all_gather(mlp_own, ("x", "yh", "yl", "z"), axis=0, tiled=False)

    slab_all = placement // tiles
    column_all = placement % tiles
    group_all = jnp.arange(placement.shape[0], dtype=jnp.int32) // tiles
    slab_local = lax.dynamic_slice_in_dim(slab_all, here * tiles, tiles, 0)
    selector = (slab_local[None, :] == jnp.arange(groups, dtype=jnp.int32)[:, None]).astype(BF16)
    in_slab = slab_all == here
    column_hot = (
        column_all[:, None] == jnp.arange(tiles, dtype=jnp.int32)[None, :]
    ) & in_slab[:, None]
    group_hot = group_all[:, None] == jnp.arange(groups, dtype=jnp.int32)[None, :]
    arrange = jnp.einsum(
        "tk,tg->kg", column_hot.astype(F32), group_hot.astype(F32)
    ).astype(BF16)
    marked = jnp.where((land_mask == 0)[:, None, None], jnp.asarray(FAR, BF16), tokens)
    marked, _ = lax.optimization_barrier((marked, attn_piece))
    outgoing = jnp.einsum("sj,jpd->spd", selector, marked, preferred_element_type=F32).astype(BF16)
    incoming = lax.all_to_all(outgoing, TILE, split_axis=0, concat_axis=0, tiled=True)
    slab_tokens = jnp.einsum(
        "kg,gpd->kpd", arrange, incoming, preferred_element_type=F32
    ).astype(BF16)
    land = slab_tokens[:, 0, 0] < FAR / 2
    slab_tokens, _ = lax.optimization_barrier((slab_tokens, far_half))
    tile_tokens = lax.all_to_all(slab_tokens, MP, split_axis=0, concat_axis=0, tiled=True)
    tile_tokens = tile_tokens.reshape(tiles * seg, width)
    other_tokens = swap_cores(tile_tokens)

    count = tiles * seg
    near, far = attention(
        (x_at % 2).astype(jnp.int32).reshape(1),
        tile_tokens,
        other_tokens,
        ln_gain_one.reshape(1, width),
        attn_w,
    )
    middle = (near + swap_cores(far).astype(F32)).astype(BF16)

    total = lax.axis_size(AXES)
    forward = [(i, i + 1) for i in range(total - 1)]
    backward = [(b, a) for a, b in forward]
    rows = guide.shape[0]
    guide_ends, _ = lax.optimization_barrier(((guide[rows - 3 :], guide[:3]), far))
    guide_low = lax.ppermute(guide_ends[0], AXES, forward)
    guide_high = lax.ppermute(guide_ends[1], AXES, backward)

    middle = lax.all_to_all(
        middle.reshape(tiles, seg, width), MP, split_axis=0, concat_axis=0, tiled=True
    ).reshape(count, width)
    middle, guide_low, guide_high = lax.optimization_barrier((middle, guide_low, guide_high))
    near, far = mlp(middle, swap_cores(middle), ln_gain_two.reshape(1, width), mlp_w)
    features = (near + swap_cores(far).astype(F32)).astype(BF16)
    embed = jnp.einsum("pd,dc->pc", features, proj_weight, preferred_element_type=F32).astype(BF16)
    channels = proj_weight.shape[1]
    token_rows = seg // SIDE
    embed = embed.reshape(tiles, token_rows, SIDE, channels) * land.astype(BF16)[:, None, None, None]
    image = jnp.transpose(embed, (1, 0, 2, 3)).reshape(token_rows, tiles * SIDE, channels)

    image_low = lax.ppermute(image, AXES, forward)
    image_high = lax.ppermute(image, AXES, backward)
    place = jnp.stack([lax.axis_index(AXES) * rows, jnp.int32(total * rows)])
    early = early_stage(image, guide, conv_weights, conv_bias)
    return late_stage(
        place, image_low, image_high, guide_low, guide_high, early, conv_weights, conv_bias
    )


def solution(mesh):
    fine = Mesh(mesh.devices.reshape(2, 4, 2, 2, 4), AXES)
    in_specs = (
        P(TILE, MP, None),
        P(),
        P(),
        P(None, None, MP),
        P(MP, None),
        P(MP, None),
        P(MP, None),
        P(),
        P(TILE),
        P(),
        P(AXES, None, None),
        P(),
        P(),
    )
    return jax.shard_map(
        per_device, mesh=fine, in_specs=in_specs, out_specs=P(AXES, None, None), check_vma=False
    )
```

```python
import jax
import jax.numpy as jnp
from jax import lax
from jax.experimental import pallas as pl
from jax.experimental.pallas import tpu as pltpu
from jax.sharding import Mesh, PartitionSpec as P

HEAD = 64
SIDE = 16
AXES = ("yl", "x", "c", "yh", "z")
TILE = ("yl", "x", "c")
MP = ("yh", "z")
F32 = jnp.float32
BF16 = jnp.bfloat16
FAR = 64.0

def shift(block, axis, step):
    if axis == "y":
        def at(pos):
            return (pos % 2) * 2 + pos // 2

        pairs = [(at((pos + step) % 4), at(pos)) for pos in range(4)]
        return lax.ppermute(block, ("yl", "yh"), pairs)
    count = lax.axis_size(axis)
    return lax.ppermute(block, axis, [((i + step) % count, i) for i in range(count)])


def swap_cores(block):
    return lax.ppermute(block, "c", [(0, 1), (1, 0)])


def type_exchange(mine, sent):
    def at(pos, core):
        return ((pos % 2) * 2 + core) * 2 + pos // 2

    pairs = []
    for core in range(2):
        for pos in range(4):
            if pos // 2 == core:
                pairs.append((at(pos, core), at(3 - pos, core)))
    received = lax.ppermute(sent, ("yl", "c", "yh"), pairs)
    return jnp.where(lax.axis_index("yh") == lax.axis_index("c"), mine, received)


def across(half, end):
    return half, shift(half, "x", 1), shift(half, "x", 3), shift(half, "y", end)


NT = (((1,), (1,)), ((), ()))
PARTS = 4


def whole(memory):
    return pl.BlockSpec(memory_space=memory)


def normalise(values, gain):
    widened = values.astype(F32)
    centre = jnp.mean(widened, axis=-1, keepdims=True)
    spread = jnp.mean((widened - centre) ** 2, axis=-1, keepdims=True)
    return ((widened - centre) * lax.rsqrt(spread + 1e-06) * gain).astype(BF16)


def attention_kernel(
    parity, own, other, gain, *rest
):
    groups = rest[:8]
    near_out, far_out, held_base, held_plus, held_minus, held_two, normed, queries, values, context, sems = rest[8:]
    stacks = (held_base, held_plus, held_minus, held_two)
    copies = [
        pltpu.make_async_copy(
            group, stacks[at % 4].at[at // 4 * 2 : at // 4 * 2 + 2], sems.at[at]
        )
        for at, group in enumerate(groups)
    ]
    for copy in copies:
        copy.start()
    even = parity[0] == 0
    count = own.shape[0]
    normed[0:count] = normalise(own[...], gain[...])
    normed[count:] = normalise(other[...], gain[...])
    for copy in copies:
        copy.wait()
    width = own.shape[1]
    half = 4 * HEAD

    def pick(one, two, rows):
        first = one[:, rows].reshape(-1, width)
        return jnp.where(even, first, two[:, rows].reshape(-1, width))

    everything = slice(0, 2 * HEAD)
    upper = slice(0, HEAD)
    lower = slice(HEAD, 2 * HEAD)
    sides = (
        ((held_base, held_minus), (held_plus, held_base)),
        ((held_two, held_plus), (held_minus, held_two)),
    )
    for side, (qk, vo) in enumerate(sides):
        queries[:, side * 2 * half : (side + 1) * 2 * half] = lax.dot_general(
            normed[...], pick(*qk, everything), NT, preferred_element_type=F32
        ).astype(BF16)
        values[:, side * half : (side + 1) * half] = lax.dot_general(
            normed[...], pick(*vo, upper), NT, preferred_element_type=F32
        ).astype(BF16)
    for tile in range(2):
        rows = slice(tile * count, (tile + 1) * count)
        for head in range(8):
            q = queries[rows, head * 2 * HEAD : head * 2 * HEAD + HEAD] * BF16(HEAD ** (-0.5))
            k = queries[rows, head * 2 * HEAD + HEAD : (head + 1) * 2 * HEAD]
            v = values[rows, head * HEAD : (head + 1) * HEAD]
            scores = lax.dot_general(q, k, NT, preferred_element_type=F32)
            scores = jnp.exp(scores - jnp.max(scores, axis=-1, keepdims=True))
            soft = (scores * (1.0 / jnp.sum(scores, axis=-1, keepdims=True))).astype(BF16)
            context[rows, head * HEAD : (head + 1) * HEAD] = jnp.dot(
                soft, v, preferred_element_type=F32
            ).astype(BF16)
    total = None
    for side, (qk, vo) in enumerate(sides):
        term = jnp.dot(
            context[:, side * half : (side + 1) * half], pick(*vo, lower), preferred_element_type=F32
        )
        total = term if total is None else total + term
    near_out[...] = own[...].astype(F32) + total[:count]
    far_out[...] = total[count:].astype(BF16)


def attention(parity, own, other, gain, groups):
    count, width = own.shape
    stack = pltpu.VMEM((4, 2 * HEAD, width), BF16)
    return pl.pallas_call(
        attention_kernel,
        out_shape=(
            jax.ShapeDtypeStruct((count, width), F32),
            jax.ShapeDtypeStruct((count, width), BF16),
        ),
        in_specs=[whole(pltpu.SMEM)] + [whole(pltpu.VMEM)] * 3 + [whole(pl.ANY)] * 8,
        out_specs=(whole(pltpu.VMEM), whole(pltpu.VMEM)),
        scratch_shapes=[stack] * 4
        + [
            pltpu.VMEM((2 * count, width), BF16),
            pltpu.VMEM((2 * count, 16 * HEAD), BF16),
            pltpu.VMEM((2 * count, 8 * HEAD), BF16),
            pltpu.VMEM((2 * count, 8 * HEAD), BF16),
            pltpu.SemaphoreType.DMA((8,)),
        ],
        compiler_params=pltpu.CompilerParams(vmem_limit_bytes=24 * 2**20),
        cost_estimate=pl.CostEstimate(flops=3 * 10**9, bytes_accessed=7 * 10**6, transcendentals=2**20),
        name="attention",
    )(parity, own, other, gain, *groups)


def mlp_kernel(own, other, gain, weights, near_out, far_out, held, normed, total, sems):
    parts = sems.shape[0]
    size = weights.shape[0] // parts
    half = weights.shape[1] // 2
    copies = [
        pltpu.make_async_copy(
            weights.at[at * size : (at + 1) * size], held.at[at * size : (at + 1) * size], sems.at[at]
        )
        for at in range(parts)
    ]
    for copy in copies:
        copy.start()
    count, width = own.shape
    normed[0:count] = normalise(own[...], gain[...])
    normed[count:] = normalise(other[...], gain[...])
    for at in range(parts):
        copies[at].wait()
        w_in = held[at * size : (at + 1) * size, :half].reshape(-1, width)
        w_out = held[at * size : (at + 1) * size, half:].reshape(-1, width)
        hidden = lax.dot_general(normed[...], w_in, NT, preferred_element_type=F32)
        hidden = jax.nn.gelu(hidden).astype(BF16)
        term = jnp.dot(hidden, w_out, preferred_element_type=F32)
        if at == 0:
            total[...] = term
        else:
            total[...] += term
    near_out[...] = own[...].astype(F32) + total[:count]
    far_out[...] = total[count:].astype(BF16)


def mlp(own, other, gain, weights, parts=PARTS):
    count, width = own.shape
    return pl.pallas_call(
        mlp_kernel,
        out_shape=(
            jax.ShapeDtypeStruct((count, width), F32),
            jax.ShapeDtypeStruct((count, width), BF16),
        ),
        in_specs=[whole(pltpu.VMEM)] * 3 + [whole(pl.ANY)],
        out_specs=(whole(pltpu.VMEM), whole(pltpu.VMEM)),
        scratch_shapes=[
            pltpu.VMEM(weights.shape, BF16),
            pltpu.VMEM((2 * count, width), BF16),
            pltpu.VMEM((2 * count, width), F32),
            pltpu.SemaphoreType.DMA((parts,)),
        ],
        compiler_params=pltpu.CompilerParams(vmem_limit_bytes=56 * 2**20),
        cost_estimate=pl.CostEstimate(flops=5 * 10**9, bytes_accessed=12 * 10**6, transcendentals=2**20),
        name="mlp",
    )(own, other, gain, weights)


def spread_tokens(cols, tokens):
    pixel = lax.broadcasted_iota(jnp.int32, (cols, tokens), 0)
    token = lax.broadcasted_iota(jnp.int32, (cols, tokens), 1)
    return jnp.where(pixel // 2 == token, 1.0, 0.0).astype(BF16)


def conv_terms(terms, weights):
    sums = []
    for col in range(3):
        total = None
        for row, at in terms:
            term = jnp.dot(row, weights[at, col], preferred_element_type=F32)
            total = term if total is None else total + term
        sums.append(total)
    cols = sums[0].shape[0]
    column = lax.broadcasted_iota(jnp.int32, sums[0].shape, 0)
    left = jnp.where(column == 0, 0.0, pltpu.roll(sums[0], 1, 0))
    right = jnp.where(column == cols - 1, 0.0, pltpu.roll(sums[2], cols - 1, 0))
    return sums[1] + left + right


def near_terms(rows, out_row):
    return [(rows[at], at - out_row + 1) for at in sorted(rows) if -1 <= at - out_row <= 1]


def early_kernel(image, guide, weights, bias, guided, part_one, first, part_two, held, sems):
    copies = [pltpu.make_async_copy(weights.at[k], held.at[k], sems.at[k]) for k in range(2)]
    for copy in copies:
        copy.start()
    rows, cols, _ = guide.shape
    spread = spread_tokens(cols, image.shape[1])
    for at in range(rows // 2):
        wide = jnp.dot(spread, image[at], preferred_element_type=F32)
        for row in (2 * at, 2 * at + 1):
            guided[row] = (wide + guide[row].astype(F32)).astype(BF16)
    own = {at: guided[at] for at in range(rows)}
    copies[0].wait()
    for at in range(rows - 2):
        value = conv_terms(near_terms(own, at + 1), held.at[0]) + bias[0:1, :]
        first[at] = jax.nn.gelu(value).astype(BF16)
    for at, row in enumerate((-1, 0, rows - 1, rows)):
        part_one[at] = conv_terms(near_terms(own, row), held.at[0]) + bias[0:1, :]
    copies[1].wait()
    inner = {at + 1: first[at] for at in range(rows - 2)}
    for at in range(rows):
        part_two[at] = conv_terms(near_terms(inner, at), held.at[1]) + bias[1:2, :]


def late_kernel(
    place, image_low, image_high, guide_low, guide_high, guided, part_one, first, part_two, weights, bias,
    out, outer, second, held, sems
):
    copies = [pltpu.make_async_copy(weights.at[k], held.at[k], sems.at[k]) for k in range(3)]
    for copy in copies:
        copy.start()
    rows, cols, _ = guided.shape
    spread = spread_tokens(cols, image_low.shape[1])
    beside = {}
    for source, addend, top in ((image_low, guide_low, -4), (image_high, guide_high, rows)):
        for at in range(2):
            wide = jnp.dot(spread, source[at], preferred_element_type=F32)
            for row in (top + 2 * at, top + 2 * at + 1):
                if -3 <= row < rows + 3:
                    added = addend[row + 3 if row < 0 else row - rows]
                    beside[row] = (wide + added.astype(F32)).astype(BF16)
    first_row = place[0]
    last_row = place[1]

    def inside(value, row):
        at = first_row + row
        return jnp.where(jnp.logical_and(at >= 0, at < last_row), value, 0.0).astype(BF16)

    copies[0].wait()
    layer = {}
    saved = {-1: 0, 0: 1, rows - 1: 2, rows: 3}
    for at, row in enumerate((-2, -1, 0, rows - 1, rows, rows + 1)):
        value = conv_terms(near_terms(beside, row), held.at[0])
        value = value + (part_one[saved[row]] if row in saved else bias[0:1, :])
        outer[at] = inside(jax.nn.gelu(value), row)
        layer[row] = outer.at[at]
    copies[1].wait()
    shown = {}
    for row in range(-1, rows + 1):
        value = conv_terms([(ref[...], at) for ref, at in near_terms(layer, row)], held.at[1]) if near_terms(
            layer, row
        ) else 0.0
        value = value + (part_two[row] if 0 <= row < rows else bias[1:2, :])
        second[row + 1] = inside(jax.nn.gelu(value), row)
        shown[row] = second.at[row + 1]
    copies[2].wait()
    for row in range(rows):
        value = conv_terms([(ref[...], at) for ref, at in near_terms(shown, row)], held.at[2])
        out[row] = (value + bias[2:3, :] + guided[row].astype(F32)).astype(BF16)


def early_stage(image, guide, weights, bias):
    rows, cols, channels = guide.shape
    wide = (rows, cols, channels)
    return pl.pallas_call(
        early_kernel,
        out_shape=(
            jax.ShapeDtypeStruct(wide, BF16),
            jax.ShapeDtypeStruct((4, cols, channels), F32),
            jax.ShapeDtypeStruct((rows - 2, cols, channels), BF16),
            jax.ShapeDtypeStruct(wide, F32),
        ),
        in_specs=[whole(pltpu.VMEM)] * 2 + [whole(pl.ANY), whole(pltpu.VMEM)],
        out_specs=(whole(pltpu.VMEM),) * 4,
        scratch_shapes=[
            pltpu.VMEM((2,) + weights.shape[1:], BF16),
            pltpu.SemaphoreType.DMA((2,)),
        ],
        compiler_params=pltpu.CompilerParams(vmem_limit_bytes=24 * 2**20),
        cost_estimate=pl.CostEstimate(flops=3 * 10**9, bytes_accessed=4 * 10**6, transcendentals=2**20),
        name="early",
    )(image, guide, weights, bias)


def late_stage(place, image_low, image_high, guide_low, guide_high, early, weights, bias):
    rows, cols, channels = early[0].shape
    return pl.pallas_call(
        late_kernel,
        out_shape=jax.ShapeDtypeStruct((rows, cols, channels), BF16),
        in_specs=[whole(pltpu.SMEM)] + [whole(pltpu.VMEM)] * 8 + [whole(pl.ANY), whole(pltpu.VMEM)],
        out_specs=whole(pltpu.VMEM),
        scratch_shapes=[
            pltpu.VMEM((6, cols, channels), BF16),
            pltpu.VMEM((rows + 2, cols, channels), BF16),
            pltpu.VMEM(weights.shape, BF16),
            pltpu.SemaphoreType.DMA((3,)),
        ],
        compiler_params=pltpu.CompilerParams(vmem_limit_bytes=32 * 2**20),
        cost_estimate=pl.CostEstimate(flops=4 * 10**9, bytes_accessed=6 * 10**6, transcendentals=2**20),
        name="late",
    )(place, image_low, image_high, guide_low, guide_high, *early, weights, bias)


def per_device(
    tokens,
    ln_gain_one,
    ln_gain_two,
    qkv_weight,
    out_weight,
    in_weight,
    mlp_out_weight,
    proj_weight,
    land_mask,
    placement,
    guide,
    conv_weights,
    conv_bias,
):
    tiles, seg, width = tokens.shape
    groups = lax.axis_size(TILE)
    here = lax.axis_index(TILE)

    x_at = lax.axis_index("x")
    y_at = lax.axis_index("yh") * 2 + lax.axis_index("yl")
    colour_x = (x_at + 2 * y_at) % 4
    colour_x_beside = (x_at + 2 * (3 - y_at)) % 4

    by_head = jnp.transpose(qkv_weight, (0, 2, 1)).reshape(3, 2, HEAD, width)
    out_heads = out_weight.reshape(2, HEAD, width)
    attn_all = jnp.stack(
        [by_head[0], by_head[1], by_head[2], out_heads], axis=1
    ).reshape(4, 2 * HEAD, width)
    attn_piece = type_exchange(attn_all[colour_x], attn_all[colour_x_beside])
    near_half = jnp.stack([attn_piece, shift(attn_piece, "z", 1)])
    far_half = jnp.stack([shift(attn_piece, "z", 3), shift(attn_piece, "z", 2)])
    attn_w = across(near_half, 1) + across(far_half, 3)

    slice_rows = in_weight.shape[0] // 4
    start = (lax.axis_index("c") * 2 + lax.axis_index("yl")) * slice_rows
    mlp_own = jnp.concatenate(
        [
            lax.dynamic_slice_in_dim(in_weight, start, slice_rows, 0),
            lax.dynamic_slice_in_dim(mlp_out_weight, start, slice_rows, 0),
        ],
        axis=0,
    )
    mlp_w = lax.all_gather(mlp_own, ("yh", "yl", "z"), axis=0, tiled=False)

    slab_all = placement // tiles
    column_all = placement % tiles
    group_all = jnp.arange(placement.shape[0], dtype=jnp.int32) // tiles
    slab_local = lax.dynamic_slice_in_dim(slab_all, here * tiles, tiles, 0)
    selector = (slab_local[None, :] == jnp.arange(groups, dtype=jnp.int32)[:, None]).astype(BF16)
    in_slab = slab_all == here
    column_hot = (
        column_all[:, None] == jnp.arange(tiles, dtype=jnp.int32)[None, :]
    ) & in_slab[:, None]
    group_hot = group_all[:, None] == jnp.arange(groups, dtype=jnp.int32)[None, :]
    arrange = jnp.einsum(
        "tk,tg->kg", column_hot.astype(F32), group_hot.astype(F32)
    ).astype(BF16)
    marked = jnp.where((land_mask == 0)[:, None, None], jnp.asarray(FAR, BF16), tokens)
    marked, _ = lax.optimization_barrier((marked, attn_piece))
    outgoing = jnp.einsum("sj,jpd->spd", selector, marked, preferred_element_type=F32).astype(BF16)
    incoming = lax.all_to_all(outgoing, TILE, split_axis=0, concat_axis=0, tiled=True)
    slab_tokens = jnp.einsum(
        "kg,gpd->kpd", arrange, incoming, preferred_element_type=F32
    ).astype(BF16)
    land = slab_tokens[:, 0, 0] < FAR / 2
    slab_tokens, _ = lax.optimization_barrier((slab_tokens, far_half))
    tile_tokens = lax.all_to_all(slab_tokens, MP, split_axis=0, concat_axis=0, tiled=True)
    tile_tokens = tile_tokens.reshape(tiles * seg, width)
    other_tokens = swap_cores(tile_tokens)

    count = tiles * seg
    near, far = attention(
        (x_at % 2).astype(jnp.int32).reshape(1),
        tile_tokens,
        other_tokens,
        ln_gain_one.reshape(1, width),
        attn_w,
    )
    middle = (near + swap_cores(far).astype(F32)).astype(BF16)

    total = lax.axis_size(AXES)
    forward = [(i, i + 1) for i in range(total - 1)]
    backward = [(b, a) for a, b in forward]
    rows = guide.shape[0]
    guide_ends, _ = lax.optimization_barrier(((guide[rows - 3 :], guide[:3]), far))
    guide_low = lax.ppermute(guide_ends[0], AXES, forward)
    guide_high = lax.ppermute(guide_ends[1], AXES, backward)

    middle = lax.all_to_all(
        middle.reshape(tiles, seg, width), MP, split_axis=0, concat_axis=0, tiled=True
    ).reshape(count, width)
    middle, guide_low, guide_high = lax.optimization_barrier((middle, guide_low, guide_high))
    near, far = mlp(middle, swap_cores(middle), ln_gain_two.reshape(1, width), mlp_w)
    features = (near + swap_cores(far).astype(F32)).astype(BF16)
    embed = jnp.einsum("pd,dc->pc", features, proj_weight, preferred_element_type=F32).astype(BF16)
    channels = proj_weight.shape[1]
    token_rows = seg // SIDE
    embed = embed.reshape(tiles, token_rows, SIDE, channels) * land.astype(BF16)[:, None, None, None]
    image = jnp.transpose(embed, (1, 0, 2, 3)).reshape(token_rows, tiles * SIDE, channels)

    image_low = lax.ppermute(image, AXES, forward)
    image_high = lax.ppermute(image, AXES, backward)
    place = jnp.stack([lax.axis_index(AXES) * rows, jnp.int32(total * rows)])
    early = early_stage(image, guide, conv_weights, conv_bias)
    return late_stage(
        place, image_low, image_high, guide_low, guide_high, early, conv_weights, conv_bias
    )


def solution(mesh):
    fine = Mesh(mesh.devices.reshape(2, 4, 2, 2, 4), AXES)
    in_specs = (
        P(TILE, MP, None),
        P(),
        P(),
        P(None, None, MP),
        P(MP, None),
        P(MP, None),
        P(MP, None),
        P(),
        P(TILE),
        P(),
        P(AXES, None, None),
        P(),
        P(),
    )
    return jax.shard_map(
        per_device, mesh=fine, in_specs=in_specs, out_specs=P(AXES, None, None), check_vma=False
    )
```

```python
import jax
import jax.numpy as jnp
from jax import lax
from jax.experimental import pallas as pl
from jax.experimental.pallas import tpu as pltpu
from jax.sharding import Mesh, PartitionSpec as P

HEAD = 64
SIDE = 16
AXES = ("yl", "x", "c", "yh", "z")
TILE = ("yl", "x", "c")
MP = ("yh", "z")
F32 = jnp.float32
BF16 = jnp.bfloat16
FAR = 64.0

def shift(block, axis, step):
    if axis == "y":
        def at(pos):
            return (pos % 2) * 2 + pos // 2

        pairs = [(at((pos + step) % 4), at(pos)) for pos in range(4)]
        return lax.ppermute(block, ("yl", "yh"), pairs)
    count = lax.axis_size(axis)
    return lax.ppermute(block, axis, [((i + step) % count, i) for i in range(count)])


def swap_cores(block):
    return lax.ppermute(block, "c", [(0, 1), (1, 0)])


def type_exchange(mine, sent):
    def at(pos, core):
        return ((pos % 2) * 2 + core) * 2 + pos // 2

    pairs = []
    for core in range(2):
        for pos in range(4):
            if pos // 2 == core:
                pairs.append((at(pos, core), at(3 - pos, core)))
    received = lax.ppermute(sent, ("yl", "c", "yh"), pairs)
    return jnp.where(lax.axis_index("yh") == lax.axis_index("c"), mine, received)


def across(half, end):
    return half, shift(half, "x", 1), shift(half, "x", 3), shift(half, "y", end)


NT = (((1,), (1,)), ((), ()))
PARTS = 4


def whole(memory):
    return pl.BlockSpec(memory_space=memory)


def normalise(values, gain):
    widened = values.astype(F32)
    centre = jnp.mean(widened, axis=-1, keepdims=True)
    spread = jnp.mean((widened - centre) ** 2, axis=-1, keepdims=True)
    return ((widened - centre) * lax.rsqrt(spread + 1e-06) * gain).astype(BF16)


def attention_kernel(
    parity, own, other, gain, *rest
):
    groups = rest[:8]
    near_out, far_out, held_base, held_plus, held_minus, held_two, normed, queries, values, context, sems = rest[8:]
    stacks = (held_base, held_plus, held_minus, held_two)
    copies = [
        pltpu.make_async_copy(
            group, stacks[at % 4].at[at // 4 * 2 : at // 4 * 2 + 2], sems.at[at]
        )
        for at, group in enumerate(groups)
    ]
    for copy in copies:
        copy.start()
    even = parity[0] == 0
    count = own.shape[0]
    normed[0:count] = normalise(own[...], gain[...])
    normed[count:] = normalise(other[...], gain[...])
    for copy in copies:
        copy.wait()
    width = own.shape[1]
    half = 4 * HEAD

    def pick(one, two, rows):
        first = one[:, rows].reshape(-1, width)
        return jnp.where(even, first, two[:, rows].reshape(-1, width))

    everything = slice(0, 2 * HEAD)
    upper = slice(0, HEAD)
    lower = slice(HEAD, 2 * HEAD)
    sides = (
        ((held_base, held_minus), (held_plus, held_base)),
        ((held_two, held_plus), (held_minus, held_two)),
    )
    for side, (qk, vo) in enumerate(sides):
        queries[:, side * 2 * half : (side + 1) * 2 * half] = lax.dot_general(
            normed[...], pick(*qk, everything), NT, preferred_element_type=F32
        ).astype(BF16)
        values[:, side * half : (side + 1) * half] = lax.dot_general(
            normed[...], pick(*vo, upper), NT, preferred_element_type=F32
        ).astype(BF16)
    for tile in range(2):
        rows = slice(tile * count, (tile + 1) * count)
        for head in range(8):
            q = queries[rows, head * 2 * HEAD : head * 2 * HEAD + HEAD] * BF16(HEAD ** (-0.5))
            k = queries[rows, head * 2 * HEAD + HEAD : (head + 1) * 2 * HEAD]
            v = values[rows, head * HEAD : (head + 1) * HEAD]
            scores = lax.dot_general(q, k, NT, preferred_element_type=F32)
            scores = jnp.exp(scores - jnp.max(scores, axis=-1, keepdims=True))
            soft = (scores * (1.0 / jnp.sum(scores, axis=-1, keepdims=True))).astype(BF16)
            context[rows, head * HEAD : (head + 1) * HEAD] = jnp.dot(
                soft, v, preferred_element_type=F32
            ).astype(BF16)
    total = None
    for side, (qk, vo) in enumerate(sides):
        term = jnp.dot(
            context[:, side * half : (side + 1) * half], pick(*vo, lower), preferred_element_type=F32
        )
        total = term if total is None else total + term
    near_out[...] = own[...].astype(F32) + total[:count]
    far_out[...] = total[count:].astype(BF16)


def attention(parity, own, other, gain, groups):
    count, width = own.shape
    stack = pltpu.VMEM((4, 2 * HEAD, width), BF16)
    return pl.pallas_call(
        attention_kernel,
        out_shape=(
            jax.ShapeDtypeStruct((count, width), F32),
            jax.ShapeDtypeStruct((count, width), BF16),
        ),
        in_specs=[whole(pltpu.SMEM)] + [whole(pltpu.VMEM)] * 3 + [whole(pl.ANY)] * 8,
        out_specs=(whole(pltpu.VMEM), whole(pltpu.VMEM)),
        scratch_shapes=[stack] * 4
        + [
            pltpu.VMEM((2 * count, width), BF16),
            pltpu.VMEM((2 * count, 16 * HEAD), BF16),
            pltpu.VMEM((2 * count, 8 * HEAD), BF16),
            pltpu.VMEM((2 * count, 8 * HEAD), BF16),
            pltpu.SemaphoreType.DMA((8,)),
        ],
        compiler_params=pltpu.CompilerParams(vmem_limit_bytes=24 * 2**20),
        cost_estimate=pl.CostEstimate(flops=3 * 10**9, bytes_accessed=7 * 10**6, transcendentals=2**20),
        name="attention",
    )(parity, own, other, gain, *groups)


def mlp_kernel(own, other, gain, weights, near_out, far_out, held, normed, total, sems):
    parts = sems.shape[0]
    size = weights.shape[0] // parts
    half = weights.shape[1] // 2
    copies = [
        pltpu.make_async_copy(
            weights.at[at * size : (at + 1) * size], held.at[at * size : (at + 1) * size], sems.at[at]
        )
        for at in range(parts)
    ]
    for copy in copies:
        copy.start()
    count, width = own.shape
    normed[0:count] = normalise(own[...], gain[...])
    normed[count:] = normalise(other[...], gain[...])
    for at in range(parts):
        copies[at].wait()
        w_in = held[at * size : (at + 1) * size, :half].reshape(-1, width)
        w_out = held[at * size : (at + 1) * size, half:].reshape(-1, width)
        hidden = lax.dot_general(normed[...], w_in, NT, preferred_element_type=F32)
        hidden = jax.nn.gelu(hidden).astype(BF16)
        term = jnp.dot(hidden, w_out, preferred_element_type=F32)
        if at == 0:
            total[...] = term
        else:
            total[...] += term
    near_out[...] = own[...].astype(F32) + total[:count]
    far_out[...] = total[count:].astype(BF16)


def mlp(own, other, gain, weights, parts=PARTS):
    count, width = own.shape
    return pl.pallas_call(
        mlp_kernel,
        out_shape=(
            jax.ShapeDtypeStruct((count, width), F32),
            jax.ShapeDtypeStruct((count, width), BF16),
        ),
        in_specs=[whole(pltpu.VMEM)] * 3 + [whole(pl.ANY)],
        out_specs=(whole(pltpu.VMEM), whole(pltpu.VMEM)),
        scratch_shapes=[
            pltpu.VMEM(weights.shape, BF16),
            pltpu.VMEM((2 * count, width), BF16),
            pltpu.VMEM((2 * count, width), F32),
            pltpu.SemaphoreType.DMA((parts,)),
        ],
        compiler_params=pltpu.CompilerParams(vmem_limit_bytes=56 * 2**20),
        cost_estimate=pl.CostEstimate(flops=10**6, bytes_accessed=10**4, transcendentals=0),
        name="mlp",
    )(own, other, gain, weights)


def spread_tokens(cols, tokens):
    pixel = lax.broadcasted_iota(jnp.int32, (cols, tokens), 0)
    token = lax.broadcasted_iota(jnp.int32, (cols, tokens), 1)
    return jnp.where(pixel // 2 == token, 1.0, 0.0).astype(BF16)


def conv_terms(terms, weights):
    sums = []
    for col in range(3):
        total = None
        for row, at in terms:
            term = jnp.dot(row, weights[at, col], preferred_element_type=F32)
            total = term if total is None else total + term
        sums.append(total)
    cols = sums[0].shape[0]
    column = lax.broadcasted_iota(jnp.int32, sums[0].shape, 0)
    left = jnp.where(column == 0, 0.0, pltpu.roll(sums[0], 1, 0))
    right = jnp.where(column == cols - 1, 0.0, pltpu.roll(sums[2], cols - 1, 0))
    return sums[1] + left + right


def near_terms(rows, out_row):
    return [(rows[at], at - out_row + 1) for at in sorted(rows) if -1 <= at - out_row <= 1]


def early_kernel(image, guide, weights, bias, guided, part_one, first, part_two, held, sems):
    copies = [pltpu.make_async_copy(weights.at[k], held.at[k], sems.at[k]) for k in range(2)]
    for copy in copies:
        copy.start()
    rows, cols, _ = guide.shape
    spread = spread_tokens(cols, image.shape[1])
    for at in range(rows // 2):
        wide = jnp.dot(spread, image[at], preferred_element_type=F32)
        for row in (2 * at, 2 * at + 1):
            guided[row] = (wide + guide[row].astype(F32)).astype(BF16)
    own = {at: guided[at] for at in range(rows)}
    copies[0].wait()
    for at in range(rows - 2):
        value = conv_terms(near_terms(own, at + 1), held.at[0]) + bias[0:1, :]
        first[at] = jax.nn.gelu(value).astype(BF16)
    for at, row in enumerate((-1, 0, rows - 1, rows)):
        part_one[at] = conv_terms(near_terms(own, row), held.at[0]) + bias[0:1, :]
    copies[1].wait()
    inner = {at + 1: first[at] for at in range(rows - 2)}
    for at in range(rows):
        part_two[at] = conv_terms(near_terms(inner, at), held.at[1]) + bias[1:2, :]


def late_kernel(
    place, image_low, image_high, guide_low, guide_high, guided, part_one, first, part_two, weights, bias,
    out, outer, second, held, sems
):
    copies = [pltpu.make_async_copy(weights.at[k], held.at[k], sems.at[k]) for k in range(3)]
    for copy in copies:
        copy.start()
    rows, cols, _ = guided.shape
    spread = spread_tokens(cols, image_low.shape[1])
    beside = {}
    for source, addend, top in ((image_low, guide_low, -4), (image_high, guide_high, rows)):
        for at in range(2):
            wide = jnp.dot(spread, source[at], preferred_element_type=F32)
            for row in (top + 2 * at, top + 2 * at + 1):
                if -3 <= row < rows + 3:
                    added = addend[row + 3 if row < 0 else row - rows]
                    beside[row] = (wide + added.astype(F32)).astype(BF16)
    first_row = place[0]
    last_row = place[1]

    def inside(value, row):
        at = first_row + row
        return jnp.where(jnp.logical_and(at >= 0, at < last_row), value, 0.0).astype(BF16)

    copies[0].wait()
    layer = {}
    saved = {-1: 0, 0: 1, rows - 1: 2, rows: 3}
    for at, row in enumerate((-2, -1, 0, rows - 1, rows, rows + 1)):
        value = conv_terms(near_terms(beside, row), held.at[0])
        value = value + (part_one[saved[row]] if row in saved else bias[0:1, :])
        outer[at] = inside(jax.nn.gelu(value), row)
        layer[row] = outer.at[at]
    copies[1].wait()
    shown = {}
    for row in range(-1, rows + 1):
        value = conv_terms([(ref[...], at) for ref, at in near_terms(layer, row)], held.at[1]) if near_terms(
            layer, row
        ) else 0.0
        value = value + (part_two[row] if 0 <= row < rows else bias[1:2, :])
        second[row + 1] = inside(jax.nn.gelu(value), row)
        shown[row] = second.at[row + 1]
    copies[2].wait()
    for row in range(rows):
        value = conv_terms([(ref[...], at) for ref, at in near_terms(shown, row)], held.at[2])
        out[row] = (value + bias[2:3, :] + guided[row].astype(F32)).astype(BF16)


def early_stage(image, guide, weights, bias):
    rows, cols, channels = guide.shape
    wide = (rows, cols, channels)
    return pl.pallas_call(
        early_kernel,
        out_shape=(
            jax.ShapeDtypeStruct(wide, BF16),
            jax.ShapeDtypeStruct((4, cols, channels), F32),
            jax.ShapeDtypeStruct((rows - 2, cols, channels), BF16),
            jax.ShapeDtypeStruct(wide, F32),
        ),
        in_specs=[whole(pltpu.VMEM)] * 2 + [whole(pl.ANY), whole(pltpu.VMEM)],
        out_specs=(whole(pltpu.VMEM),) * 4,
        scratch_shapes=[
            pltpu.VMEM((2,) + weights.shape[1:], BF16),
            pltpu.SemaphoreType.DMA((2,)),
        ],
        compiler_params=pltpu.CompilerParams(vmem_limit_bytes=24 * 2**20),
        cost_estimate=pl.CostEstimate(flops=3 * 10**9, bytes_accessed=4 * 10**6, transcendentals=2**20),
        name="early",
    )(image, guide, weights, bias)


def late_stage(place, image_low, image_high, guide_low, guide_high, early, weights, bias):
    rows, cols, channels = early[0].shape
    return pl.pallas_call(
        late_kernel,
        out_shape=jax.ShapeDtypeStruct((rows, cols, channels), BF16),
        in_specs=[whole(pltpu.SMEM)] + [whole(pltpu.VMEM)] * 8 + [whole(pl.ANY), whole(pltpu.VMEM)],
        out_specs=whole(pltpu.VMEM),
        scratch_shapes=[
            pltpu.VMEM((6, cols, channels), BF16),
            pltpu.VMEM((rows + 2, cols, channels), BF16),
            pltpu.VMEM(weights.shape, BF16),
            pltpu.SemaphoreType.DMA((3,)),
        ],
        compiler_params=pltpu.CompilerParams(vmem_limit_bytes=32 * 2**20),
        cost_estimate=pl.CostEstimate(flops=4 * 10**9, bytes_accessed=6 * 10**6, transcendentals=2**20),
        name="late",
    )(place, image_low, image_high, guide_low, guide_high, *early, weights, bias)


def per_device(
    tokens,
    ln_gain_one,
    ln_gain_two,
    qkv_weight,
    out_weight,
    in_weight,
    mlp_out_weight,
    proj_weight,
    land_mask,
    placement,
    guide,
    conv_weights,
    conv_bias,
):
    tiles, seg, width = tokens.shape
    groups = lax.axis_size(TILE)
    here = lax.axis_index(TILE)

    x_at = lax.axis_index("x")
    y_at = lax.axis_index("yh") * 2 + lax.axis_index("yl")
    colour_x = (x_at + 2 * y_at) % 4
    colour_x_beside = (x_at + 2 * (3 - y_at)) % 4

    by_head = jnp.transpose(qkv_weight, (0, 2, 1)).reshape(3, 2, HEAD, width)
    out_heads = out_weight.reshape(2, HEAD, width)
    attn_all = jnp.stack(
        [by_head[0], by_head[1], by_head[2], out_heads], axis=1
    ).reshape(4, 2 * HEAD, width)
    attn_piece = type_exchange(attn_all[colour_x], attn_all[colour_x_beside])
    near_half = jnp.stack([attn_piece, shift(attn_piece, "z", 1)])
    far_half = jnp.stack([shift(attn_piece, "z", 3), shift(attn_piece, "z", 2)])
    attn_w = across(near_half, 1) + across(far_half, 3)

    slice_rows = in_weight.shape[0] // 16
    start = (lax.axis_index("c") * 8 + lax.axis_index(("x", "yl"))) * slice_rows
    mlp_own = jnp.concatenate(
        [
            lax.dynamic_slice_in_dim(in_weight, start, slice_rows, 0),
            lax.dynamic_slice_in_dim(mlp_out_weight, start, slice_rows, 0),
        ],
        axis=0,
    )
    mlp_w = lax.all_gather(mlp_own, ("x", "yh", "yl", "z"), axis=0, tiled=False)

    slab_all = placement // tiles
    column_all = placement % tiles
    group_all = jnp.arange(placement.shape[0], dtype=jnp.int32) // tiles
    slab_local = lax.dynamic_slice_in_dim(slab_all, here * tiles, tiles, 0)
    selector = (slab_local[None, :] == jnp.arange(groups, dtype=jnp.int32)[:, None]).astype(BF16)
    in_slab = slab_all == here
    column_hot = (
        column_all[:, None] == jnp.arange(tiles, dtype=jnp.int32)[None, :]
    ) & in_slab[:, None]
    group_hot = group_all[:, None] == jnp.arange(groups, dtype=jnp.int32)[None, :]
    arrange = jnp.einsum(
        "tk,tg->kg", column_hot.astype(F32), group_hot.astype(F32)
    ).astype(BF16)
    marked = jnp.where((land_mask == 0)[:, None, None], jnp.asarray(FAR, BF16), tokens)
    marked, _ = lax.optimization_barrier((marked, attn_piece))
    outgoing = jnp.einsum("sj,jpd->spd", selector, marked, preferred_element_type=F32).astype(BF16)
    incoming = lax.all_to_all(outgoing, TILE, split_axis=0, concat_axis=0, tiled=True)
    slab_tokens = jnp.einsum(
        "kg,gpd->kpd", arrange, incoming, preferred_element_type=F32
    ).astype(BF16)
    land = slab_tokens[:, 0, 0] < FAR / 2
    slab_tokens, _ = lax.optimization_barrier((slab_tokens, far_half))
    tile_tokens = lax.all_to_all(slab_tokens, MP, split_axis=0, concat_axis=0, tiled=True)
    tile_tokens = tile_tokens.reshape(tiles * seg, width)
    other_tokens = swap_cores(tile_tokens)

    count = tiles * seg
    near, far = attention(
        (x_at % 2).astype(jnp.int32).reshape(1),
        tile_tokens,
        other_tokens,
        ln_gain_one.reshape(1, width),
        attn_w,
    )
    middle = (near + swap_cores(far).astype(F32)).astype(BF16)

    total = lax.axis_size(AXES)
    forward = [(i, i + 1) for i in range(total - 1)]
    backward = [(b, a) for a, b in forward]
    rows = guide.shape[0]
    guide_ends, _ = lax.optimization_barrier(((guide[rows - 3 :], guide[:3]), far))
    guide_low = lax.ppermute(guide_ends[0], AXES, forward)
    guide_first, _ = lax.optimization_barrier((guide_ends[1], guide_low))
    guide_high = lax.ppermute(guide_first, AXES, backward)

    middle = lax.all_to_all(
        middle.reshape(tiles, seg, width), MP, split_axis=0, concat_axis=0, tiled=True
    ).reshape(count, width)
    middle, guide_low = lax.optimization_barrier((middle, guide_low))
    near, far = mlp(middle, swap_cores(middle), ln_gain_two.reshape(1, width), mlp_w)
    far, guide_high = lax.optimization_barrier((far, guide_high))
    features = (near + swap_cores(far).astype(F32)).astype(BF16)
    embed = jnp.einsum("pd,dc->pc", features, proj_weight, preferred_element_type=F32).astype(BF16)
    channels = proj_weight.shape[1]
    token_rows = seg // SIDE
    embed = embed.reshape(tiles, token_rows, SIDE, channels) * land.astype(BF16)[:, None, None, None]
    image = jnp.transpose(embed, (1, 0, 2, 3)).reshape(token_rows, tiles * SIDE, channels)

    image_low = lax.ppermute(image, AXES, forward)
    image_high = lax.ppermute(image, AXES, backward)
    place = jnp.stack([lax.axis_index(AXES) * rows, jnp.int32(total * rows)])
    early = early_stage(image, guide, conv_weights, conv_bias)
    return late_stage(
        place, image_low, image_high, guide_low, guide_high, early, conv_weights, conv_bias
    )


def solution(mesh):
    fine = Mesh(mesh.devices.reshape(2, 4, 2, 2, 4), AXES)
    in_specs = (
        P(TILE, MP, None),
        P(),
        P(),
        P(None, None, MP),
        P(MP, None),
        P(MP, None),
        P(MP, None),
        P(),
        P(TILE),
        P(),
        P(AXES, None, None),
        P(),
        P(),
    )
    return jax.shard_map(
        per_device, mesh=fine, in_specs=in_specs, out_specs=P(AXES, None, None), check_vma=False
    )
```

```python
import jax
import jax.numpy as jnp
from jax import lax
from jax.experimental import pallas as pl
from jax.experimental.pallas import tpu as pltpu
from jax.sharding import Mesh, PartitionSpec as P

HEAD = 64
SIDE = 16
AXES = ("yl", "x", "c", "yh", "z")
TILE = ("yl", "x", "c")
MP = ("yh", "z")
F32 = jnp.float32
BF16 = jnp.bfloat16
FAR = 64.0

def shift(block, axis, step):
    if axis == "y":
        def at(pos):
            return (pos % 2) * 2 + pos // 2

        pairs = [(at((pos + step) % 4), at(pos)) for pos in range(4)]
        return lax.ppermute(block, ("yl", "yh"), pairs)
    count = lax.axis_size(axis)
    return lax.ppermute(block, axis, [((i + step) % count, i) for i in range(count)])


def swap_cores(block):
    return lax.ppermute(block, "c", [(0, 1), (1, 0)])


def type_exchange(mine, sent):
    def at(pos, core):
        return ((pos % 2) * 2 + core) * 2 + pos // 2

    pairs = []
    for core in range(2):
        for pos in range(4):
            if pos // 2 == core:
                pairs.append((at(pos, core), at(3 - pos, core)))
    received = lax.ppermute(sent, ("yl", "c", "yh"), pairs)
    return jnp.where(lax.axis_index("yh") == lax.axis_index("c"), mine, received)


def across(half, end):
    return half, shift(half, "x", 1), shift(half, "x", 3), shift(half, "y", end)


NT = (((1,), (1,)), ((), ()))
PARTS = 4


def whole(memory):
    return pl.BlockSpec(memory_space=memory)


def normalise(values, gain):
    widened = values.astype(F32)
    centre = jnp.mean(widened, axis=-1, keepdims=True)
    spread = jnp.mean((widened - centre) ** 2, axis=-1, keepdims=True)
    return ((widened - centre) * lax.rsqrt(spread + 1e-06) * gain).astype(BF16)


def attention_kernel(
    parity, own, other, gain, *rest
):
    groups = rest[:8]
    near_out, far_out, held_base, held_plus, held_minus, held_two, normed, queries, values, context, sems = rest[8:]
    stacks = (held_base, held_plus, held_minus, held_two)
    copies = [
        pltpu.make_async_copy(
            group, stacks[at % 4].at[at // 4 * 2 : at // 4 * 2 + 2], sems.at[at]
        )
        for at, group in enumerate(groups)
    ]
    for copy in copies:
        copy.start()
    even = parity[0] == 0
    count = own.shape[0]
    normed[0:count] = normalise(own[...], gain[...])
    normed[count:] = normalise(other[...], gain[...])
    for copy in copies:
        copy.wait()
    width = own.shape[1]
    half = 4 * HEAD

    def pick(one, two, rows):
        first = one[:, rows].reshape(-1, width)
        return jnp.where(even, first, two[:, rows].reshape(-1, width))

    everything = slice(0, 2 * HEAD)
    upper = slice(0, HEAD)
    lower = slice(HEAD, 2 * HEAD)
    sides = (
        ((held_base, held_minus), (held_plus, held_base)),
        ((held_two, held_plus), (held_minus, held_two)),
    )
    for side, (qk, vo) in enumerate(sides):
        queries[:, side * 2 * half : (side + 1) * 2 * half] = lax.dot_general(
            normed[...], pick(*qk, everything), NT, preferred_element_type=F32
        ).astype(BF16)
        values[:, side * half : (side + 1) * half] = lax.dot_general(
            normed[...], pick(*vo, upper), NT, preferred_element_type=F32
        ).astype(BF16)
    for tile in range(2):
        rows = slice(tile * count, (tile + 1) * count)
        for head in range(8):
            q = queries[rows, head * 2 * HEAD : head * 2 * HEAD + HEAD] * BF16(HEAD ** (-0.5))
            k = queries[rows, head * 2 * HEAD + HEAD : (head + 1) * 2 * HEAD]
            v = values[rows, head * HEAD : (head + 1) * HEAD]
            scores = lax.dot_general(q, k, NT, preferred_element_type=F32)
            scores = jnp.exp(scores - jnp.max(scores, axis=-1, keepdims=True))
            soft = (scores * (1.0 / jnp.sum(scores, axis=-1, keepdims=True))).astype(BF16)
            context[rows, head * HEAD : (head + 1) * HEAD] = jnp.dot(
                soft, v, preferred_element_type=F32
            ).astype(BF16)
    total = None
    for side, (qk, vo) in enumerate(sides):
        term = jnp.dot(
            context[:, side * half : (side + 1) * half], pick(*vo, lower), preferred_element_type=F32
        )
        total = term if total is None else total + term
    near_out[...] = own[...].astype(F32) + total[:count]
    far_out[...] = total[count:].astype(BF16)


def attention(parity, own, other, gain, groups):
    count, width = own.shape
    stack = pltpu.VMEM((4, 2 * HEAD, width), BF16)
    return pl.pallas_call(
        attention_kernel,
        out_shape=(
            jax.ShapeDtypeStruct((count, width), F32),
            jax.ShapeDtypeStruct((count, width), BF16),
        ),
        in_specs=[whole(pltpu.SMEM)] + [whole(pltpu.VMEM)] * 3 + [whole(pl.ANY)] * 8,
        out_specs=(whole(pltpu.VMEM), whole(pltpu.VMEM)),
        scratch_shapes=[stack] * 4
        + [
            pltpu.VMEM((2 * count, width), BF16),
            pltpu.VMEM((2 * count, 16 * HEAD), BF16),
            pltpu.VMEM((2 * count, 8 * HEAD), BF16),
            pltpu.VMEM((2 * count, 8 * HEAD), BF16),
            pltpu.SemaphoreType.DMA((8,)),
        ],
        compiler_params=pltpu.CompilerParams(vmem_limit_bytes=24 * 2**20),
        cost_estimate=pl.CostEstimate(flops=3 * 10**9, bytes_accessed=7 * 10**6, transcendentals=2**20),
        name="attention",
    )(parity, own, other, gain, *groups)


def mlp_kernel(own, other, gain, weights, near_out, far_out, held, normed, total, sems):
    parts = sems.shape[0]
    size = weights.shape[0] // parts
    half = weights.shape[1] // 2
    copies = [
        pltpu.make_async_copy(
            weights.at[at * size : (at + 1) * size], held.at[at * size : (at + 1) * size], sems.at[at]
        )
        for at in range(parts)
    ]
    for copy in copies:
        copy.start()
    count, width = own.shape
    normed[0:count] = normalise(own[...], gain[...])
    normed[count:] = normalise(other[...], gain[...])
    for at in range(parts):
        copies[at].wait()
        w_in = held[at * size : (at + 1) * size, :half].reshape(-1, width)
        w_out = held[at * size : (at + 1) * size, half:].reshape(-1, width)
        hidden = lax.dot_general(normed[...], w_in, NT, preferred_element_type=F32)
        hidden = jax.nn.gelu(hidden).astype(BF16)
        term = jnp.dot(hidden, w_out, preferred_element_type=F32)
        if at == 0:
            total[...] = term
        else:
            total[...] += term
    near_out[...] = own[...].astype(F32) + total[:count]
    far_out[...] = total[count:].astype(BF16)


def mlp(own, other, gain, weights, parts=PARTS):
    count, width = own.shape
    return pl.pallas_call(
        mlp_kernel,
        out_shape=(
            jax.ShapeDtypeStruct((count, width), F32),
            jax.ShapeDtypeStruct((count, width), BF16),
        ),
        in_specs=[whole(pltpu.VMEM)] * 3 + [whole(pl.ANY)],
        out_specs=(whole(pltpu.VMEM), whole(pltpu.VMEM)),
        scratch_shapes=[
            pltpu.VMEM(weights.shape, BF16),
            pltpu.VMEM((2 * count, width), BF16),
            pltpu.VMEM((2 * count, width), F32),
            pltpu.SemaphoreType.DMA((parts,)),
        ],
        compiler_params=pltpu.CompilerParams(vmem_limit_bytes=56 * 2**20),
        cost_estimate=pl.CostEstimate(flops=10**6, bytes_accessed=10**4, transcendentals=0),
        name="mlp",
    )(own, other, gain, weights)


def spread_tokens(cols, tokens):
    pixel = lax.broadcasted_iota(jnp.int32, (cols, tokens), 0)
    token = lax.broadcasted_iota(jnp.int32, (cols, tokens), 1)
    return jnp.where(pixel // 2 == token, 1.0, 0.0).astype(BF16)


def conv_terms(terms, weights):
    sums = []
    for col in range(3):
        total = None
        for row, at in terms:
            term = jnp.dot(row, weights[at, col], preferred_element_type=F32)
            total = term if total is None else total + term
        sums.append(total)
    cols = sums[0].shape[0]
    column = lax.broadcasted_iota(jnp.int32, sums[0].shape, 0)
    left = jnp.where(column == 0, 0.0, pltpu.roll(sums[0], 1, 0))
    right = jnp.where(column == cols - 1, 0.0, pltpu.roll(sums[2], cols - 1, 0))
    return sums[1] + left + right


def near_terms(rows, out_row):
    return [(rows[at], at - out_row + 1) for at in sorted(rows) if -1 <= at - out_row <= 1]


def early_kernel(image, guide, weights, bias, guided, part_one, first, part_two, held, sems):
    copies = [pltpu.make_async_copy(weights.at[k], held.at[k], sems.at[k]) for k in range(2)]
    for copy in copies:
        copy.start()
    rows, cols, _ = guide.shape
    spread = spread_tokens(cols, image.shape[1])
    for at in range(rows // 2):
        wide = jnp.dot(spread, image[at], preferred_element_type=F32)
        for row in (2 * at, 2 * at + 1):
            guided[row] = (wide + guide[row].astype(F32)).astype(BF16)
    own = {at: guided[at] for at in range(rows)}
    copies[0].wait()
    for at in range(rows - 2):
        value = conv_terms(near_terms(own, at + 1), held.at[0]) + bias[0:1, :]
        first[at] = jax.nn.gelu(value).astype(BF16)
    for at, row in enumerate((-1, 0, rows - 1, rows)):
        part_one[at] = conv_terms(near_terms(own, row), held.at[0]) + bias[0:1, :]
    copies[1].wait()
    inner = {at + 1: first[at] for at in range(rows - 2)}
    for at in range(rows):
        part_two[at] = conv_terms(near_terms(inner, at), held.at[1]) + bias[1:2, :]


def late_kernel(
    place, image_low, image_high, guide_low, guide_high, guided, part_one, first, part_two, weights, bias,
    out, outer, second, held, sems
):
    copies = [pltpu.make_async_copy(weights.at[k], held.at[k], sems.at[k]) for k in range(3)]
    for copy in copies:
        copy.start()
    rows, cols, _ = guided.shape
    spread = spread_tokens(cols, image_low.shape[1])
    beside = {}
    for source, addend, top in ((image_low, guide_low, -4), (image_high, guide_high, rows)):
        for at in range(2):
            wide = jnp.dot(spread, source[at], preferred_element_type=F32)
            for row in (top + 2 * at, top + 2 * at + 1):
                if -3 <= row < rows + 3:
                    added = addend[row + 3 if row < 0 else row - rows]
                    beside[row] = (wide + added.astype(F32)).astype(BF16)
    first_row = place[0]
    last_row = place[1]

    def inside(value, row):
        at = first_row + row
        return jnp.where(jnp.logical_and(at >= 0, at < last_row), value, 0.0).astype(BF16)

    copies[0].wait()
    layer = {}
    saved = {-1: 0, 0: 1, rows - 1: 2, rows: 3}
    for at, row in enumerate((-2, -1, 0, rows - 1, rows, rows + 1)):
        value = conv_terms(near_terms(beside, row), held.at[0])
        value = value + (part_one[saved[row]] if row in saved else bias[0:1, :])
        outer[at] = inside(jax.nn.gelu(value), row)
        layer[row] = outer.at[at]
    copies[1].wait()
    shown = {}
    for row in range(-1, rows + 1):
        value = conv_terms([(ref[...], at) for ref, at in near_terms(layer, row)], held.at[1]) if near_terms(
            layer, row
        ) else 0.0
        value = value + (part_two[row] if 0 <= row < rows else bias[1:2, :])
        second[row + 1] = inside(jax.nn.gelu(value), row)
        shown[row] = second.at[row + 1]
    copies[2].wait()
    for row in range(rows):
        value = conv_terms([(ref[...], at) for ref, at in near_terms(shown, row)], held.at[2])
        out[row] = (value + bias[2:3, :] + guided[row].astype(F32)).astype(BF16)


def early_stage(image, guide, weights, bias):
    rows, cols, channels = guide.shape
    wide = (rows, cols, channels)
    return pl.pallas_call(
        early_kernel,
        out_shape=(
            jax.ShapeDtypeStruct(wide, BF16),
            jax.ShapeDtypeStruct((4, cols, channels), F32),
            jax.ShapeDtypeStruct((rows - 2, cols, channels), BF16),
            jax.ShapeDtypeStruct(wide, F32),
        ),
        in_specs=[whole(pltpu.VMEM)] * 2 + [whole(pl.ANY), whole(pltpu.VMEM)],
        out_specs=(whole(pltpu.VMEM),) * 4,
        scratch_shapes=[
            pltpu.VMEM((2,) + weights.shape[1:], BF16),
            pltpu.SemaphoreType.DMA((2,)),
        ],
        compiler_params=pltpu.CompilerParams(vmem_limit_bytes=24 * 2**20),
        cost_estimate=pl.CostEstimate(flops=3 * 10**9, bytes_accessed=4 * 10**6, transcendentals=2**20),
        name="early",
    )(image, guide, weights, bias)


def late_stage(place, image_low, image_high, guide_low, guide_high, early, weights, bias):
    rows, cols, channels = early[0].shape
    return pl.pallas_call(
        late_kernel,
        out_shape=jax.ShapeDtypeStruct((rows, cols, channels), BF16),
        in_specs=[whole(pltpu.SMEM)] + [whole(pltpu.VMEM)] * 8 + [whole(pl.ANY), whole(pltpu.VMEM)],
        out_specs=whole(pltpu.VMEM),
        scratch_shapes=[
            pltpu.VMEM((6, cols, channels), BF16),
            pltpu.VMEM((rows + 2, cols, channels), BF16),
            pltpu.VMEM(weights.shape, BF16),
            pltpu.SemaphoreType.DMA((3,)),
        ],
        compiler_params=pltpu.CompilerParams(vmem_limit_bytes=32 * 2**20),
        cost_estimate=pl.CostEstimate(flops=4 * 10**9, bytes_accessed=6 * 10**6, transcendentals=2**20),
        name="late",
    )(place, image_low, image_high, guide_low, guide_high, *early, weights, bias)


def per_device(
    tokens,
    ln_gain_one,
    ln_gain_two,
    qkv_weight,
    out_weight,
    in_weight,
    mlp_out_weight,
    proj_weight,
    land_mask,
    placement,
    guide,
    conv_weights,
    conv_bias,
):
    tiles, seg, width = tokens.shape
    groups = lax.axis_size(TILE)
    here = lax.axis_index(TILE)

    x_at = lax.axis_index("x")
    y_at = lax.axis_index("yh") * 2 + lax.axis_index("yl")
    colour_x = (x_at + 2 * y_at) % 4
    colour_x_beside = (x_at + 2 * (3 - y_at)) % 4

    by_head = jnp.transpose(qkv_weight, (0, 2, 1)).reshape(3, 2, HEAD, width)
    out_heads = out_weight.reshape(2, HEAD, width)
    attn_all = jnp.stack(
        [by_head[0], by_head[1], by_head[2], out_heads], axis=1
    ).reshape(4, 2 * HEAD, width)
    attn_piece = type_exchange(attn_all[colour_x], attn_all[colour_x_beside])
    near_half = jnp.stack([attn_piece, shift(attn_piece, "z", 1)])
    far_half = jnp.stack([shift(attn_piece, "z", 3), shift(attn_piece, "z", 2)])
    attn_w = across(near_half, 1) + across(far_half, 3)

    slice_rows = in_weight.shape[0] // 16
    start = (lax.axis_index("c") * 8 + lax.axis_index(("x", "yl"))) * slice_rows
    mlp_own = jnp.concatenate(
        [
            lax.dynamic_slice_in_dim(in_weight, start, slice_rows, 0),
            lax.dynamic_slice_in_dim(mlp_out_weight, start, slice_rows, 0),
        ],
        axis=0,
    )
    mlp_w = lax.all_gather(mlp_own, ("x", "yh", "yl", "z"), axis=0, tiled=False)

    slab_all = placement // tiles
    column_all = placement % tiles
    group_all = jnp.arange(placement.shape[0], dtype=jnp.int32) // tiles
    slab_local = lax.dynamic_slice_in_dim(slab_all, here * tiles, tiles, 0)
    selector = (slab_local[None, :] == jnp.arange(groups, dtype=jnp.int32)[:, None]).astype(BF16)
    in_slab = slab_all == here
    column_hot = (
        column_all[:, None] == jnp.arange(tiles, dtype=jnp.int32)[None, :]
    ) & in_slab[:, None]
    group_hot = group_all[:, None] == jnp.arange(groups, dtype=jnp.int32)[None, :]
    arrange = jnp.einsum(
        "tk,tg->kg", column_hot.astype(F32), group_hot.astype(F32)
    ).astype(BF16)
    marked = jnp.where((land_mask == 0)[:, None, None], jnp.asarray(FAR, BF16), tokens)
    marked, _ = lax.optimization_barrier((marked, attn_piece))
    outgoing = jnp.einsum("sj,jpd->spd", selector, marked, preferred_element_type=F32).astype(BF16)
    incoming = lax.all_to_all(outgoing, TILE, split_axis=0, concat_axis=0, tiled=True)
    slab_tokens = jnp.einsum(
        "kg,gpd->kpd", arrange, incoming, preferred_element_type=F32
    ).astype(BF16)
    land = slab_tokens[:, 0, 0] < FAR / 2
    slab_tokens, _ = lax.optimization_barrier((slab_tokens, far_half))
    tile_tokens = lax.all_to_all(slab_tokens, MP, split_axis=0, concat_axis=0, tiled=True)
    tile_tokens = tile_tokens.reshape(tiles * seg, width)
    other_tokens = swap_cores(tile_tokens)

    count = tiles * seg
    near, far = attention(
        (x_at % 2).astype(jnp.int32).reshape(1),
        tile_tokens,
        other_tokens,
        ln_gain_one.reshape(1, width),
        attn_w,
    )
    middle = (near + swap_cores(far).astype(F32)).astype(BF16)

    total = lax.axis_size(AXES)
    forward = [(i, i + 1) for i in range(total - 1)]
    backward = [(b, a) for a, b in forward]
    rows = guide.shape[0]
    guide_ends, _ = lax.optimization_barrier(((guide[rows - 3 :], guide[:3]), far))
    guide_low = lax.ppermute(guide_ends[0], AXES, forward)
    guide_high = lax.ppermute(guide_ends[1], AXES, backward)

    middle = lax.all_to_all(
        middle.reshape(tiles, seg, width), MP, split_axis=0, concat_axis=0, tiled=True
    ).reshape(count, width)
    near, far = mlp(middle, swap_cores(middle), ln_gain_two.reshape(1, width), mlp_w)
    far, guide_low, guide_high = lax.optimization_barrier((far, guide_low, guide_high))
    features = (near + swap_cores(far).astype(F32)).astype(BF16)
    embed = jnp.einsum("pd,dc->pc", features, proj_weight, preferred_element_type=F32).astype(BF16)
    channels = proj_weight.shape[1]
    token_rows = seg // SIDE
    embed = embed.reshape(tiles, token_rows, SIDE, channels) * land.astype(BF16)[:, None, None, None]
    image = jnp.transpose(embed, (1, 0, 2, 3)).reshape(token_rows, tiles * SIDE, channels)

    image_low = lax.ppermute(image, AXES, forward)
    image_high = lax.ppermute(image, AXES, backward)
    place = jnp.stack([lax.axis_index(AXES) * rows, jnp.int32(total * rows)])
    early = early_stage(image, guide, conv_weights, conv_bias)
    return late_stage(
        place, image_low, image_high, guide_low, guide_high, early, conv_weights, conv_bias
    )


def solution(mesh):
    fine = Mesh(mesh.devices.reshape(2, 4, 2, 2, 4), AXES)
    in_specs = (
        P(TILE, MP, None),
        P(),
        P(),
        P(None, None, MP),
        P(MP, None),
        P(MP, None),
        P(MP, None),
        P(),
        P(TILE),
        P(),
        P(AXES, None, None),
        P(),
        P(),
    )
    return jax.shard_map(
        per_device, mesh=fine, in_specs=in_specs, out_specs=P(AXES, None, None), check_vma=False
    )
```
